32 devices in a mesh: groups: 2 (over y), gy: 4 (over x, core), gx: 4 (over z).
Axes of the slice: x: 2, y: 2, z: 4, core: 2. Of those that a mesh axis runs over, the one named last changes fastest.
Arguments:
- tokens: bfloat16 [128, 128, 768], P(('groups', 'gy'), 'gx'), parts along dimension 0, may hold values from -6 to 6
- conv_kernel: bfloat16 [7, 7, 768], replicated, may hold values from -0.875 to 0.875
- project_in: bfloat16 [768, 2304], P(('gy', 'gx')), may hold values from -0.21875 to 0.21875
- project_out: bfloat16 [768, 768], P(('gy', 'gx')), may hold values from -0.21875 to 0.21875
- rel_bias: float32 [24, 64, 64], replicated, may hold values from -4 to 4
- expert_in: bfloat16 [32, 1536, 768], P('gy'), may hold values from -0.21875 to 0.21875
- expert_out: bfloat16 [32, 1536, 768], P('gy'), may hold values from -0.15625 to 0.15625
- const_table: float32 [16, 768], replicated, may hold values from -5 to 5
- expert_ids: int32 [128, 128], P(('groups', 'gy'), 'gx'), parts along dimension 0, may hold values from 0 to 33, as said below
- slots: int32 [128, 128], P(('groups', 'gy'), 'gx'), parts along dimension 0, may hold values from 0 to 15, as said below
- const_index: int32 [128, 128], P(('groups', 'gy'), 'gx'), parts along dimension 0, may hold values from 0 to 15
Outputs:
- output: bfloat16 [128, 128, 768], P(('groups', 'gy'), 'gx'), parts along dimension 0
The draws below stay inside these ranges and needn't reach their ends.
There are 2 independent parts, one for each index of `groups`. The reference program is written for one: setup_inputs(seed, part) draws one part's arguments, and reference() takes and returns one part's arrays. A program takes and returns all parts, laid end to end along the dimension named above; an argument that names none is the same for every part. Nothing has to cross between parts.
Inputs may be any that keep to these rules, and one draw needn't show every extreme that they name: `expert_ids`: values below 32 name real experts, 32 the constant expert, 33 the zero expert. Among the tokens of one tile no real expert is named more than 16 times, and in every tile some real expert is named exactly 16 times. Tokens of one tile that name the same real expert have distinct slots; tokens of the constant or zero expert have slot 0.
All inputs are finite; a program needn't handle non-finite values.
Results may differ from the reference program's by a relative error of at most 0.008.
Values may be sent and summed in bfloat16 or wider, within the bound.
No kernel may reach another device: no remote copies, remote signals or barrier semaphores. Data moves between devices by JAX's collectives and lax.ppermute only.
A program may use at most 128 MiB of HBM per device.

```python
import jax
import jax.numpy as jnp
from jax import lax

D = 768
HD = 32
HEADS = 24
FF = 1536
EXPERTS = 32
NCONST = 16
WIN = 8
SHIFT = 4
KERNEL = 7
TH = 16
TW = 32
CAP = 16
H = 64
W = 128
N_GY = 4
N_GX = 4


def routing(key):
    block_count = H // TH * (W // TW)
    tile_size = TH * TW
    real_slots = EXPERTS * CAP
    pool_size = real_slots + tile_size // 2
    block_keys = jax.random.split(key, block_count)

    def one_block(block_key):
        first_key, second_key, third_key = jax.random.split(block_key, 3)
        full_expert = jax.random.randint(first_key, (), 0, EXPERTS)
        others = jnp.arange(pool_size - CAP, dtype=jnp.int32)
        others = jnp.where(others < full_expert * CAP, others, others + CAP)
        picked = jax.random.permutation(second_key, others)[:tile_size - CAP]
        chosen = jnp.concatenate([full_expert * CAP + jnp.arange(CAP, dtype=jnp.int32), picked])
        return jax.random.permutation(third_key, chosen)
    entries = jax.vmap(one_block)(block_keys)
    beyond = entries - real_slots
    expert_of = jnp.where(entries < real_slots, entries // CAP, jnp.where(beyond < tile_size // 4, EXPERTS, EXPERTS + 1))
    slot_of = jnp.where(entries < real_slots, entries % CAP, 0)

    def arrange(tiled):
        grid_form = tiled.reshape(H // TH, W // TW, TH, TW).transpose(0, 2, 1, 3)
        return grid_form.reshape(H, W).astype(jnp.int32)
    return (arrange(expert_of), arrange(slot_of))


def draw_expert_ids(key, part):
    expert_of, slot_of = routing(key)
    return expert_of


def draw_slots(key, part):
    expert_of, slot_of = routing(key)
    return slot_of


def plant(result, stream_key, smallest, high):
    spot = [jax.random.randint(jax.random.fold_in(stream_key, axis), (), 0, length) for axis, length in enumerate(result.shape)]
    longest = result.shape.index(max(result.shape))
    next_to = spot[:longest] + [(spot[longest] + 1) % result.shape[longest]] + spot[longest + 1:]
    return result.at[tuple(spot)].set(smallest).at[tuple(next_to)].set(high)


def block_scale(own_key, dims, cuts, smallest, largest):
    factor_of, own = 1.0, jax.random.fold_in(own_key, 6)
    for axis_at, parts in cuts:
        steps = jnp.exp(jax.random.uniform(jax.random.fold_in(own, axis_at), (parts,), jnp.float32, smallest / len(cuts), largest / len(cuts)))
        factor_of = factor_of * jnp.repeat(steps, dims[axis_at] // parts).reshape([-1 if axis == axis_at else 1 for axis in range(len(dims))])
    return factor_of


def scatter_about(own_key, shape, width, reach, cuts=(), kind=jnp.bfloat16):
    values = jax.random.normal(own_key, shape, jnp.float32) * width
    if len(cuts) > 0:
        values = block_scale(own_key, shape, cuts, -0.22, 0.18) * values
    return jnp.clip(values, min=-reach, max=reach).astype(kind)


def setup_inputs(seed: int = 0, part: int = 0) -> dict:
    keys = jax.random.split(jax.random.key(seed), 12)
    part_keys = jax.random.split(jax.random.fold_in(keys[11], part), 12)
    tokens = scatter_about(part_keys[0], (H, W, D), 1.0, 6.0, ((0, 4), (1, 4)))
    conv_kernel = scatter_about(keys[1], (KERNEL, KERNEL, D), (KERNEL * KERNEL) ** -0.5, 0.875)
    project_in = scatter_about(keys[2], (D, 3 * D), D ** -0.5, 0.21875, ((0, 16),))
    project_out = scatter_about(keys[3], (D, D), D ** -0.5, 0.21875, ((0, 16),))
    rel_bias = scatter_about(keys[4], (HEADS, WIN * WIN, WIN * WIN), 1.0, 4.0, (), jnp.float32)
    expert_in = scatter_about(keys[5], (EXPERTS, FF, D), D ** -0.5, 0.21875, ((0, 4),))
    expert_out = scatter_about(keys[6], (EXPERTS, FF, D), FF ** -0.5, 0.15625, ((0, 4),))
    const_table = scatter_about(keys[7], (NCONST, D), 1.0, 5.0, (), jnp.float32)
    expert_ids = draw_expert_ids(jax.random.fold_in(jax.random.fold_in(keys[11], part), 71), part)
    slots = draw_slots(jax.random.fold_in(jax.random.fold_in(keys[11], part), 71), part)
    const_index = plant(jax.random.randint(part_keys[10], (H, W), 0, NCONST), jax.random.fold_in(part_keys[10], 1), 0, NCONST - 1).astype(jnp.int32)
    return {"tokens": tokens, "conv_kernel": conv_kernel, "project_in": project_in, "project_out": project_out, "rel_bias": rel_bias, "expert_in": expert_in, "expert_out": expert_out, "const_table": const_table, "expert_ids": expert_ids, "slots": slots, "const_index": const_index}


def layer_norm(values):
    values = values.astype(jnp.float32)
    centred = values - lax.optimization_barrier(jnp.mean(values, axis=-1, keepdims=True))
    spread = lax.optimization_barrier(jnp.mean(centred * centred, axis=-1, keepdims=True))
    return (centred * lax.rsqrt(spread + 1e-05)).astype(jnp.bfloat16)

def to_windows(grid_field):
    height, width_all, channels = grid_field.shape
    blocks = grid_field.reshape(height // WIN, WIN, width_all // WIN, WIN, channels)
    return blocks.transpose(0, 2, 1, 3, 4).reshape(-1, WIN * WIN, channels)

def from_windows(blocks, height, width_all):
    channels = blocks.shape[-1]
    grid_field = blocks.reshape(height // WIN, width_all // WIN, WIN, WIN, channels)
    return grid_field.transpose(0, 2, 1, 3, 4).reshape(height, width_all, channels)

def attend(region, side_rows, side_cols, project_in, project_out, rel_bias):
    height, width_all, channels = region.shape
    head_count = channels // HD
    normed = layer_norm(region).reshape(height * width_all, channels)
    mixed = jnp.dot(normed, project_in, preferred_element_type=jnp.float32).astype(jnp.bfloat16)
    windows = to_windows(mixed.reshape(height, width_all, 3 * channels))
    window_count = windows.shape[0]
    query_part = windows[:, :, :channels].reshape(window_count, WIN * WIN, head_count, HD).astype(jnp.float32)
    key_part = windows[:, :, channels:2 * channels].reshape(window_count, WIN * WIN, head_count, HD).astype(jnp.float32)
    value_part = windows[:, :, 2 * channels:].reshape(window_count, WIN * WIN, head_count, HD).astype(jnp.float32)
    scores = jnp.einsum('wqhd,wkhd->whqk', query_part, key_part) * HD ** (-0.5) + rel_bias[None].astype(jnp.float32)
    labels = side_rows.astype(jnp.int32)[:, None] * 2 + side_cols.astype(jnp.int32)[None, :]
    label_win = to_windows(labels[:, :, None]).reshape(window_count, WIN * WIN)
    allowed = label_win[:, :, None] == label_win[:, None, :]
    weights = jnp.where(allowed[:, None], jnp.exp(scores), 0.0)
    weights_norm = (weights / lax.optimization_barrier(jnp.sum(weights, axis=-1, keepdims=True))).astype(jnp.bfloat16)
    context = jnp.einsum('whqk,wkhd->wqhd', weights_norm.astype(jnp.float32), value_part).astype(jnp.bfloat16)
    context = from_windows(context.reshape(window_count, WIN * WIN, channels), height, width_all)
    update = jnp.dot(context.reshape(height * width_all, channels), project_out, preferred_element_type=jnp.float32)
    summed = region.astype(jnp.float32).reshape(height * width_all, channels) + update
    return summed.astype(jnp.bfloat16).reshape(height, width_all, channels)

def expert_step(inputs):
    rows_in, weight_in, weight_out = inputs
    hidden = jax.nn.gelu(jnp.dot(rows_in, weight_in.T, preferred_element_type=jnp.float32), approximate=False)
    hidden = hidden.astype(jnp.bfloat16)
    return jnp.dot(hidden, weight_out, preferred_element_type=jnp.float32).astype(jnp.bfloat16)

def reference(tokens, conv_kernel, project_in, project_out, rel_bias, expert_in, expert_out, const_table, expert_ids, slots, const_index):
    height = TH * N_GY
    width_all = TW * N_GX
    channels = D
    margin = KERNEL // 2
    widened = tokens.astype(jnp.float32)
    padded = jnp.pad(widened, ((margin, margin), (margin, margin), (0, 0)))
    summed = jnp.zeros_like(widened)
    for row_off in range(KERNEL):
        for col_off in range(KERNEL):
            weight = conv_kernel[row_off, col_off].astype(jnp.float32)
            summed = summed + padded[row_off:row_off + height, col_off:col_off + width_all] * weight
    encoded = (widened + summed).astype(jnp.bfloat16)
    rolled = jnp.roll(encoded, (SHIFT, SHIFT), axis=(0, 1))
    side_rows = jnp.roll(jnp.arange(height) >= height - SHIFT, SHIFT)
    side_cols = jnp.roll(jnp.arange(width_all) >= width_all - SHIFT, SHIFT)
    attended_rolled = attend(rolled, side_rows, side_cols, project_in, project_out, rel_bias)
    attended = jnp.roll(attended_rolled, (-SHIFT, -SHIFT), axis=(0, 1))
    normed = layer_norm(attended).reshape(height * width_all, channels)
    tile_index = ((jnp.arange(height) // TH)[:, None] * N_GX + (jnp.arange(width_all) // TW)[None, :]).reshape(-1).astype(jnp.int32)
    expert_of = expert_ids.reshape(-1).astype(jnp.int32)
    slot_of = slots.reshape(-1).astype(jnp.int32)
    is_real = expert_of < EXPERTS
    tile_count = N_GY * N_GX
    buffer_size = EXPERTS * tile_count * CAP
    position = jnp.where(is_real, (expert_of * tile_count + tile_index) * CAP + slot_of, buffer_size).astype(jnp.int32)
    buffer = jnp.zeros((buffer_size, channels), jnp.bfloat16).at[position].set(normed, mode='drop')
    buffer = buffer.reshape(EXPERTS, tile_count * CAP, channels)
    results = lax.map(expert_step, (buffer, expert_in, expert_out)).reshape(buffer_size, channels)
    picked = results[jnp.minimum(position, buffer_size - 1)].astype(jnp.float32)
    constant = const_table[const_index.reshape(-1)].astype(jnp.float32)
    mixture = jnp.where(is_real[:, None], picked, jnp.where((expert_of == EXPERTS)[:, None], constant, 0.0))
    output = attended.reshape(height * width_all, channels).astype(jnp.float32) + mixture
    return output.astype(jnp.bfloat16).reshape(height, width_all, channels)
```

```python
import jax
import jax.numpy as jnp
from jax import lax
from jax.sharding import PartitionSpec as P

HD = 32
EXPERTS = 32
WIN = 8
SHIFT = 4
KERNEL = 7
CAP = 16


def shifted(x, axis, by):
    size = lax.axis_size(axis)
    return lax.ppermute(x, axis, [(i, (i + by) % size) for i in range(size)])


def layer_norm(values):
    values = values.astype(jnp.float32)
    centred = values - jnp.mean(values, axis=-1, keepdims=True)
    spread = jnp.mean(centred * centred, axis=-1, keepdims=True)
    return (centred * lax.rsqrt(spread + 1e-05)).astype(jnp.bfloat16)


def to_windows(grid_field):
    height, width_all, channels = grid_field.shape
    blocks = grid_field.reshape(height // WIN, WIN, width_all // WIN, WIN, channels)
    return blocks.transpose(0, 2, 1, 3, 4).reshape(-1, WIN * WIN, channels)


def from_windows(blocks, height, width_all):
    channels = blocks.shape[-1]
    grid_field = blocks.reshape(height // WIN, width_all // WIN, WIN, WIN, channels)
    return grid_field.transpose(0, 2, 1, 3, 4).reshape(height, width_all, channels)


def attend(region, side_rows, side_cols, project_in, project_out, rel_bias):
    height, width_all, channels = region.shape
    head_count = channels // HD
    row_total = height * width_all
    normed = layer_norm(region).reshape(row_total, channels)
    columns = normed
    mixed = jnp.dot(
        columns,
        lax.all_gather(project_in, ("gy", "gx"), axis=0, tiled=True),
        preferred_element_type=jnp.float32,
    )
    mixed = mixed.astype(jnp.bfloat16)
    windows = to_windows(mixed.reshape(height, width_all, 3 * channels))
    window_count = windows.shape[0]
    query_part = windows[:, :, :channels].reshape(window_count, WIN * WIN, head_count, HD)
    key_part = windows[:, :, channels : 2 * channels].reshape(
        window_count, WIN * WIN, head_count, HD
    )
    value_part = windows[:, :, 2 * channels :].reshape(window_count, WIN * WIN, head_count, HD)
    scores = jnp.einsum("wqhd,wkhd->whqk", query_part, key_part, preferred_element_type=jnp.float32)
    scores = scores * HD ** (-0.5) + rel_bias[None]
    labels = side_rows.astype(jnp.int32)[:, None] * 2 + side_cols.astype(jnp.int32)[None, :]
    label_win = to_windows(labels[:, :, None]).reshape(window_count, WIN * WIN)
    allowed = label_win[:, :, None] == label_win[:, None, :]
    weights = jnp.where(allowed[:, None], jnp.exp(scores), 0.0)
    weights_norm = (weights / jnp.sum(weights, axis=-1, keepdims=True)).astype(jnp.bfloat16)
    context = jnp.einsum(
        "whqk,wkhd->wqhd", weights_norm, value_part, preferred_element_type=jnp.float32
    ).astype(jnp.bfloat16)
    context = from_windows(context.reshape(window_count, WIN * WIN, channels), height, width_all)
    context = context.reshape(row_total, channels)
    columns = context
    update = jnp.dot(
        columns,
        lax.all_gather(project_out, ("gy", "gx"), axis=0, tiled=True),
        preferred_element_type=jnp.float32,
    )
    summed = region.astype(jnp.float32).reshape(row_total, channels) + update
    return summed.astype(jnp.bfloat16).reshape(height, width_all, channels)


def position_code(
    extended, conv_kernel, first_row, first_col, height_all, width_all, region_rows, region_cols
):
    widened = extended.astype(jnp.float32)
    margin = KERNEL // 2
    row_global = first_row + jnp.arange(region_rows)
    col_global = first_col + jnp.arange(region_cols)
    summed = jnp.zeros((region_rows, region_cols, widened.shape[-1]), jnp.float32)
    for row_off in range(KERNEL):
        row_ok = (
            jnp.floor_divide(row_global + row_off - margin, height_all)
            == jnp.floor_divide(row_global, height_all)
        ).astype(jnp.float32)
        for col_off in range(KERNEL):
            col_ok = (
                jnp.floor_divide(col_global + col_off - margin, width_all)
                == jnp.floor_divide(col_global, width_all)
            ).astype(jnp.float32)
            weight = conv_kernel[row_off, col_off].astype(jnp.float32)
            masked = widened[row_off : row_off + region_rows, col_off : col_off + region_cols] * (
                row_ok[:, None, None] * col_ok[None, :, None]
            )
            summed = summed + masked * weight
    centre = widened[margin : margin + region_rows, margin : margin + region_cols]
    return (centre + summed).astype(jnp.bfloat16)


def shards(
    tokens,
    conv_kernel,
    project_in,
    project_out,
    rel_bias,
    expert_in,
    expert_out,
    const_table,
    expert_ids,
    slots,
    const_index,
):
    tile_rows, tile_cols, channels = tokens.shape
    grid_rows = lax.axis_size("gy")
    grid_cols = lax.axis_size("gx")
    height_all = tile_rows * grid_rows
    width_all = tile_cols * grid_cols
    first_row = lax.axis_index("gy") * tile_rows - SHIFT
    first_col = lax.axis_index("gx") * tile_cols - SHIFT
    reach = KERNEL // 2 + SHIFT
    above = shifted(tokens[tile_rows - reach :], "gy", 1)
    stacked = jnp.concatenate([above, tokens], axis=0)
    beside = shifted(stacked[:, tile_cols - reach :], "gx", 1)
    extended = jnp.concatenate([beside, stacked], axis=1)
    encoded = position_code(
        extended, conv_kernel, first_row, first_col, height_all, width_all, tile_rows, tile_cols
    )
    side_rows = (first_row + jnp.arange(tile_rows)) % height_all >= height_all - SHIFT
    side_cols = (first_col + jnp.arange(tile_cols)) % width_all >= width_all - SHIFT
    rolled_out = attend(encoded, side_rows, side_cols, project_in, project_out, rel_bias)
    below = shifted(rolled_out[:SHIFT], "gy", -1)
    joined = jnp.concatenate([rolled_out, below], axis=0)
    right_side = shifted(joined[:, :SHIFT], "gx", -1)
    joined = jnp.concatenate([joined, right_side], axis=1)
    attended = joined[SHIFT : SHIFT + tile_rows, SHIFT : SHIFT + tile_cols]
    normed = layer_norm(attended).reshape(tile_rows * tile_cols, channels)
    expert_of = expert_ids.reshape(-1)
    slot_of = slots.reshape(-1)
    is_real = expert_of < EXPERTS
    row_experts = EXPERTS // grid_rows
    buffer_size = CAP * EXPERTS
    position = jnp.where(is_real, expert_of * CAP + slot_of, buffer_size)
    place = jnp.arange(buffer_size, dtype=jnp.int32)
    onehot = (position[None, :] == place[:, None]).astype(jnp.bfloat16)
    buffer = jnp.dot(onehot, normed, preferred_element_type=jnp.float32).astype(jnp.bfloat16)
    outgoing = buffer.reshape(grid_rows, row_experts, CAP, channels)
    incoming = lax.all_to_all(outgoing, "gy", split_axis=0, concat_axis=0, tiled=True)
    hidden = jnp.einsum("nrsd,rfd->rnsf", incoming, expert_in, preferred_element_type=jnp.float32)
    hidden = jax.nn.gelu(hidden, approximate=False).astype(jnp.bfloat16)
    result = jnp.einsum("rnsf,rfd->nrsd", hidden, expert_out, preferred_element_type=jnp.float32)
    results = lax.all_to_all(
        result.astype(jnp.bfloat16), "gy", split_axis=0, concat_axis=0, tiled=True
    )
    back = (position[:, None] == place[None, :]).astype(jnp.bfloat16)
    picked = jnp.dot(
        back, results.reshape(buffer_size, channels), preferred_element_type=jnp.float32
    )
    table_rows = const_table.shape[0]
    selector = (const_index.reshape(-1)[:, None] == jnp.arange(table_rows)[None, :]).astype(
        jnp.float32
    )
    constant = jnp.dot(selector, const_table, precision=lax.Precision.HIGHEST)
    mixture = jnp.where(
        is_real[:, None], picked, jnp.where((expert_of == EXPERTS)[:, None], constant, 0.0)
    )
    output = attended.reshape(tile_rows * tile_cols, channels).astype(jnp.float32) + mixture
    return output.astype(jnp.bfloat16).reshape(tile_rows, tile_cols, channels)


def solution(mesh):
    placed = (
        P(("groups", "gy"), "gx", None),
        P(),
        P(("gy", "gx"), None),
        P(("gy", "gx"), None),
        P(),
        P("gy", None, None),
        P("gy", None, None),
        P(),
        P(("groups", "gy"), "gx"),
        P(("groups", "gy"), "gx"),
        P(("groups", "gy"), "gx"),
    )
    return jax.shard_map(
        shards,
        mesh=mesh,
        in_specs=placed,
        out_specs=P(("groups", "gy"), "gx", None),
        check_vma=False,
    )
```

```python
import functools

import jax
import jax.numpy as jnp
from jax import lax
from jax.experimental import pallas as pl
from jax.experimental.pallas import tpu as pltpu
from jax.sharding import PartitionSpec as P

HD = 32
EXPERTS = 32
WIN = 8
SHIFT = 4
KERNEL = 7
CAP = 16
LANES = 128
GROUP = LANES // HD
SPOTS = WIN * WIN
HALO = 8
VMEM = pl.BlockSpec(memory_space=pltpu.VMEM)
SMEM = pl.BlockSpec(memory_space=pltpu.SMEM)
ANY = pl.BlockSpec(memory_space=pl.ANY)
LARGEST = 3.38e38


def shifted(x, axis, by):
    size = lax.axis_size(axis)
    return lax.ppermute(x, axis, [(i, (i + by) % size) for i in range(size)])


def shifted_both(x, by):
    rows, cols = lax.axis_size("gy"), lax.axis_size("gx")
    pairs = [
        (i * cols + j, ((i + by) % rows) * cols + (j + by) % cols)
        for i in range(rows)
        for j in range(cols)
    ]
    return lax.ppermute(x, ("gy", "gx"), pairs)


def exchanged(x, axis, mask):
    size = lax.axis_size(axis)
    return lax.ppermute(x, axis, [(i, i ^ mask) for i in range(size)])


def normalized(values):
    centred = values - jnp.mean(values, axis=-1, keepdims=True)
    spread = jnp.mean(centred * centred, axis=-1, keepdims=True)
    return (centred * lax.rsqrt(spread + 1e-05)).astype(jnp.bfloat16)


def encode_kernel(place, tokens, above, beside, taps, encoded, normed, extended, weights):
    rows, cols, channels = tokens.shape
    reach = KERNEL // 2 + SHIFT
    extended[:, :HALO] = beside[...].astype(jnp.float32)
    extended[:reach, HALO:] = above[...].astype(jnp.float32)
    extended[reach:, HALO:] = tokens[...].astype(jnp.float32)
    weights[...] = taps[...].astype(jnp.float32)
    inner_row = jnp.where(place[0] == 0, 0.0, 1.0)
    first_col = place[1] == 0
    window_cols = cols // WIN
    col = lax.broadcasted_iota(jnp.int32, (WIN, LANES), 0)

    def block(index, _):
        lanes = pl.ds(pl.multiple_of(index * LANES, LANES), LANES)
        for tile in range(window_cols):
            sums = [None] * rows
            for col_off in range(KERNEL):
                column = [
                    jnp.broadcast_to(weights[row_off, pl.ds(col_off, 1), lanes], (WIN, LANES))
                    for row_off in range(KERNEL)
                ]
                if tile == 0:
                    near = (col < SHIFT) == (col + col_off < reach)
                    keep = jnp.where(near | jnp.logical_not(first_col), 1.0, 0.0)
                for row in range(rows + KERNEL - 1):
                    here = extended[row, tile * WIN : tile * WIN + WIN, lanes]
                    after = extended[row, (tile + 1) * WIN : (tile + 2) * WIN, lanes]
                    line = jnp.where(col > col_off, here, after)
                    line = pltpu.roll(line, WIN - 1 - col_off, 0)
                    if tile == 0:
                        line = line * keep
                    cut = line * inner_row if SHIFT <= row < reach + KERNEL // 2 else line
                    for out in range(max(0, row - KERNEL + 1), min(rows, row + 1)):
                        row_off = row - out
                        same = (out < SHIFT) == (row < reach)
                        term = (line if same else cut) * column[row_off]
                        if row_off == KERNEL // 2 and col_off == KERNEL // 2:
                            term = term + line
                        sums[out] = term if sums[out] is None else sums[out] + term
            for window_row in range(rows // WIN):
                stacked = jnp.concatenate(sums[window_row * WIN : (window_row + 1) * WIN], axis=0)
                first = (window_row * window_cols + tile) * SPOTS
                encoded[first : first + SPOTS, lanes] = stacked.astype(jnp.bfloat16)
        return 0

    lax.fori_loop(0, channels // LANES, block, 0)

    def norm(index, _):
        part = pl.ds(pl.multiple_of(index * SPOTS, SPOTS), SPOTS)
        normed[part, :] = normalized(encoded[part, :].astype(jnp.float32))
        return 0

    lax.fori_loop(0, rows * cols // SPOTS, norm, 0)


def encode(place, tokens, above, beside, taps):
    rows, cols, channels = tokens.shape
    flat = jax.ShapeDtypeStruct((rows * cols, channels), jnp.bfloat16)
    reach = KERNEL // 2 + SHIFT
    return pl.pallas_call(
        encode_kernel,
        out_shape=(flat, flat),
        in_specs=[SMEM] + [VMEM] * 4,
        out_specs=(VMEM, VMEM),
        scratch_shapes=[
            pltpu.VMEM((rows + reach, cols + HALO, channels), jnp.float32),
            pltpu.VMEM(taps.shape, jnp.float32),
        ],
        compiler_params=pltpu.CompilerParams(vmem_limit_bytes=12 * 1024 * 1024),
        cost_estimate=pl.CostEstimate(
            flops=2 * rows * cols * channels * KERNEL * KERNEL,
            bytes_accessed=6 * rows * cols * channels,
            transcendentals=0,
        ),
        name="encode",
    )(place, tokens, above, beside, taps)


def fetch(place, grid_cols, pieces, ids, target, sems):
    copies = []
    for piece, parts in zip(pieces, ids, strict=True):
        size = piece.shape[0] // len(parts)
        for at, (mask_row, mask_col) in enumerate(parts):
            if mask_row is None:
                first = 0
            else:
                owner = (place[0] ^ mask_row) * grid_cols + (place[1] ^ mask_col)
                first = pl.multiple_of(owner * size, 16)
            copy = pltpu.make_async_copy(
                piece.at[pl.ds(at * size, size), pl.ds(0, target.shape[1])],
                target.at[pl.ds(first, size), :],
                sems.at[len(copies)],
            )
            copy.start()
            copies.append(copy)
    return copies


def attend_kernel(shape, ids, grid_cols, *refs):
    rows, cols = shape
    place, normed, rel_bias = refs[:3]
    context, weight, mixed, bias, sems = refs[3 + len(ids) :]
    channels = normed.shape[1]
    copies = fetch(place, grid_cols, refs[3 : 3 + len(ids)], ids, weight, sems)
    groups = channels // LANES
    for head in range(rel_bias.shape[0]):
        at = head % GROUP * SPOTS
        bias[head // GROUP, :, at : at + SPOTS] = rel_bias[head]
    for copy in copies:
        copy.wait()
    wide = 2 * LANES

    def project(index, _):
        lanes = pl.ds(pl.multiple_of(index * wide, wide), wide)
        mixed[:, lanes] = jnp.dot(
            normed[...], weight[:, lanes], preferred_element_type=jnp.float32
        ).astype(jnp.bfloat16)
        return 0

    lax.fori_loop(0, 3 * channels // wide, project, 0)

    window_cols = cols // WIN
    keys = GROUP * SPOTS
    query_at = lax.broadcasted_iota(jnp.int32, (SPOTS, keys), 0)
    key_at = lax.broadcasted_iota(jnp.int32, (SPOTS, keys), 1) % SPOTS
    row_differs = (query_at < SPOTS // 2) != (key_at < SPOTS // 2)
    col_differs = (query_at % WIN < SHIFT) != (key_at % WIN < SHIFT)
    lane = lax.broadcasted_iota(jnp.int32, (SPOTS, LANES), 1) // HD
    head_masks = [jnp.where(lane == h, 1.0, 0.0).astype(jnp.bfloat16) for h in range(GROUP)]
    block_row = lax.broadcasted_iota(jnp.int32, (keys, keys), 0) // SPOTS
    block_col = lax.broadcasted_iota(jnp.int32, (keys, keys), 1) // SPOTS
    same_head = jnp.where(block_row == block_col, 1.0, 0.0).astype(jnp.bfloat16)

    def window(index, _):
        part = pl.ds(pl.multiple_of(index * SPOTS, SPOTS), SPOTS)
        cut_rows = jnp.logical_and(place[0] == 0, index < window_cols)
        cut_cols = jnp.logical_and(place[1] == 0, index % window_cols == 0)
        hidden = (row_differs & cut_rows) | (col_differs & cut_cols)
        barrier = jnp.where(hidden, -1e30, 0.0)
        all_weights = []
        for group in range(groups):
            first = group * LANES
            query = mixed[part, first : first + LANES]
            key = mixed[part, channels + first : channels + first + LANES]
            key_all = jnp.concatenate([key * m for m in head_masks], axis=0)
            scores = lax.dot_general(
                query, key_all, (((1,), (1,)), ((), ())), preferred_element_type=jnp.float32
            )
            all_weights.append(jnp.exp(scores * HD ** (-0.5) + (bias[group] + barrier)))
        weights = jnp.concatenate(all_weights, axis=0)
        total = jnp.dot(
            jnp.minimum(weights, LARGEST).astype(jnp.bfloat16),
            same_head,
            preferred_element_type=jnp.float32,
        )
        probs = (weights * pl.reciprocal(total)).astype(jnp.bfloat16)
        for group in range(groups):
            first = group * LANES
            value = mixed[part, 2 * channels + first : 2 * channels + first + LANES]
            value_all = jnp.concatenate([value * m for m in head_masks], axis=0)
            context[part, first : first + LANES] = jnp.dot(
                probs[group * SPOTS : (group + 1) * SPOTS],
                value_all,
                preferred_element_type=jnp.float32,
            ).astype(jnp.bfloat16)
        return 0

    lax.fori_loop(0, rows * cols // SPOTS, window, 0)


def attend(place, shape, normed, rel_bias, pieces, grid_cols):
    rows, cols = shape
    channels = normed.shape[1]
    ids = [p[1] for p in pieces]
    return pl.pallas_call(
        functools.partial(attend_kernel, shape, ids, grid_cols),
        out_shape=jax.ShapeDtypeStruct((rows * cols, channels), jnp.bfloat16),
        in_specs=[SMEM, VMEM, VMEM] + [ANY] * len(pieces),
        out_specs=VMEM,
        scratch_shapes=[
            pltpu.VMEM((channels, 3 * channels), jnp.bfloat16),
            pltpu.VMEM((rows * cols, 3 * channels), jnp.bfloat16),
            pltpu.VMEM((channels // LANES, SPOTS, GROUP * SPOTS), jnp.float32),
            pltpu.SemaphoreType.DMA((sum(len(p) for p in ids),)),
        ],
        compiler_params=pltpu.CompilerParams(vmem_limit_bytes=14 * 1024 * 1024),
        cost_estimate=pl.CostEstimate(
            flops=2 * rows * cols * channels * 4 * channels,
            bytes_accessed=6 * channels * channels,
            transcendentals=rows * cols * SPOTS * channels // HD,
        ),
        name="attend",
    )(place, normed, rel_bias, *[p[0] for p in pieces])


def project_kernel(shape, ids, grid_cols, *refs):
    rows, cols = shape
    place, context, encoded = refs[:3]
    rolled, top, side, corner, weight, sems = refs[3 + len(ids) :]
    channels = context.shape[1]
    for copy in fetch(place, grid_cols, refs[3 : 3 + len(ids)], ids, weight, sems):
        copy.wait()
    window_cols = cols // WIN
    wide = 2 * LANES
    sublane = lax.broadcasted_iota(jnp.int32, (WIN, wide), 0)

    def finish(index, _):
        lanes = pl.ds(pl.multiple_of(index * wide, wide), wide)
        update = jnp.dot(context[...], weight[:, lanes], preferred_element_type=jnp.float32)
        summed = encoded[:, lanes].astype(jnp.float32) + update
        edge = []
        for row in range(rows):
            tiles = []
            for tile in range(window_cols):
                first = (row // WIN * window_cols + tile) * SPOTS + row % WIN * WIN
                tiles.append(summed[first : first + WIN])
            for pair in range(window_cols // 2):
                both = jnp.concatenate(tiles[2 * pair : 2 * pair + 2], axis=0)
                both = both.astype(jnp.bfloat16)
                at = pair * 2 * WIN
                rolled[row, at : at + 2 * WIN, lanes] = both
                if row < SHIFT:
                    top[row, at : at + 2 * WIN, lanes] = both
            edge.append(tiles[0])
        for quad in range(rows // 4):
            halves = [
                jnp.where(
                    sublane < SHIFT,
                    edge[4 * quad + two],
                    pltpu.roll(edge[4 * quad + two + 1], SHIFT, 0),
                )
                for two in (0, 2)
            ]
            packed = jnp.concatenate(halves, axis=0).astype(jnp.bfloat16)
            if quad == 0:
                corner[:, lanes] = packed
            else:
                side[(quad - 1) * 16 : quad * 16, lanes] = packed
        return 0

    lax.fori_loop(0, channels // wide, finish, 0)


def project(place, shape, context, encoded, pieces, grid_cols):
    rows, cols = shape
    channels = context.shape[1]
    bf16 = functools.partial(jax.ShapeDtypeStruct, dtype=jnp.bfloat16)
    ids = [p[1] for p in pieces]
    return pl.pallas_call(
        functools.partial(project_kernel, shape, ids, grid_cols),
        out_shape=(
            bf16((rows, cols, channels)),
            bf16((SHIFT, cols, channels)),
            bf16(((rows - SHIFT) * SHIFT, channels)),
            bf16((SHIFT * SHIFT, channels)),
        ),
        in_specs=[SMEM, VMEM, VMEM] + [ANY] * len(pieces),
        out_specs=(VMEM,) * 4,
        scratch_shapes=[
            pltpu.VMEM((channels, channels), jnp.bfloat16),
            pltpu.SemaphoreType.DMA((sum(len(p) for p in ids),)),
        ],
        compiler_params=pltpu.CompilerParams(vmem_limit_bytes=12 * 1024 * 1024),
        cost_estimate=pl.CostEstimate(
            flops=2 * rows * cols * channels * channels,
            bytes_accessed=2 * channels * channels,
            transcendentals=0,
        ),
        name="project",
    )(place, context, encoded, *[p[0] for p in pieces])


def dispatch_kernel(place, rolled, below, right, corner, position, *refs):
    rows, cols, channels = rolled.shape
    attended, outgoing, normed = refs[0], refs[1:-1], refs[-1]
    sublane = lax.broadcasted_iota(jnp.int32, (WIN, channels), 0)
    for row in range(rows):
        if row < rows - SHIFT:
            line, beside, at = rolled[row + SHIFT], right, row
        else:
            line, beside, at = below[row + SHIFT - rows], corner, row + SHIFT - rows
        line = line.astype(jnp.float32)
        tiles = [
            pltpu.roll(line[tile * WIN : (tile + 1) * WIN], SHIFT, 0) for tile in range(cols // WIN)
        ]
        block = at * SHIFT // 16 * 16
        last = beside[block : block + 16].astype(jnp.float32)
        within = at * SHIFT - block
        last = last[within // WIN * WIN : within // WIN * WIN + WIN]
        tiles.append(last if within % WIN else pltpu.roll(last, SHIFT, 0))
        line = jnp.concatenate(
            [
                jnp.where(sublane < SHIFT, tiles[tile], tiles[tile + 1])
                for tile in range(cols // WIN)
            ],
            axis=0,
        )
        attended[row * cols : (row + 1) * cols] = line.astype(jnp.bfloat16)
        normed[row * cols : (row + 1) * cols] = normalized(line)
    for mask, target in enumerate(outgoing):
        count = target.shape[0]
        spot = lax.broadcasted_iota(jnp.int32, (count, rows * cols), 0)
        spot = spot + (place[0] ^ mask) * count
        chosen = jnp.where(position[...] == spot, 1.0, 0.0).astype(jnp.bfloat16)
        target[...] = jnp.dot(
            chosen, normed[...], preferred_element_type=jnp.float32
        ).astype(jnp.bfloat16)


def dispatch(place, rolled, below, right, corner, position, grid_rows):
    rows, cols, channels = rolled.shape
    bf16 = functools.partial(jax.ShapeDtypeStruct, dtype=jnp.bfloat16)
    slot_rows = EXPERTS * CAP // grid_rows
    return pl.pallas_call(
        dispatch_kernel,
        out_shape=(bf16((rows * cols, channels)),) + (bf16((slot_rows, channels)),) * grid_rows,
        in_specs=[SMEM] + [VMEM] * 5,
        out_specs=(VMEM,) * (grid_rows + 1),
        scratch_shapes=[pltpu.VMEM((rows * cols, channels), jnp.bfloat16)],
        compiler_params=pltpu.CompilerParams(vmem_limit_bytes=24 * 1024 * 1024),
        name="dispatch",
    )(place, rolled, below, right, corner, position)


def expert_kernel(count, *refs):
    incoming, (weight_in, weight_out), results = refs[:count], refs[count : count + 2], refs[count + 2 :]
    rows = jnp.concatenate([ref[...] for ref in incoming], axis=0)
    hidden = lax.dot_general(
        rows, weight_in[0], (((1,), (1,)), ((), ())), preferred_element_type=jnp.float32
    )
    hidden = (0.5 * hidden * (1.0 + lax.erf(hidden * 0.5**0.5))).astype(jnp.bfloat16)
    result = jnp.dot(hidden, weight_out[0], preferred_element_type=jnp.float32)
    result = result.astype(jnp.bfloat16)
    for at, ref in enumerate(results):
        ref[...] = result[at * CAP : (at + 1) * CAP]


def serve(incoming, expert_in, expert_out):
    count = len(incoming)
    experts, hidden, channels = expert_in.shape
    slot = pl.BlockSpec((CAP, channels), lambda e: (e, 0))
    weight = pl.BlockSpec((1, hidden, channels), lambda e: (e, 0, 0))
    return pl.pallas_call(
        functools.partial(expert_kernel, count),
        grid=(experts,),
        out_shape=tuple(jax.ShapeDtypeStruct(x.shape, x.dtype) for x in incoming),
        in_specs=[slot] * count + [weight, weight],
        out_specs=(slot,) * count,
        compiler_params=pltpu.CompilerParams(vmem_limit_bytes=32 * 1024 * 1024),
        cost_estimate=pl.CostEstimate(
            flops=4 * count * CAP * experts * hidden * channels,
            bytes_accessed=4 * experts * hidden * channels,
            transcendentals=count * CAP * experts * hidden,
        ),
        name="experts",
    )(*incoming, expert_in, expert_out)


def combine_kernel(place, attended, position, constant_at, table, *refs):
    results, output = refs[:-1], refs[-1]
    tokens = attended.shape[0]
    total = attended[...].astype(jnp.float32)
    for mask, result in enumerate(results):
        count = result.shape[0]
        spot = lax.broadcasted_iota(jnp.int32, (tokens, count), 1)
        spot = spot + (place[0] ^ mask) * count
        chosen = jnp.where(position[...] == spot, 1.0, 0.0).astype(jnp.bfloat16)
        total = total + jnp.dot(chosen, result[...], preferred_element_type=jnp.float32)
    entries = table.shape[0]
    spot = lax.broadcasted_iota(jnp.int32, (tokens, entries), 1)
    chosen = jnp.where(constant_at[...] == spot, 1.0, 0.0).astype(jnp.bfloat16)
    rest = table[...]
    constant = None
    for _ in range(3):
        part = rest.astype(jnp.bfloat16)
        rest = rest - part.astype(jnp.float32)
        term = jnp.dot(chosen, part, preferred_element_type=jnp.float32)
        constant = term if constant is None else constant + term
    output[...] = (total + constant).astype(jnp.bfloat16)


def combine(place, attended, position, constant_at, table, results):
    return pl.pallas_call(
        combine_kernel,
        out_shape=jax.ShapeDtypeStruct(attended.shape, jnp.bfloat16),
        in_specs=[SMEM] + [VMEM] * (4 + len(results)),
        out_specs=VMEM,
        compiler_params=pltpu.CompilerParams(vmem_limit_bytes=24 * 1024 * 1024),
        name="combine",
    )(place, attended, position, constant_at, table, *results)


def stacked(parts):
    return jnp.concatenate([p[0] for p in parts], axis=0), sum([p[1] for p in parts], [])


def along(part, axis, mask):
    array, ids = part
    change = (mask, 0) if axis == "gy" else (0, mask)
    return exchanged(array, axis, mask), [(a ^ change[0], b ^ change[1]) for a, b in ids]


def held(*values):
    return lax.optimization_barrier(values)


def shards(
    tokens,
    conv_kernel,
    project_in,
    project_out,
    rel_bias,
    expert_in,
    expert_out,
    const_table,
    expert_ids,
    slots,
    const_index,
):
    rows, cols, channels = tokens.shape
    grid_rows, grid_cols = lax.axis_size("gy"), lax.axis_size("gx")
    place = jnp.stack([lax.axis_index("gy"), lax.axis_index("gx")]).astype(jnp.int32)
    reach = KERNEL // 2 + SHIFT
    above = shifted(tokens[rows - reach :], "gy", 1)
    quick = grid_rows == 4 and grid_cols == 4
    if quick:
        own = [(0, 0)]
        line = [exchanged(project_in, "gx", mask) for mask in (3, 2, 1)]
        both = jnp.concatenate([project_in, project_out], axis=1)
        facing = exchanged(both, "gy", 2)
        *line, facing, above = held(*line, facing, above)
    edge = jnp.concatenate([above[:, cols - HALO :], tokens[:, cols - HALO :]], axis=0)
    beside = shifted(edge, "gx", 1)
    if quick:
        line = stacked([(array, [(0, mask)]) for array, mask in zip(line, (3, 2, 1), strict=True)])
        facing = (facing, [(2, 0)])
        pair = stacked([(project_out, own), (facing[0][:, 3 * channels :], facing[1])])
        far = along(line, "gy", 2)
        plane = stacked([pair] + [along(pair, "gx", mask) for mask in (3, 2, 1)])
    else:
        whole = [(None, None)]
        pieces_in = [(lax.all_gather(project_in, ("gy", "gx"), axis=0, tiled=True), whole)]
        pieces_out = [(lax.all_gather(project_out, ("gy", "gx"), axis=0, tiled=True), whole)]
    encoded, normed = encode(place, tokens, above, beside, conv_kernel)
    if quick:
        near = [(project_in, own), line, facing]
        pieces_in = near + [far] + [along(part, "gy", 1) for part in near + [far]]
        pieces_out = [plane, along(plane, "gy", 1)]
    context = attend(place, (rows, cols), normed, rel_bias, pieces_in, grid_cols)
    rolled, top, side, corner = project(
        place, (rows, cols), context, encoded, pieces_out, grid_cols
    )
    below = shifted(top, "gy", -1)
    right = shifted(side, "gx", -1)
    last = shifted_both(corner, -1)
    expert_of, slot_of = expert_ids.reshape(-1), slots.reshape(-1)
    position = jnp.where(expert_of < EXPERTS, expert_of * CAP + slot_of, -1)
    constant_at = jnp.where(expert_of == EXPERTS, const_index.reshape(-1), -1)
    attended, *outgoing = dispatch(
        place, rolled, below, right, last, position[None, :], grid_rows
    )
    incoming = [outgoing[0]] + [exchanged(outgoing[m], "gy", m) for m in range(1, grid_rows)]
    served = serve(incoming, expert_in, expert_out)
    results = [served[0]] + [exchanged(served[m], "gy", m) for m in range(1, grid_rows)]
    output = combine(
        place, attended, position[:, None], constant_at[:, None], const_table, results
    )
    return output.reshape(rows, cols, channels)


def solution(mesh):
    placed = (
        P(("groups", "gy"), "gx", None),
        P(),
        P(("gy", "gx"), None),
        P(("gy", "gx"), None),
        P(),
        P("gy", None, None),
        P("gy", None, None),
        P(),
        P(("groups", "gy"), "gx"),
        P(("groups", "gy"), "gx"),
        P(("groups", "gy"), "gx"),
    )
    return jax.shard_map(
        shards,
        mesh=mesh,
        in_specs=placed,
        out_specs=P(("groups", "gy"), "gx", None),
        check_vma=False,
    )
```

```python
import functools

import jax
import jax.numpy as jnp
from jax import lax
from jax.experimental import pallas as pl
from jax.experimental.pallas import tpu as pltpu
from jax.sharding import PartitionSpec as P

HD = 32
EXPERTS = 32
WIN = 8
SHIFT = 4
KERNEL = 7
CAP = 16
LANES = 128
GROUP = LANES // HD
SPOTS = WIN * WIN
HALO = 8
VMEM = pl.BlockSpec(memory_space=pltpu.VMEM)
SMEM = pl.BlockSpec(memory_space=pltpu.SMEM)
ANY = pl.BlockSpec(memory_space=pl.ANY)
HBM = pl.BlockSpec(memory_space=pltpu.HBM)
LARGEST = 3.38e38
DEPTH = 3
PARTS = 2


def lasting(microseconds):
    return pl.CostEstimate(
        flops=int(microseconds * 1.15e9), bytes_accessed=0, transcendentals=0
    )


def shifted(x, axis, by):
    size = lax.axis_size(axis)
    return lax.ppermute(x, axis, [(i, (i + by) % size) for i in range(size)])


def shifted_both(x, by):
    rows, cols = lax.axis_size("gy"), lax.axis_size("gx")
    pairs = [
        (i * cols + j, ((i + by) % rows) * cols + (j + by) % cols)
        for i in range(rows)
        for j in range(cols)
    ]
    return lax.ppermute(x, ("gy", "gx"), pairs)


def exchanged(x, axis, mask):
    size = lax.axis_size(axis)
    return lax.ppermute(x, axis, [(i, i ^ mask) for i in range(size)])


def normalized(values):
    centred = values - jnp.mean(values, axis=-1, keepdims=True)
    spread = jnp.mean(centred * centred, axis=-1, keepdims=True)
    return (centred * lax.rsqrt(spread + 1e-05)).astype(jnp.bfloat16)


def encode_kernel(
    place, tokens_at, above, beside, taps_at, rel_bias, encoded, normed, bias, extended, weights, tokens, taps, sems
):
    copies = [
        pltpu.make_async_copy(tokens_at, tokens, sems.at[0]),
        pltpu.make_async_copy(taps_at, taps, sems.at[1]),
    ]
    for copy in copies:
        copy.start()
    rows, cols, channels = tokens.shape
    reach = KERNEL // 2 + SHIFT
    extended[:, :HALO] = beside[...].astype(jnp.float32)
    extended[:reach, HALO:] = above[...].astype(jnp.float32)
    for copy in copies:
        copy.wait()
    extended[reach:, HALO:] = tokens[...].astype(jnp.float32)
    weights[...] = taps[...].astype(jnp.float32)
    for head in range(rel_bias.shape[0]):
        at = head % GROUP * SPOTS
        bias[head // GROUP, :, at : at + SPOTS] = rel_bias[head]
    inner_row = jnp.where(place[0] == 0, 0.0, 1.0)
    first_col = place[1] == 0
    window_cols = cols // WIN
    col = lax.broadcasted_iota(jnp.int32, (WIN, LANES), 0)

    def block(index, _):
        lanes = pl.ds(pl.multiple_of(index * LANES, LANES), LANES)
        for tile in range(window_cols):
            sums = [None] * rows
            for col_off in range(KERNEL):
                column = [
                    jnp.broadcast_to(weights[row_off, pl.ds(col_off, 1), lanes], (WIN, LANES))
                    for row_off in range(KERNEL)
                ]
                if tile == 0:
                    near = (col < SHIFT) == (col + col_off < reach)
                    keep = jnp.where(near | jnp.logical_not(first_col), 1.0, 0.0)
                for row in range(rows + KERNEL - 1):
                    here = extended[row, tile * WIN : tile * WIN + WIN, lanes]
                    after = extended[row, (tile + 1) * WIN : (tile + 2) * WIN, lanes]
                    line = jnp.where(col > col_off, here, after)
                    line = pltpu.roll(line, WIN - 1 - col_off, 0)
                    if tile == 0:
                        line = line * keep
                    cut = line * inner_row if SHIFT <= row < reach + KERNEL // 2 else line
                    for out in range(max(0, row - KERNEL + 1), min(rows, row + 1)):
                        row_off = row - out
                        same = (out < SHIFT) == (row < reach)
                        term = (line if same else cut) * column[row_off]
                        if row_off == KERNEL // 2 and col_off == KERNEL // 2:
                            term = term + line
                        sums[out] = term if sums[out] is None else sums[out] + term
            for window_row in range(rows // WIN):
                stacked = jnp.concatenate(sums[window_row * WIN : (window_row + 1) * WIN], axis=0)
                first = (window_row * window_cols + tile) * SPOTS
                encoded[first : first + SPOTS, lanes] = stacked.astype(jnp.bfloat16)
        return 0

    lax.fori_loop(0, channels // LANES, block, 0)

    def norm(index, _):
        part = pl.ds(pl.multiple_of(index * SPOTS, SPOTS), SPOTS)
        normed[part, :] = normalized(encoded[part, :].astype(jnp.float32))
        return 0

    lax.fori_loop(0, rows * cols // SPOTS, norm, 0)


def encode(place, tokens, above, beside, taps, rel_bias):
    rows, cols, channels = tokens.shape
    flat = jax.ShapeDtypeStruct((rows * cols, channels), jnp.bfloat16)
    reach = KERNEL // 2 + SHIFT
    bias_shape = (rel_bias.shape[0] // GROUP, SPOTS, GROUP * SPOTS)
    return pl.pallas_call(
        encode_kernel,
        out_shape=(flat, flat, jax.ShapeDtypeStruct(bias_shape, jnp.float32)),
        in_specs=[SMEM, HBM, VMEM, VMEM, HBM, VMEM],
        out_specs=(VMEM, VMEM, VMEM),
        scratch_shapes=[
            pltpu.VMEM((rows + reach, cols + HALO, channels), jnp.float32),
            pltpu.VMEM(taps.shape, jnp.float32),
            pltpu.VMEM(tokens.shape, jnp.bfloat16),
            pltpu.VMEM(taps.shape, jnp.bfloat16),
            pltpu.SemaphoreType.DMA((2,)),
        ],
        compiler_params=pltpu.CompilerParams(vmem_limit_bytes=12 * 1024 * 1024),
        cost_estimate=lasting(0.1),
        name="encode",
    )(place, tokens, above, beside, taps, rel_bias)


def fetch(place, grid_cols, pieces, ids, target, sems):
    copies = []
    for piece, (parts, half) in zip(pieces, ids, strict=True):
        size = piece.shape[0] // len(parts)
        wide = min(piece.shape[1], target.shape[1])
        left = 0 if half is None else pl.multiple_of((place[2] ^ half) * wide, LANES)
        for at, (mask_row, mask_col) in enumerate(parts):
            if mask_row is None:
                first = 0
            else:
                owner = (place[0] ^ mask_row) * grid_cols + (place[1] ^ mask_col)
                first = pl.multiple_of(owner * size, 16)
            copy = pltpu.make_async_copy(
                piece.at[pl.ds(at * size, size), pl.ds(0, wide)],
                target.at[pl.ds(first, size), pl.ds(left, wide)],
                sems.at[len(copies)],
            )
            copy.start()
            copies.append(copy)
    return copies


def attend_kernel(shape, ids, grid_cols, *refs):
    rows, cols = shape
    place, normed, bias = refs[:3]
    context, weight, mixed, sems = refs[3 + len(ids) :]
    channels = normed.shape[1]
    copies = fetch(place, grid_cols, refs[3 : 3 + len(ids)], ids, weight, sems)
    groups = channels // LANES
    for copy in copies:
        copy.wait()
    wide = channels

    def project(index, _):
        lanes = pl.ds(pl.multiple_of(index * wide, wide), wide)
        mixed[:, lanes] = jnp.dot(
            normed[...], weight[:, lanes], preferred_element_type=jnp.float32
        ).astype(jnp.bfloat16)
        return 0

    lax.fori_loop(0, 3 * channels // wide, project, 0)

    window_cols = cols // WIN
    keys = GROUP * SPOTS
    query_at = lax.broadcasted_iota(jnp.int32, (SPOTS, keys), 0)
    key_at = lax.broadcasted_iota(jnp.int32, (SPOTS, keys), 1) % SPOTS
    row_differs = (query_at < SPOTS // 2) != (key_at < SPOTS // 2)
    col_differs = (query_at % WIN < SHIFT) != (key_at % WIN < SHIFT)
    lane = lax.broadcasted_iota(jnp.int32, (SPOTS, LANES), 1) // HD
    head_masks = [jnp.where(lane == h, 1.0, 0.0).astype(jnp.bfloat16) for h in range(GROUP)]
    block_row = lax.broadcasted_iota(jnp.int32, (keys, keys), 0) // SPOTS
    block_col = lax.broadcasted_iota(jnp.int32, (keys, keys), 1) // SPOTS
    same_head = jnp.where(block_row == block_col, 1.0, 0.0).astype(jnp.bfloat16)

    def window(index, _):
        part = pl.ds(pl.multiple_of(index * SPOTS, SPOTS), SPOTS)
        cut_rows = jnp.logical_and(place[0] == 0, index < window_cols)
        cut_cols = jnp.logical_and(place[1] == 0, index % window_cols == 0)
        hidden = (row_differs & cut_rows) | (col_differs & cut_cols)
        barrier = jnp.where(hidden, -1e30, 0.0)
        all_weights = []
        for group in range(groups):
            first = group * LANES
            query = mixed[part, first : first + LANES]
            key = mixed[part, channels + first : channels + first + LANES]
            key_all = jnp.concatenate([key * m for m in head_masks], axis=0)
            scores = lax.dot_general(
                query, key_all, (((1,), (1,)), ((), ())), preferred_element_type=jnp.float32
            )
            all_weights.append(jnp.exp(scores * HD ** (-0.5) + (bias[group] + barrier)))
        weights = jnp.concatenate(all_weights, axis=0)
        total = jnp.dot(
            jnp.minimum(weights, LARGEST).astype(jnp.bfloat16),
            same_head,
            preferred_element_type=jnp.float32,
        )
        probs = (weights * pl.reciprocal(total)).astype(jnp.bfloat16)
        for group in range(groups):
            first = group * LANES
            value = mixed[part, 2 * channels + first : 2 * channels + first + LANES]
            value_all = jnp.concatenate([value * m for m in head_masks], axis=0)
            context[part, first : first + LANES] = jnp.dot(
                probs[group * SPOTS : (group + 1) * SPOTS],
                value_all,
                preferred_element_type=jnp.float32,
            ).astype(jnp.bfloat16)
        return 0

    lax.fori_loop(0, rows * cols // SPOTS, window, 0)


def attend(place, shape, normed, bias, pieces, grid_cols):
    rows, cols = shape
    channels = normed.shape[1]
    ids = [p[1:] for p in pieces]
    return pl.pallas_call(
        functools.partial(attend_kernel, shape, ids, grid_cols),
        out_shape=jax.ShapeDtypeStruct((rows * cols, channels), jnp.bfloat16),
        in_specs=[SMEM, VMEM, VMEM] + [ANY] * len(pieces),
        out_specs=VMEM,
        scratch_shapes=[
            pltpu.VMEM((channels, 3 * channels), jnp.bfloat16),
            pltpu.VMEM((rows * cols, 3 * channels), jnp.bfloat16),
            pltpu.SemaphoreType.DMA((sum(len(p[0]) for p in ids),)),
        ],
        compiler_params=pltpu.CompilerParams(vmem_limit_bytes=18 * 1024 * 1024),
        cost_estimate=lasting(10),
        name="attend",
    )(place, normed, bias, *[p[0] for p in pieces])


def project_kernel(shape, ids, grid_cols, *refs):
    rows, cols = shape
    place, context, encoded = refs[:3]
    rolled, top, side, corner, weight, sems = refs[3 + len(ids) :]
    channels = context.shape[1]
    for copy in fetch(place, grid_cols, refs[3 : 3 + len(ids)], ids, weight, sems):
        copy.wait()
    window_cols = cols // WIN
    wide = 2 * LANES
    sublane = lax.broadcasted_iota(jnp.int32, (WIN, wide), 0)

    def finish(index, _):
        lanes = pl.ds(pl.multiple_of(index * wide, wide), wide)
        update = jnp.dot(context[...], weight[:, lanes], preferred_element_type=jnp.float32)
        summed = encoded[:, lanes].astype(jnp.float32) + update
        edge = []
        for row in range(rows):
            tiles = []
            for tile in range(window_cols):
                first = (row // WIN * window_cols + tile) * SPOTS + row % WIN * WIN
                tiles.append(summed[first : first + WIN])
            for pair in range(window_cols // 2):
                both = jnp.concatenate(tiles[2 * pair : 2 * pair + 2], axis=0)
                both = both.astype(jnp.bfloat16)
                at = pair * 2 * WIN
                rolled[row, at : at + 2 * WIN, lanes] = both
                if row < SHIFT:
                    top[row, at : at + 2 * WIN, lanes] = both
            edge.append(tiles[0])
        for quad in range(rows // 4):
            halves = [
                jnp.where(
                    sublane < SHIFT,
                    edge[4 * quad + two],
                    pltpu.roll(edge[4 * quad + two + 1], SHIFT, 0),
                )
                for two in (0, 2)
            ]
            packed = jnp.concatenate(halves, axis=0).astype(jnp.bfloat16)
            if quad == 0:
                corner[:, lanes] = packed
            else:
                side[(quad - 1) * 16 : quad * 16, lanes] = packed
        return 0

    lax.fori_loop(0, channels // wide, finish, 0)


def project(place, shape, context, encoded, pieces, grid_cols):
    rows, cols = shape
    channels = context.shape[1]
    bf16 = functools.partial(jax.ShapeDtypeStruct, dtype=jnp.bfloat16)
    ids = [p[1:] for p in pieces]
    return pl.pallas_call(
        functools.partial(project_kernel, shape, ids, grid_cols),
        out_shape=(
            bf16((rows, cols, channels)),
            bf16((SHIFT, cols, channels)),
            bf16(((rows - SHIFT) * SHIFT, channels)),
            bf16((SHIFT * SHIFT, channels)),
        ),
        in_specs=[SMEM, VMEM, VMEM] + [ANY] * len(pieces),
        out_specs=(VMEM,) * 4,
        scratch_shapes=[
            pltpu.VMEM((channels, channels), jnp.bfloat16),
            pltpu.SemaphoreType.DMA((sum(len(p[0]) for p in ids),)),
        ],
        compiler_params=pltpu.CompilerParams(vmem_limit_bytes=12 * 1024 * 1024),
        cost_estimate=lasting(3),
        name="project",
    )(place, context, encoded, *[p[0] for p in pieces])


def dispatch_kernel(place, rolled, below, right, corner, position, *refs):
    rows, cols, channels = rolled.shape
    attended, outgoing, normed = refs[0], refs[1:-1], refs[-1]
    sublane = lax.broadcasted_iota(jnp.int32, (WIN, channels), 0)
    for row in range(rows):
        if row < rows - SHIFT:
            line, beside, at = rolled[row + SHIFT], right, row
        else:
            line, beside, at = below[row + SHIFT - rows], corner, row + SHIFT - rows
        line = line.astype(jnp.float32)
        tiles = [
            pltpu.roll(line[tile * WIN : (tile + 1) * WIN], SHIFT, 0) for tile in range(cols // WIN)
        ]
        block = at * SHIFT // 16 * 16
        last = beside[block : block + 16].astype(jnp.float32)
        within = at * SHIFT - block
        last = last[within // WIN * WIN : within // WIN * WIN + WIN]
        tiles.append(last if within % WIN else pltpu.roll(last, SHIFT, 0))
        line = jnp.concatenate(
            [
                jnp.where(sublane < SHIFT, tiles[tile], tiles[tile + 1])
                for tile in range(cols // WIN)
            ],
            axis=0,
        )
        attended[row * cols : (row + 1) * cols] = line.astype(jnp.bfloat16)
        normed[row * cols : (row + 1) * cols] = normalized(line)
    for mask, target in enumerate(outgoing):
        count = target.shape[0]
        spot = lax.broadcasted_iota(jnp.int32, (count, rows * cols), 0)
        spot = spot + (place[0] ^ mask) * count
        chosen = jnp.where(position[...] == spot, 1.0, 0.0).astype(jnp.bfloat16)
        target[...] = jnp.dot(
            chosen, normed[...], preferred_element_type=jnp.float32
        ).astype(jnp.bfloat16)


def dispatch(place, rolled, below, right, corner, position, grid_rows):
    rows, cols, channels = rolled.shape
    bf16 = functools.partial(jax.ShapeDtypeStruct, dtype=jnp.bfloat16)
    slot_rows = EXPERTS * CAP // grid_rows
    return pl.pallas_call(
        dispatch_kernel,
        out_shape=(bf16((rows * cols, channels)),) + (bf16((slot_rows, channels)),) * grid_rows,
        in_specs=[SMEM] + [VMEM] * 5,
        out_specs=(VMEM,) * (grid_rows + 1),
        scratch_shapes=[pltpu.VMEM((rows * cols, channels), jnp.bfloat16)],
        compiler_params=pltpu.CompilerParams(vmem_limit_bytes=24 * 1024 * 1024),
        name="dispatch",
    )(place, rolled, below, right, corner, position)


def expert_kernel(count, *refs):
    incoming, (all_in, all_out), results = refs[:count], refs[count : count + 2], refs[count + 2 : -3]
    held_in, held_out, sems = refs[-3:]
    experts, hidden_units = all_in.shape[:2]
    part = hidden_units // PARTS

    def copies(expert):
        slot = expert % held_in.shape[0]
        return [
            pltpu.make_async_copy(
                source.at[expert, pl.ds(at * part, part), :],
                target.at[slot, pl.ds(at * part, part), :],
                sems.at[slot, which, at],
            )
            for which, (source, target) in enumerate(((all_in, held_in), (all_out, held_out)))
            for at in range(PARTS)
        ]

    for expert in range(min(experts, held_in.shape[0])):
        for copy in copies(expert):
            copy.start()
    for expert in range(experts):
        slot = expert % held_in.shape[0]
        own = pl.ds(expert * CAP, CAP)
        rows = jnp.concatenate([ref[own, :] for ref in incoming], axis=0)
        arriving = copies(expert)
        for copy in arriving[:PARTS]:
            copy.wait()
        hidden = lax.dot_general(
            rows, held_in[slot], (((1,), (1,)), ((), ())), preferred_element_type=jnp.float32
        )
        hidden = (0.5 * hidden * (1.0 + lax.erf(hidden * 0.5**0.5))).astype(jnp.bfloat16)
        for copy in arriving[PARTS:]:
            copy.wait()
        result = jnp.dot(hidden, held_out[slot], preferred_element_type=jnp.float32)
        result = result.astype(jnp.bfloat16)
        for at, ref in enumerate(results):
            ref[own, :] = result[at * CAP : (at + 1) * CAP]
        if expert + held_in.shape[0] < experts:
            for copy in copies(expert + held_in.shape[0]):
                copy.start()


def serve(incoming, expert_in, expert_out):
    count = len(incoming)
    experts, hidden, channels = expert_in.shape
    depth = min(DEPTH, experts)
    return pl.pallas_call(
        functools.partial(expert_kernel, count),
        out_shape=tuple(jax.ShapeDtypeStruct(x.shape, x.dtype) for x in incoming),
        in_specs=[VMEM] * count + [HBM, HBM],
        out_specs=(VMEM,) * count,
        scratch_shapes=[
            pltpu.VMEM((depth, hidden, channels), jnp.bfloat16),
            pltpu.VMEM((depth, hidden, channels), jnp.bfloat16),
            pltpu.SemaphoreType.DMA((depth, 2, PARTS)),
        ],
        compiler_params=pltpu.CompilerParams(vmem_limit_bytes=56 * 1024 * 1024),
        cost_estimate=lasting(12),
        name="experts",
    )(*incoming, expert_in, expert_out)


def combine_kernel(place, attended, position, constant_at, table, *refs):
    results, output = refs[:-1], refs[-1]
    tokens = attended.shape[0]
    total = attended[...].astype(jnp.float32)
    for mask, result in enumerate(results):
        count = result.shape[0]
        spot = lax.broadcasted_iota(jnp.int32, (tokens, count), 1)
        spot = spot + (place[0] ^ mask) * count
        chosen = jnp.where(position[...] == spot, 1.0, 0.0).astype(jnp.bfloat16)
        total = total + jnp.dot(chosen, result[...], preferred_element_type=jnp.float32)
    entries = table.shape[0]
    spot = lax.broadcasted_iota(jnp.int32, (tokens, entries), 1)
    chosen = jnp.where(constant_at[...] == spot, 1.0, 0.0).astype(jnp.bfloat16)
    rest = table[...]
    constant = None
    for _ in range(3):
        part = rest.astype(jnp.bfloat16)
        rest = rest - part.astype(jnp.float32)
        term = jnp.dot(chosen, part, preferred_element_type=jnp.float32)
        constant = term if constant is None else constant + term
    output[...] = (total + constant).astype(jnp.bfloat16)


def combine(place, attended, position, constant_at, table, results):
    return pl.pallas_call(
        combine_kernel,
        out_shape=jax.ShapeDtypeStruct(attended.shape, jnp.bfloat16),
        in_specs=[SMEM] + [VMEM] * (4 + len(results)),
        out_specs=VMEM,
        compiler_params=pltpu.CompilerParams(vmem_limit_bytes=24 * 1024 * 1024),
        name="combine",
    )(place, attended, position, constant_at, table, *results)


def stacked(parts):
    ids = sum([part[1] for part in parts], [])
    return jnp.concatenate([part[0] for part in parts], axis=0), ids, None


def along(part, axis, mask):
    array, ids, half = part
    moved = exchanged(array, axis, mask)
    if axis == "groups":
        return moved, ids, half ^ mask
    change = (mask, 0) if axis == "gy" else (0, mask)
    return moved, [(a ^ change[0], b ^ change[1]) for a, b in ids], half


def diagonal(part, mask):
    array, ids, half = part
    groups, rows = lax.axis_size("groups"), lax.axis_size("gy")
    pairs = [
        (i * rows + j, (i ^ 1) * rows + (j ^ mask)) for i in range(groups) for j in range(rows)
    ]
    moved = lax.ppermute(array, ("groups", "gy"), pairs)
    return moved, [(a ^ mask, b) for a, b in ids], half ^ 1


def held(*values):
    return lax.optimization_barrier(values)


def shards(
    tokens,
    conv_kernel,
    project_in,
    project_out,
    rel_bias,
    expert_in,
    expert_out,
    const_table,
    expert_ids,
    slots,
    const_index,
):
    rows, cols, channels = tokens.shape
    grid_rows, grid_cols = lax.axis_size("gy"), lax.axis_size("gx")
    place = jnp.stack([lax.axis_index(axis) for axis in ("gy", "gx", "groups")]).astype(jnp.int32)
    reach = KERNEL // 2 + SHIFT
    quick = grid_rows == 4 and grid_cols == 4 and lax.axis_size("groups") == 2
    above = shifted(tokens[rows - reach :], "gy", 1)
    if quick:
        beyond = exchanged(project_in, "gx", 1)
        facing_out = exchanged(project_out, "gy", 2)
        beyond, facing_out, above = held(beyond, facing_out, above)
        two = (jnp.concatenate([project_in, beyond], axis=0), [(0, 0), (0, 1)], None)
        wide = two[0].shape[1] // 2
        mine = lax.dynamic_slice_in_dim(two[0], lax.axis_index("groups") * wide, wide, axis=1)
        far = along((mine, two[1], 0), "gx", 2)
        facing = along(two, "gy", 2)
    edge = jnp.concatenate([above[:, cols - HALO :], tokens[:, cols - HALO :]], axis=0)
    beside = shifted(edge, "gx", 1)
    encoded, normed, bias = encode(place, tokens, above, beside, conv_kernel, rel_bias)
    if quick:
        first, second, normed = held(far[0], facing[0], normed)
        far, facing = (first, *far[1:]), (second, *facing[1:])
        across = along(far, "gy", 2)
        pair = stacked([(project_out, [(0, 0)]), (facing_out, [(2, 0)])])
        plane = [pair] + [along(pair, "gx", mask) for mask in (3, 2, 1)]
        far_rest, across_rest = along(far, "groups", 1), diagonal(far, 2)
        pieces_in = [two, facing, far, far_rest, across]
        pieces_in = pieces_in + [along(part, "gy", 1) for part in pieces_in]
        pieces_in = pieces_in + [across_rest, along(across_rest, "gy", 1)]
    else:
        whole = [(None, None)]
        pieces_in = [(lax.all_gather(project_in, ("gy", "gx"), axis=0, tiled=True), whole, None)]
        pieces_out = [(lax.all_gather(project_out, ("gy", "gx"), axis=0, tiled=True), whole, None)]
    context = attend(place, (rows, cols), normed, bias, pieces_in, grid_cols)
    if quick:
        *arrays, context = held(*[part[0] for part in plane], context)
        plane = stacked([(array, *part[1:]) for array, part in zip(arrays, plane, strict=True)])
        pieces_out = [plane, along(plane, "gy", 1)]
    rolled, top, side, corner = project(
        place, (rows, cols), context, encoded, pieces_out, grid_cols
    )
    below = shifted(top, "gy", -1)
    right = shifted(side, "gx", -1)
    last = shifted_both(corner, -1)
    expert_of, slot_of = expert_ids.reshape(-1), slots.reshape(-1)
    position = jnp.where(expert_of < EXPERTS, expert_of * CAP + slot_of, -1)
    constant_at = jnp.where(expert_of == EXPERTS, const_index.reshape(-1), -1)
    attended, *outgoing = dispatch(
        place, rolled, below, right, last, position[None, :], grid_rows
    )
    incoming = [outgoing[0]] + [exchanged(outgoing[m], "gy", m) for m in range(1, grid_rows)]
    served = serve(incoming, expert_in, expert_out)
    results = [served[0]] + [exchanged(served[m], "gy", m) for m in range(1, grid_rows)]
    output = combine(
        place, attended, position[:, None], constant_at[:, None], const_table, results
    )
    return output.reshape(rows, cols, channels)


def solution(mesh):
    placed = (
        P(("groups", "gy"), "gx", None),
        P(),
        P(("gy", "gx"), None),
        P(("gy", "gx"), None),
        P(),
        P("gy", None, None),
        P("gy", None, None),
        P(),
        P(("groups", "gy"), "gx"),
        P(("groups", "gy"), "gx"),
        P(("groups", "gy"), "gx"),
    )
    return jax.shard_map(
        shards,
        mesh=mesh,
        in_specs=placed,
        out_specs=P(("groups", "gy"), "gx", None),
        check_vma=False,
    )
```

```python
import functools

import jax
import jax.numpy as jnp
from jax import lax
from jax.experimental import pallas as pl
from jax.experimental.pallas import tpu as pltpu
from jax.sharding import PartitionSpec as P

HD = 32
EXPERTS = 32
WIN = 8
SHIFT = 4
KERNEL = 7
CAP = 16
LANES = 128
GROUP = LANES // HD
SPOTS = WIN * WIN
HALO = 8
VMEM = pl.BlockSpec(memory_space=pltpu.VMEM)
SMEM = pl.BlockSpec(memory_space=pltpu.SMEM)
ANY = pl.BlockSpec(memory_space=pl.ANY)
HBM = pl.BlockSpec(memory_space=pltpu.HBM)
LARGEST = 3.38e38


def lasting(microseconds):
    return pl.CostEstimate(
        flops=int(microseconds * 1.15e9), bytes_accessed=0, transcendentals=0
    )


def shifted(x, axis, by):
    size = lax.axis_size(axis)
    return lax.ppermute(x, axis, [(i, (i + by) % size) for i in range(size)])


def shifted_both(x, by):
    rows, cols = lax.axis_size("gy"), lax.axis_size("gx")
    pairs = [
        (i * cols + j, ((i + by) % rows) * cols + (j + by) % cols)
        for i in range(rows)
        for j in range(cols)
    ]
    return lax.ppermute(x, ("gy", "gx"), pairs)


def exchanged(x, axis, mask):
    size = lax.axis_size(axis)
    return lax.ppermute(x, axis, [(i, i ^ mask) for i in range(size)])


def normalized(values):
    centred = values - jnp.mean(values, axis=-1, keepdims=True)
    spread = jnp.mean(centred * centred, axis=-1, keepdims=True)
    return (centred * lax.rsqrt(spread + 1e-05)).astype(jnp.bfloat16)


def encode_kernel(
    place, tokens_at, above, beside, taps_at, rel_bias, encoded, normed, bias, extended, weights, tokens, taps, sems
):
    copies = [
        pltpu.make_async_copy(tokens_at, tokens, sems.at[0]),
        pltpu.make_async_copy(taps_at, taps, sems.at[1]),
    ]
    for copy in copies:
        copy.start()
    rows, cols, channels = tokens.shape
    reach = KERNEL // 2 + SHIFT
    extended[:, :HALO] = beside[...].astype(jnp.float32)
    extended[:reach, HALO:] = above[...].astype(jnp.float32)
    for copy in copies:
        copy.wait()
    extended[reach:, HALO:] = tokens[...].astype(jnp.float32)
    weights[...] = taps[...].astype(jnp.float32)
    for head in range(rel_bias.shape[0]):
        at = head % GROUP * SPOTS
        bias[head // GROUP, :, at : at + SPOTS] = rel_bias[head]
    inner_row = jnp.where(place[0] == 0, 0.0, 1.0)
    first_col = place[1] == 0
    window_cols = cols // WIN
    col = lax.broadcasted_iota(jnp.int32, (WIN, LANES), 0)

    def block(index, _):
        lanes = pl.ds(pl.multiple_of(index * LANES, LANES), LANES)
        for tile in range(window_cols):
            sums = [None] * rows
            for col_off in range(KERNEL):
                column = [
                    jnp.broadcast_to(weights[row_off, pl.ds(col_off, 1), lanes], (WIN, LANES))
                    for row_off in range(KERNEL)
                ]
                if tile == 0:
                    near = (col < SHIFT) == (col + col_off < reach)
                    keep = jnp.where(near | jnp.logical_not(first_col), 1.0, 0.0)
                for row in range(rows + KERNEL - 1):
                    here = extended[row, tile * WIN : tile * WIN + WIN, lanes]
                    after = extended[row, (tile + 1) * WIN : (tile + 2) * WIN, lanes]
                    line = jnp.where(col > col_off, here, after)
                    line = pltpu.roll(line, WIN - 1 - col_off, 0)
                    if tile == 0:
                        line = line * keep
                    cut = line * inner_row if SHIFT <= row < reach + KERNEL // 2 else line
                    for out in range(max(0, row - KERNEL + 1), min(rows, row + 1)):
                        row_off = row - out
                        same = (out < SHIFT) == (row < reach)
                        term = (line if same else cut) * column[row_off]
                        if row_off == KERNEL // 2 and col_off == KERNEL // 2:
                            term = term + line
                        sums[out] = term if sums[out] is None else sums[out] + term
            for window_row in range(rows // WIN):
                stacked = jnp.concatenate(sums[window_row * WIN : (window_row + 1) * WIN], axis=0)
                first = (window_row * window_cols + tile) * SPOTS
                encoded[first : first + SPOTS, lanes] = stacked.astype(jnp.bfloat16)
        return 0

    lax.fori_loop(0, channels // LANES, block, 0)

    def norm(index, _):
        part = pl.ds(pl.multiple_of(index * SPOTS, SPOTS), SPOTS)
        normed[part, :] = normalized(encoded[part, :].astype(jnp.float32))
        return 0

    lax.fori_loop(0, rows * cols // SPOTS, norm, 0)


def encode(place, tokens, above, beside, taps, rel_bias):
    rows, cols, channels = tokens.shape
    flat = jax.ShapeDtypeStruct((rows * cols, channels), jnp.bfloat16)
    reach = KERNEL // 2 + SHIFT
    bias_shape = (rel_bias.shape[0] // GROUP, SPOTS, GROUP * SPOTS)
    return pl.pallas_call(
        encode_kernel,
        out_shape=(flat, flat, jax.ShapeDtypeStruct(bias_shape, jnp.float32)),
        in_specs=[SMEM, HBM, VMEM, VMEM, HBM, VMEM],
        out_specs=(VMEM, VMEM, VMEM),
        scratch_shapes=[
            pltpu.VMEM((rows + reach, cols + HALO, channels), jnp.float32),
            pltpu.VMEM(taps.shape, jnp.float32),
            pltpu.VMEM(tokens.shape, jnp.bfloat16),
            pltpu.VMEM(taps.shape, jnp.bfloat16),
            pltpu.SemaphoreType.DMA((2,)),
        ],
        compiler_params=pltpu.CompilerParams(vmem_limit_bytes=12 * 1024 * 1024),
        cost_estimate=lasting(0.1),
        name="encode",
    )(place, tokens, above, beside, taps, rel_bias)


def fetch(place, grid_cols, pieces, ids, target, sems):
    copies = []
    for piece, (parts, half) in zip(pieces, ids, strict=True):
        size = piece.shape[0] // len(parts)
        wide = min(piece.shape[1], target.shape[1])
        left = 0 if half is None else pl.multiple_of((place[2] ^ half) * wide, LANES)
        for at, (mask_row, mask_col) in enumerate(parts):
            if mask_row is None:
                first = 0
            else:
                owner = (place[0] ^ mask_row) * grid_cols + (place[1] ^ mask_col)
                first = pl.multiple_of(owner * size, 16)
            copy = pltpu.make_async_copy(
                piece.at[pl.ds(at * size, size), pl.ds(0, wide)],
                target.at[pl.ds(first, size), pl.ds(left, wide)],
                sems.at[len(copies)],
            )
            copy.start()
            copies.append(copy)
    return copies


def attend_kernel(shape, ids, grid_cols, *refs):
    rows, cols = shape
    place, normed, bias = refs[:3]
    context, weight, mixed, sems = refs[3 + len(ids) :]
    channels = normed.shape[1]
    copies = fetch(place, grid_cols, refs[3 : 3 + len(ids)], ids, weight, sems)
    groups = channels // LANES
    for copy in copies:
        copy.wait()
    wide = channels

    def project(index, _):
        lanes = pl.ds(pl.multiple_of(index * wide, wide), wide)
        mixed[:, lanes] = jnp.dot(
            normed[...], weight[:, lanes], preferred_element_type=jnp.float32
        ).astype(jnp.bfloat16)
        return 0

    lax.fori_loop(0, 3 * channels // wide, project, 0)

    window_cols = cols // WIN
    keys = GROUP * SPOTS
    query_at = lax.broadcasted_iota(jnp.int32, (SPOTS, keys), 0)
    key_at = lax.broadcasted_iota(jnp.int32, (SPOTS, keys), 1) % SPOTS
    row_differs = (query_at < SPOTS // 2) != (key_at < SPOTS // 2)
    col_differs = (query_at % WIN < SHIFT) != (key_at % WIN < SHIFT)
    lane = lax.broadcasted_iota(jnp.int32, (SPOTS, LANES), 1) // HD
    head_masks = [jnp.where(lane == h, 1.0, 0.0).astype(jnp.bfloat16) for h in range(GROUP)]
    block_row = lax.broadcasted_iota(jnp.int32, (keys, keys), 0) // SPOTS
    block_col = lax.broadcasted_iota(jnp.int32, (keys, keys), 1) // SPOTS
    same_head = jnp.where(block_row == block_col, 1.0, 0.0).astype(jnp.bfloat16)

    def window(index, _):
        part = pl.ds(pl.multiple_of(index * SPOTS, SPOTS), SPOTS)
        cut_rows = jnp.logical_and(place[0] == 0, index < window_cols)
        cut_cols = jnp.logical_and(place[1] == 0, index % window_cols == 0)
        hidden = (row_differs & cut_rows) | (col_differs & cut_cols)
        barrier = jnp.where(hidden, -1e30, 0.0)
        all_weights = []
        for group in range(groups):
            first = group * LANES
            query = mixed[part, first : first + LANES]
            key = mixed[part, channels + first : channels + first + LANES]
            key_all = jnp.concatenate([key * m for m in head_masks], axis=0)
            scores = lax.dot_general(
                query, key_all, (((1,), (1,)), ((), ())), preferred_element_type=jnp.float32
            )
            all_weights.append(jnp.exp(scores * HD ** (-0.5) + (bias[group] + barrier)))
        weights = jnp.concatenate(all_weights, axis=0)
        total = jnp.dot(
            jnp.minimum(weights, LARGEST).astype(jnp.bfloat16),
            same_head,
            preferred_element_type=jnp.float32,
        )
        probs = (weights * pl.reciprocal(total)).astype(jnp.bfloat16)
        for group in range(groups):
            first = group * LANES
            value = mixed[part, 2 * channels + first : 2 * channels + first + LANES]
            value_all = jnp.concatenate([value * m for m in head_masks], axis=0)
            context[part, first : first + LANES] = jnp.dot(
                probs[group * SPOTS : (group + 1) * SPOTS],
                value_all,
                preferred_element_type=jnp.float32,
            ).astype(jnp.bfloat16)
        return 0

    lax.fori_loop(0, rows * cols // SPOTS, window, 0)


def attend(place, shape, normed, bias, pieces, grid_cols):
    rows, cols = shape
    channels = normed.shape[1]
    ids = [p[1:] for p in pieces]
    return pl.pallas_call(
        functools.partial(attend_kernel, shape, ids, grid_cols),
        out_shape=jax.ShapeDtypeStruct((rows * cols, channels), jnp.bfloat16),
        in_specs=[SMEM, VMEM, VMEM] + [ANY] * len(pieces),
        out_specs=VMEM,
        scratch_shapes=[
            pltpu.VMEM((channels, 3 * channels), jnp.bfloat16),
            pltpu.VMEM((rows * cols, 3 * channels), jnp.bfloat16),
            pltpu.SemaphoreType.DMA((sum(len(p[0]) for p in ids),)),
        ],
        compiler_params=pltpu.CompilerParams(vmem_limit_bytes=16 * 1024 * 1024),
        cost_estimate=lasting(10),
        name="attend",
    )(place, normed, bias, *[p[0] for p in pieces])


def project_kernel(shape, ids, grid_cols, *refs):
    rows, cols = shape
    place, context, encoded = refs[:3]
    rolled, top, side, corner, weight, sems = refs[3 + len(ids) :]
    channels = context.shape[1]
    for copy in fetch(place, grid_cols, refs[3 : 3 + len(ids)], ids, weight, sems):
        copy.wait()
    window_cols = cols // WIN
    wide = 2 * LANES
    sublane = lax.broadcasted_iota(jnp.int32, (WIN, wide), 0)

    def finish(index, _):
        lanes = pl.ds(pl.multiple_of(index * wide, wide), wide)
        update = jnp.dot(context[...], weight[:, lanes], preferred_element_type=jnp.float32)
        summed = encoded[:, lanes].astype(jnp.float32) + update
        edge = []
        for row in range(rows):
            tiles = []
            for tile in range(window_cols):
                first = (row // WIN * window_cols + tile) * SPOTS + row % WIN * WIN
                tiles.append(summed[first : first + WIN])
            for pair in range(window_cols // 2):
                both = jnp.concatenate(tiles[2 * pair : 2 * pair + 2], axis=0)
                both = both.astype(jnp.bfloat16)
                at = pair * 2 * WIN
                rolled[row, at : at + 2 * WIN, lanes] = both
                if row < SHIFT:
                    top[row, at : at + 2 * WIN, lanes] = both
            edge.append(tiles[0])
        for quad in range(rows // 4):
            halves = [
                jnp.where(
                    sublane < SHIFT,
                    edge[4 * quad + two],
                    pltpu.roll(edge[4 * quad + two + 1], SHIFT, 0),
                )
                for two in (0, 2)
            ]
            packed = jnp.concatenate(halves, axis=0).astype(jnp.bfloat16)
            if quad == 0:
                corner[:, lanes] = packed
            else:
                side[(quad - 1) * 16 : quad * 16, lanes] = packed
        return 0

    lax.fori_loop(0, channels // wide, finish, 0)


def project(place, shape, context, encoded, pieces, grid_cols):
    rows, cols = shape
    channels = context.shape[1]
    bf16 = functools.partial(jax.ShapeDtypeStruct, dtype=jnp.bfloat16)
    ids = [p[1:] for p in pieces]
    return pl.pallas_call(
        functools.partial(project_kernel, shape, ids, grid_cols),
        out_shape=(
            bf16((rows, cols, channels)),
            bf16((SHIFT, cols, channels)),
            bf16(((rows - SHIFT) * SHIFT, channels)),
            bf16((SHIFT * SHIFT, channels)),
        ),
        in_specs=[SMEM, VMEM, VMEM] + [ANY] * len(pieces),
        out_specs=(VMEM,) * 4,
        scratch_shapes=[
            pltpu.VMEM((channels, channels), jnp.bfloat16),
            pltpu.SemaphoreType.DMA((sum(len(p[0]) for p in ids),)),
        ],
        compiler_params=pltpu.CompilerParams(vmem_limit_bytes=10 * 1024 * 1024),
        cost_estimate=lasting(3),
        name="project",
    )(place, context, encoded, *[p[0] for p in pieces])


def dispatch_kernel(place, rolled, below, right, corner, position, *refs):
    rows, cols, channels = rolled.shape
    attended, outgoing, normed = refs[0], refs[1:-1], refs[-1]
    sublane = lax.broadcasted_iota(jnp.int32, (WIN, channels), 0)
    for row in range(rows):
        if row < rows - SHIFT:
            line, beside, at = rolled[row + SHIFT], right, row
        else:
            line, beside, at = below[row + SHIFT - rows], corner, row + SHIFT - rows
        line = line.astype(jnp.float32)
        tiles = [
            pltpu.roll(line[tile * WIN : (tile + 1) * WIN], SHIFT, 0) for tile in range(cols // WIN)
        ]
        block = at * SHIFT // 16 * 16
        last = beside[block : block + 16].astype(jnp.float32)
        within = at * SHIFT - block
        last = last[within // WIN * WIN : within // WIN * WIN + WIN]
        tiles.append(last if within % WIN else pltpu.roll(last, SHIFT, 0))
        line = jnp.concatenate(
            [
                jnp.where(sublane < SHIFT, tiles[tile], tiles[tile + 1])
                for tile in range(cols // WIN)
            ],
            axis=0,
        )
        attended[row * cols : (row + 1) * cols] = line.astype(jnp.bfloat16)
        normed[row * cols : (row + 1) * cols] = normalized(line)
    for mask in range(len(outgoing) // 2):
        halves = outgoing[2 * mask : 2 * mask + 2]
        count = 2 * halves[0].shape[0]
        spot = lax.broadcasted_iota(jnp.int32, (count, rows * cols), 0)
        spot = spot + (place[0] ^ mask) * count
        chosen = jnp.where(position[...] == spot, 1.0, 0.0).astype(jnp.bfloat16)
        slots = jnp.dot(chosen, normed[...], preferred_element_type=jnp.float32)
        slots = slots.astype(jnp.bfloat16)
        for at, target in enumerate(halves):
            target[...] = slots[at * count // 2 : (at + 1) * count // 2]


def dispatch(place, rolled, below, right, corner, position, grid_rows):
    rows, cols, channels = rolled.shape
    bf16 = functools.partial(jax.ShapeDtypeStruct, dtype=jnp.bfloat16)
    slot_rows = EXPERTS * CAP // grid_rows // 2
    return pl.pallas_call(
        dispatch_kernel,
        out_shape=(bf16((rows * cols, channels)),) + (bf16((slot_rows, channels)),) * (2 * grid_rows),
        in_specs=[SMEM] + [VMEM] * 5,
        out_specs=(VMEM,) * (2 * grid_rows + 1),
        scratch_shapes=[pltpu.VMEM((rows * cols, channels), jnp.bfloat16)],
        compiler_params=pltpu.CompilerParams(vmem_limit_bytes=10 * 1024 * 1024),
        name="dispatch",
    )(place, rolled, below, right, corner, position)


def expert_kernel(count, first, *refs):
    incoming, sources = refs[:count], refs[count : count + 2]
    results, (held_in, held_out, sems) = refs[-3 - count : -3], refs[-3:]
    copies = [
        [
            pltpu.make_async_copy(source.at[first + slot], target.at[slot], sems.at[slot, which])
            for which, (source, target) in enumerate(zip(sources, (held_in, held_out), strict=True))
        ]
        for slot in range(held_in.shape[0])
    ]
    for pair in copies:
        for copy in pair:
            copy.start()
    for slot, (copy_in, copy_out) in enumerate(copies):
        own = pl.ds(slot * CAP, CAP)
        rows = jnp.concatenate([ref[own, :] for ref in incoming], axis=0)
        copy_in.wait()
        hidden = lax.dot_general(
            rows, held_in[slot], (((1,), (1,)), ((), ())), preferred_element_type=jnp.float32
        )
        hidden = (0.5 * hidden * (1.0 + lax.erf(hidden * 0.5**0.5))).astype(jnp.bfloat16)
        copy_out.wait()
        result = jnp.dot(hidden, held_out[slot], preferred_element_type=jnp.float32)
        result = result.astype(jnp.bfloat16)
        for at, ref in enumerate(results):
            ref[own, :] = result[at * CAP : (at + 1) * CAP]


def serve(incoming, weights, first, number):
    count = len(incoming)
    shape = (number, *weights[0].shape[1:])
    return pl.pallas_call(
        functools.partial(expert_kernel, count, first),
        out_shape=tuple(jax.ShapeDtypeStruct(x.shape, x.dtype) for x in incoming),
        in_specs=[VMEM] * count + [HBM, HBM],
        out_specs=(VMEM,) * count,
        scratch_shapes=[
            pltpu.VMEM(shape, jnp.bfloat16),
            pltpu.VMEM(shape, jnp.bfloat16),
            pltpu.SemaphoreType.DMA((number, 2)),
        ],
        compiler_params=pltpu.CompilerParams(vmem_limit_bytes=52 * 1024 * 1024),
        cost_estimate=lasting(7),
        name="experts",
    )(*incoming, *weights)


def combine_kernel(place, attended, position, constant_at, table, *refs):
    results, output = refs[:-1], refs[-1]
    tokens = attended.shape[0]
    rows = jnp.concatenate([result[...] for result in results], axis=0)
    total, count = rows.shape[0], 2 * results[0].shape[0]
    spot = lax.broadcasted_iota(jnp.int32, (tokens, total), 1)
    spot = (spot // count ^ place[0]) * count + spot % count
    chosen = jnp.where(position[...] == spot, 1.0, 0.0).astype(jnp.bfloat16)
    entries = table.shape[0]
    spot = lax.broadcasted_iota(jnp.int32, (tokens, 3 * entries), 1) % entries
    constant = jnp.where(constant_at[...] == spot, 1.0, 0.0).astype(jnp.bfloat16)
    parts, rest = [], table[...]
    for _ in range(3):
        parts.append(rest.astype(jnp.bfloat16))
        rest = rest - parts[-1].astype(jnp.float32)
    parts = jnp.concatenate(parts, axis=0)
    mixture = jnp.dot(chosen, rows, preferred_element_type=jnp.float32)
    mixture = mixture + jnp.dot(constant, parts, preferred_element_type=jnp.float32)
    output[...] = (attended[...].astype(jnp.float32) + mixture).astype(jnp.bfloat16)


def combine(place, attended, position, constant_at, table, results):
    return pl.pallas_call(
        combine_kernel,
        out_shape=jax.ShapeDtypeStruct(attended.shape, jnp.bfloat16),
        in_specs=[SMEM] + [VMEM] * (4 + len(results)),
        out_specs=VMEM,
        compiler_params=pltpu.CompilerParams(vmem_limit_bytes=12 * 1024 * 1024),
        name="combine",
    )(place, attended, position, constant_at, table, *results)


def stacked(parts):
    ids = sum([part[1] for part in parts], [])
    return jnp.concatenate([part[0] for part in parts], axis=0), ids, None


def along(part, axis, mask):
    array, ids, half = part
    moved = exchanged(array, axis, mask)
    if axis == "groups":
        return moved, ids, half ^ mask
    change = (mask, 0) if axis == "gy" else (0, mask)
    return moved, [(a ^ change[0], b ^ change[1]) for a, b in ids], half


def diagonal(part, mask):
    array, ids, half = part
    groups, rows = lax.axis_size("groups"), lax.axis_size("gy")
    pairs = [
        (i * rows + j, (i ^ 1) * rows + (j ^ mask)) for i in range(groups) for j in range(rows)
    ]
    moved = lax.ppermute(array, ("groups", "gy"), pairs)
    return moved, [(a ^ mask, b) for a, b in ids], half ^ 1


def held(*values):
    return lax.optimization_barrier(values)


def shards(
    tokens,
    conv_kernel,
    project_in,
    project_out,
    rel_bias,
    expert_in,
    expert_out,
    const_table,
    expert_ids,
    slots,
    const_index,
):
    rows, cols, channels = tokens.shape
    grid_rows, grid_cols = lax.axis_size("gy"), lax.axis_size("gx")
    place = jnp.stack([lax.axis_index(axis) for axis in ("gy", "gx", "groups")]).astype(jnp.int32)
    reach = KERNEL // 2 + SHIFT
    quick = grid_rows == 4 and grid_cols == 4 and lax.axis_size("groups") == 2
    above = shifted(tokens[rows - reach :], "gy", 1)
    if quick:
        beyond = exchanged(project_in, "gx", 1)
        facing_out = exchanged(project_out, "gy", 2)
        beyond, facing_out, above = held(beyond, facing_out, above)
        two = (jnp.concatenate([project_in, beyond], axis=0), [(0, 0), (0, 1)], None)
        wide = two[0].shape[1] // 2
        mine = lax.dynamic_slice_in_dim(two[0], lax.axis_index("groups") * wide, wide, axis=1)
        far = along((mine, two[1], 0), "gx", 2)
        facing = along(two, "gy", 2)
    edge = jnp.concatenate([above[:, cols - HALO :], tokens[:, cols - HALO :]], axis=0)
    beside = shifted(edge, "gx", 1)
    encoded, normed, bias = encode(place, tokens, above, beside, conv_kernel, rel_bias)
    if quick:
        first, second, normed = held(far[0], facing[0], normed)
        far, facing = (first, *far[1:]), (second, *facing[1:])
        across = along(far, "gy", 2)
        pair = stacked([(project_out, [(0, 0)]), (facing_out, [(2, 0)])])
        plane = [pair] + [along(pair, "gx", mask) for mask in (3, 2, 1)]
        far_rest, across_rest = along(far, "groups", 1), diagonal(far, 2)
        pieces_in = [two, facing, far, far_rest, across]
        pieces_in = pieces_in + [along(part, "gy", 1) for part in pieces_in]
        pieces_in = pieces_in + [across_rest, along(across_rest, "gy", 1)]
    else:
        whole = [(None, None)]
        pieces_in = [(lax.all_gather(project_in, ("gy", "gx"), axis=0, tiled=True), whole, None)]
        pieces_out = [(lax.all_gather(project_out, ("gy", "gx"), axis=0, tiled=True), whole, None)]
    context = attend(place, (rows, cols), normed, bias, pieces_in, grid_cols)
    if quick:
        *arrays, context = held(*[part[0] for part in plane], context)
        plane = stacked([(array, *part[1:]) for array, part in zip(arrays, plane, strict=True)])
        pieces_out = [plane, along(plane, "gy", 1)]
    rolled, top, side, corner = project(
        place, (rows, cols), context, encoded, pieces_out, grid_cols
    )
    below = shifted(top, "gy", -1)
    right = shifted(side, "gx", -1)
    last = shifted_both(corner, -1)
    expert_of, slot_of = expert_ids.reshape(-1), slots.reshape(-1)
    position = jnp.where(expert_of < EXPERTS, expert_of * CAP + slot_of, -1)
    constant_at = jnp.where(expert_of == EXPERTS, const_index.reshape(-1), -1)
    attended, *outgoing = dispatch(
        place, rolled, below, right, last, position[None, :], grid_rows
    )
    half, results = expert_in.shape[0] // 2, [None] * len(outgoing)
    incoming = [
        [
            exchanged(outgoing[2 * mask + h], "gy", mask) if mask else outgoing[h]
            for mask in range(grid_rows)
        ]
        for h in range(2)
    ]
    for h, arrived in enumerate(incoming):
        served = serve(arrived, (expert_in, expert_out), h * half, half)
        for mask, array in enumerate(served):
            results[2 * mask + h] = exchanged(array, "gy", mask) if mask else array
    output = combine(
        place, attended, position[:, None], constant_at[:, None], const_table, results
    )
    return output.reshape(rows, cols, channels)


def solution(mesh):
    placed = (
        P(("groups", "gy"), "gx", None),
        P(),
        P(("gy", "gx"), None),
        P(("gy", "gx"), None),
        P(),
        P("gy", None, None),
        P("gy", None, None),
        P(),
        P(("groups", "gy"), "gx"),
        P(("groups", "gy"), "gx"),
        P(("groups", "gy"), "gx"),
    )
    return jax.shard_map(
        shards,
        mesh=mesh,
        in_specs=placed,
        out_specs=P(("groups", "gy"), "gx", None),
        check_vma=False,
    )
```

```python
import functools

import jax
import jax.numpy as jnp
from jax import lax
from jax.experimental import pallas as pl
from jax.experimental.pallas import tpu as pltpu
from jax.sharding import PartitionSpec as P

HD = 32
EXPERTS = 32
WIN = 8
SHIFT = 4
KERNEL = 7
CAP = 16
LANES = 128
GROUP = LANES // HD
SPOTS = WIN * WIN
HALO = 8
VMEM = pl.BlockSpec(memory_space=pltpu.VMEM)
SMEM = pl.BlockSpec(memory_space=pltpu.SMEM)
ANY = pl.BlockSpec(memory_space=pl.ANY)
HBM = pl.BlockSpec(memory_space=pltpu.HBM)
LARGEST = 3.38e38


def lasting(microseconds):
    return pl.CostEstimate(
        flops=int(microseconds * 1.15e9), bytes_accessed=0, transcendentals=0
    )


def shifted(x, axis, by):
    size = lax.axis_size(axis)
    return lax.ppermute(x, axis, [(i, (i + by) % size) for i in range(size)])


def shifted_both(x, by):
    rows, cols = lax.axis_size("gy"), lax.axis_size("gx")
    pairs = [
        (i * cols + j, ((i + by) % rows) * cols + (j + by) % cols)
        for i in range(rows)
        for j in range(cols)
    ]
    return lax.ppermute(x, ("gy", "gx"), pairs)


def exchanged(x, axis, mask):
    size = lax.axis_size(axis)
    return lax.ppermute(x, axis, [(i, i ^ mask) for i in range(size)])


def normalized(values):
    centred = values - jnp.mean(values, axis=-1, keepdims=True)
    spread = jnp.mean(centred * centred, axis=-1, keepdims=True)
    return (centred * lax.rsqrt(spread + 1e-05)).astype(jnp.bfloat16)


def prepare_kernel(tokens, taps, rel_bias, kept, weights, bias):
    kept[...] = tokens[...].astype(jnp.float32)
    weights[...] = taps[...].astype(jnp.float32)
    for head in range(rel_bias.shape[0]):
        at = head % GROUP * SPOTS
        bias[head // GROUP, :, at : at + SPOTS] = rel_bias[head]


def prepare(tokens, taps, rel_bias):
    bias_shape = (rel_bias.shape[0] // GROUP, SPOTS, GROUP * SPOTS)
    return pl.pallas_call(
        prepare_kernel,
        out_shape=(
            jax.ShapeDtypeStruct(tokens.shape, jnp.float32),
            jax.ShapeDtypeStruct(taps.shape, jnp.float32),
            jax.ShapeDtypeStruct(bias_shape, jnp.float32),
        ),
        in_specs=[VMEM] * 3,
        out_specs=(VMEM,) * 3,
        compiler_params=pltpu.CompilerParams(vmem_limit_bytes=8 * 1024 * 1024),
        cost_estimate=lasting(3),
        name="prepare",
    )(tokens, taps, rel_bias)


def encode_kernel(place, tokens, above, beside, weights, encoded, normed, upper, left):
    rows, cols, channels = tokens.shape
    reach = KERNEL // 2 + SHIFT
    upper[:, :HALO] = beside[:reach].astype(jnp.float32)
    upper[:, HALO:] = above[...].astype(jnp.float32)
    left[...] = beside[reach:].astype(jnp.float32)
    inner_row = jnp.where(place[0] == 0, 0.0, 1.0)
    first_col = place[1] == 0
    window_cols = cols // WIN
    col = lax.broadcasted_iota(jnp.int32, (WIN, LANES), 0)

    def extended(row, tile, lanes):
        if row < reach:
            return upper[row, tile * WIN : (tile + 1) * WIN, lanes]
        if tile == 0:
            return left[row - reach, :, lanes]
        return tokens[row - reach, (tile - 1) * WIN : tile * WIN, lanes]

    def block(index, _):
        lanes = pl.ds(pl.multiple_of(index * LANES, LANES), LANES)
        for tile in range(window_cols):
            sums = [None] * rows
            for col_off in range(KERNEL):
                column = [
                    jnp.broadcast_to(weights[row_off, pl.ds(col_off, 1), lanes], (WIN, LANES))
                    for row_off in range(KERNEL)
                ]
                if tile == 0:
                    near = (col < SHIFT) == (col + col_off < reach)
                    keep = jnp.where(near | jnp.logical_not(first_col), 1.0, 0.0)
                for row in range(rows + KERNEL - 1):
                    line = jnp.where(
                        col > col_off, extended(row, tile, lanes), extended(row, tile + 1, lanes)
                    )
                    line = pltpu.roll(line, WIN - 1 - col_off, 0)
                    if tile == 0:
                        line = line * keep
                    cut = line * inner_row if SHIFT <= row < reach + KERNEL // 2 else line
                    for out in range(max(0, row - KERNEL + 1), min(rows, row + 1)):
                        row_off = row - out
                        same = (out < SHIFT) == (row < reach)
                        term = (line if same else cut) * column[row_off]
                        if row_off == KERNEL // 2 and col_off == KERNEL // 2:
                            term = term + line
                        sums[out] = term if sums[out] is None else sums[out] + term
            for window_row in range(rows // WIN):
                stacked = jnp.concatenate(sums[window_row * WIN : (window_row + 1) * WIN], axis=0)
                first = (window_row * window_cols + tile) * SPOTS
                encoded[first : first + SPOTS, lanes] = stacked.astype(jnp.bfloat16)
        return 0

    lax.fori_loop(0, channels // LANES, block, 0)

    def norm(index, _):
        part = pl.ds(pl.multiple_of(index * SPOTS, SPOTS), SPOTS)
        normed[part, :] = normalized(encoded[part, :].astype(jnp.float32))
        return 0

    lax.fori_loop(0, rows * cols // SPOTS, norm, 0)


def encode(place, tokens, above, beside, weights):
    rows, cols, channels = tokens.shape
    flat = jax.ShapeDtypeStruct((rows * cols, channels), jnp.bfloat16)
    reach = KERNEL // 2 + SHIFT
    return pl.pallas_call(
        encode_kernel,
        out_shape=(flat, flat),
        in_specs=[SMEM] + [VMEM] * 4,
        out_specs=(VMEM, VMEM),
        scratch_shapes=[
            pltpu.VMEM((reach, cols + HALO, channels), jnp.float32),
            pltpu.VMEM((rows, HALO, channels), jnp.float32),
        ],
        compiler_params=pltpu.CompilerParams(vmem_limit_bytes=12 * 1024 * 1024),
        cost_estimate=lasting(0.1),
        name="encode",
    )(place, tokens, above, beside, weights)


def fetch(place, grid_cols, pieces, ids, target, sems):
    copies = []
    for piece, (parts, half) in zip(pieces, ids, strict=True):
        size = piece.shape[0] // len(parts)
        wide = min(piece.shape[1], target.shape[1])
        left = 0 if half is None else pl.multiple_of((place[2] ^ half) * wide, LANES)
        for at, (mask_row, mask_col) in enumerate(parts):
            if mask_row is None:
                first = 0
            else:
                owner = (place[0] ^ mask_row) * grid_cols + (place[1] ^ mask_col)
                first = pl.multiple_of(owner * size, 16)
            copy = pltpu.make_async_copy(
                piece.at[pl.ds(at * size, size), pl.ds(0, wide)],
                target.at[pl.ds(first, size), pl.ds(left, wide)],
                sems.at[len(copies)],
            )
            copy.start()
            copies.append(copy)
    return copies


def attend_kernel(shape, ids, grid_cols, *refs):
    rows, cols = shape
    place, normed, bias = refs[:3]
    context, weight, mixed, sems = refs[3 + len(ids) :]
    channels = normed.shape[1]
    copies = fetch(place, grid_cols, refs[3 : 3 + len(ids)], ids, weight, sems)
    groups = channels // LANES
    for copy in copies:
        copy.wait()
    wide = channels

    def project(index, _):
        lanes = pl.ds(pl.multiple_of(index * wide, wide), wide)
        mixed[:, lanes] = jnp.dot(
            normed[...], weight[:, lanes], preferred_element_type=jnp.float32
        ).astype(jnp.bfloat16)
        return 0

    lax.fori_loop(0, 3 * channels // wide, project, 0)

    window_cols = cols // WIN
    keys = GROUP * SPOTS
    query_at = lax.broadcasted_iota(jnp.int32, (SPOTS, keys), 0)
    key_at = lax.broadcasted_iota(jnp.int32, (SPOTS, keys), 1) % SPOTS
    row_differs = (query_at < SPOTS // 2) != (key_at < SPOTS // 2)
    col_differs = (query_at % WIN < SHIFT) != (key_at % WIN < SHIFT)
    lane = lax.broadcasted_iota(jnp.int32, (SPOTS, LANES), 1) // HD
    head_masks = [jnp.where(lane == h, 1.0, 0.0).astype(jnp.bfloat16) for h in range(GROUP)]
    block_row = lax.broadcasted_iota(jnp.int32, (keys, keys), 0) // SPOTS
    block_col = lax.broadcasted_iota(jnp.int32, (keys, keys), 1) // SPOTS
    same_head = jnp.where(block_row == block_col, 1.0, 0.0).astype(jnp.bfloat16)

    def window(index, _):
        part = pl.ds(pl.multiple_of(index * SPOTS, SPOTS), SPOTS)
        cut_rows = jnp.logical_and(place[0] == 0, index < window_cols)
        cut_cols = jnp.logical_and(place[1] == 0, index % window_cols == 0)
        hidden = (row_differs & cut_rows) | (col_differs & cut_cols)
        barrier = jnp.where(hidden, -1e30, 0.0)
        all_weights = []
        for group in range(groups):
            first = group * LANES
            query = mixed[part, first : first + LANES]
            key = mixed[part, channels + first : channels + first + LANES]
            key_all = jnp.concatenate([key * m for m in head_masks], axis=0)
            scores = lax.dot_general(
                query, key_all, (((1,), (1,)), ((), ())), preferred_element_type=jnp.float32
            )
            all_weights.append(jnp.exp(scores * HD ** (-0.5) + (bias[group] + barrier)))
        weights = jnp.concatenate(all_weights, axis=0)
        total = jnp.dot(
            jnp.minimum(weights, LARGEST).astype(jnp.bfloat16),
            same_head,
            preferred_element_type=jnp.float32,
        )
        probs = (weights * pl.reciprocal(total)).astype(jnp.bfloat16)
        for group in range(groups):
            first = group * LANES
            value = mixed[part, 2 * channels + first : 2 * channels + first + LANES]
            value_all = jnp.concatenate([value * m for m in head_masks], axis=0)
            context[part, first : first + LANES] = jnp.dot(
                probs[group * SPOTS : (group + 1) * SPOTS],
                value_all,
                preferred_element_type=jnp.float32,
            ).astype(jnp.bfloat16)
        return 0

    lax.fori_loop(0, rows * cols // SPOTS, window, 0)


def attend(place, shape, normed, bias, pieces, grid_cols):
    rows, cols = shape
    channels = normed.shape[1]
    ids = [p[1:] for p in pieces]
    return pl.pallas_call(
        functools.partial(attend_kernel, shape, ids, grid_cols),
        out_shape=jax.ShapeDtypeStruct((rows * cols, channels), jnp.bfloat16),
        in_specs=[SMEM, VMEM, VMEM] + [ANY] * len(pieces),
        out_specs=VMEM,
        scratch_shapes=[
            pltpu.VMEM((channels, 3 * channels), jnp.bfloat16),
            pltpu.VMEM((rows * cols, 3 * channels), jnp.bfloat16),
            pltpu.SemaphoreType.DMA((sum(len(p[0]) for p in ids),)),
        ],
        compiler_params=pltpu.CompilerParams(vmem_limit_bytes=16 * 1024 * 1024),
        cost_estimate=lasting(10),
        name="attend",
    )(place, normed, bias, *[p[0] for p in pieces])


def project_kernel(shape, ids, grid_cols, *refs):
    rows, cols = shape
    place, context, encoded = refs[:3]
    rolled, top, side, corner, weight, sems = refs[3 + len(ids) :]
    channels = context.shape[1]
    for copy in fetch(place, grid_cols, refs[3 : 3 + len(ids)], ids, weight, sems):
        copy.wait()
    window_cols = cols // WIN
    wide = 2 * LANES
    sublane = lax.broadcasted_iota(jnp.int32, (WIN, wide), 0)

    def finish(index, _):
        lanes = pl.ds(pl.multiple_of(index * wide, wide), wide)
        update = jnp.dot(context[...], weight[:, lanes], preferred_element_type=jnp.float32)
        summed = encoded[:, lanes].astype(jnp.float32) + update
        edge = []
        for row in range(rows):
            tiles = []
            for tile in range(window_cols):
                first = (row // WIN * window_cols + tile) * SPOTS + row % WIN * WIN
                tiles.append(summed[first : first + WIN])
            for pair in range(window_cols // 2):
                both = jnp.concatenate(tiles[2 * pair : 2 * pair + 2], axis=0)
                both = both.astype(jnp.bfloat16)
                at = pair * 2 * WIN
                rolled[row, at : at + 2 * WIN, lanes] = both
                if row < SHIFT:
                    top[row, at : at + 2 * WIN, lanes] = both
            edge.append(tiles[0])
        for quad in range(rows // 4):
            halves = [
                jnp.where(
                    sublane < SHIFT,
                    edge[4 * quad + two],
                    pltpu.roll(edge[4 * quad + two + 1], SHIFT, 0),
                )
                for two in (0, 2)
            ]
            packed = jnp.concatenate(halves, axis=0).astype(jnp.bfloat16)
            if quad == 0:
                corner[:, lanes] = packed
            else:
                side[(quad - 1) * 16 : quad * 16, lanes] = packed
        return 0

    lax.fori_loop(0, channels // wide, finish, 0)


def project(place, shape, context, encoded, pieces, grid_cols):
    rows, cols = shape
    channels = context.shape[1]
    bf16 = functools.partial(jax.ShapeDtypeStruct, dtype=jnp.bfloat16)
    ids = [p[1:] for p in pieces]
    return pl.pallas_call(
        functools.partial(project_kernel, shape, ids, grid_cols),
        out_shape=(
            bf16((rows, cols, channels)),
            bf16((SHIFT, cols, channels)),
            bf16(((rows - SHIFT) * SHIFT, channels)),
            bf16((SHIFT * SHIFT, channels)),
        ),
        in_specs=[SMEM, VMEM, VMEM] + [ANY] * len(pieces),
        out_specs=(VMEM,) * 4,
        scratch_shapes=[
            pltpu.VMEM((channels, channels), jnp.bfloat16),
            pltpu.SemaphoreType.DMA((sum(len(p[0]) for p in ids),)),
        ],
        compiler_params=pltpu.CompilerParams(vmem_limit_bytes=10 * 1024 * 1024),
        cost_estimate=lasting(3),
        name="project",
    )(place, context, encoded, *[p[0] for p in pieces])


def dispatch_kernel(place, rolled, below, right, corner, position, *refs):
    rows, cols, channels = rolled.shape
    attended, outgoing, normed = refs[0], refs[1:-1], refs[-1]
    sublane = lax.broadcasted_iota(jnp.int32, (WIN, channels), 0)
    for row in range(rows):
        if row < rows - SHIFT:
            line, beside, at = rolled[row + SHIFT], right, row
        else:
            line, beside, at = below[row + SHIFT - rows], corner, row + SHIFT - rows
        line = line.astype(jnp.float32)
        tiles = [
            pltpu.roll(line[tile * WIN : (tile + 1) * WIN], SHIFT, 0) for tile in range(cols // WIN)
        ]
        block = at * SHIFT // 16 * 16
        last = beside[block : block + 16].astype(jnp.float32)
        within = at * SHIFT - block
        last = last[within // WIN * WIN : within // WIN * WIN + WIN]
        tiles.append(last if within % WIN else pltpu.roll(last, SHIFT, 0))
        line = jnp.concatenate(
            [
                jnp.where(sublane < SHIFT, tiles[tile], tiles[tile + 1])
                for tile in range(cols // WIN)
            ],
            axis=0,
        )
        attended[row * cols : (row + 1) * cols] = line.astype(jnp.bfloat16)
        normed[row * cols : (row + 1) * cols] = normalized(line)
    for mask in range(len(outgoing) // 2):
        halves = outgoing[2 * mask : 2 * mask + 2]
        count = 2 * halves[0].shape[0]
        spot = lax.broadcasted_iota(jnp.int32, (count, rows * cols), 0)
        spot = spot + (place[0] ^ mask) * count
        chosen = jnp.where(position[...] == spot, 1.0, 0.0).astype(jnp.bfloat16)
        slots = jnp.dot(chosen, normed[...], preferred_element_type=jnp.float32)
        slots = slots.astype(jnp.bfloat16)
        for at, target in enumerate(halves):
            target[...] = slots[at * count // 2 : (at + 1) * count // 2]


def dispatch(place, rolled, below, right, corner, position, grid_rows):
    rows, cols, channels = rolled.shape
    bf16 = functools.partial(jax.ShapeDtypeStruct, dtype=jnp.bfloat16)
    slot_rows = EXPERTS * CAP // grid_rows // 2
    return pl.pallas_call(
        dispatch_kernel,
        out_shape=(bf16((rows * cols, channels)),) + (bf16((slot_rows, channels)),) * (2 * grid_rows),
        in_specs=[SMEM] + [VMEM] * 5,
        out_specs=(VMEM,) * (2 * grid_rows + 1),
        scratch_shapes=[pltpu.VMEM((rows * cols, channels), jnp.bfloat16)],
        compiler_params=pltpu.CompilerParams(vmem_limit_bytes=10 * 1024 * 1024),
        name="dispatch",
    )(place, rolled, below, right, corner, position)


def expert_kernel(count, first, *refs):
    incoming, sources = refs[:count], refs[count : count + 2]
    results, (held_in, held_out, sems) = refs[-3 - count : -3], refs[-3:]
    copies = [
        [
            pltpu.make_async_copy(source.at[first + slot], target.at[slot], sems.at[slot, which])
            for which, (source, target) in enumerate(zip(sources, (held_in, held_out), strict=True))
        ]
        for slot in range(held_in.shape[0])
    ]
    for pair in copies:
        for copy in pair:
            copy.start()
    for slot, (copy_in, copy_out) in enumerate(copies):
        own = pl.ds(slot * CAP, CAP)
        rows = jnp.concatenate([ref[own, :] for ref in incoming], axis=0)
        copy_in.wait()
        hidden = lax.dot_general(
            rows, held_in[slot], (((1,), (1,)), ((), ())), preferred_element_type=jnp.float32
        )
        hidden = (0.5 * hidden * (1.0 + lax.erf(hidden * 0.5**0.5))).astype(jnp.bfloat16)
        copy_out.wait()
        result = jnp.dot(hidden, held_out[slot], preferred_element_type=jnp.float32)
        result = result.astype(jnp.bfloat16)
        for at, ref in enumerate(results):
            ref[own, :] = result[at * CAP : (at + 1) * CAP]


def serve(incoming, weights, first, number):
    count = len(incoming)
    shape = (number, *weights[0].shape[1:])
    return pl.pallas_call(
        functools.partial(expert_kernel, count, first),
        out_shape=tuple(jax.ShapeDtypeStruct(x.shape, x.dtype) for x in incoming),
        in_specs=[VMEM] * count + [HBM, HBM],
        out_specs=(VMEM,) * count,
        scratch_shapes=[
            pltpu.VMEM(shape, jnp.bfloat16),
            pltpu.VMEM(shape, jnp.bfloat16),
            pltpu.SemaphoreType.DMA((number, 2)),
        ],
        compiler_params=pltpu.CompilerParams(vmem_limit_bytes=52 * 1024 * 1024),
        cost_estimate=lasting(7),
        name="experts",
    )(*incoming, *weights)


def combine_kernel(place, attended, position, constant_at, table, *refs):
    results, output = refs[:-1], refs[-1]
    tokens = attended.shape[0]
    rows = jnp.concatenate([result[...] for result in results], axis=0)
    total, count = rows.shape[0], 2 * results[0].shape[0]
    spot = lax.broadcasted_iota(jnp.int32, (tokens, total), 1)
    spot = (spot // count ^ place[0]) * count + spot % count
    chosen = jnp.where(position[...] == spot, 1.0, 0.0).astype(jnp.bfloat16)
    entries = table.shape[0]
    spot = lax.broadcasted_iota(jnp.int32, (tokens, 3 * entries), 1) % entries
    constant = jnp.where(constant_at[...] == spot, 1.0, 0.0).astype(jnp.bfloat16)
    parts, rest = [], table[...]
    for _ in range(3):
        parts.append(rest.astype(jnp.bfloat16))
        rest = rest - parts[-1].astype(jnp.float32)
    parts = jnp.concatenate(parts, axis=0)
    mixture = jnp.dot(chosen, rows, preferred_element_type=jnp.float32)
    mixture = mixture + jnp.dot(constant, parts, preferred_element_type=jnp.float32)
    output[...] = (attended[...].astype(jnp.float32) + mixture).astype(jnp.bfloat16)


def combine(place, attended, position, constant_at, table, results):
    return pl.pallas_call(
        combine_kernel,
        out_shape=jax.ShapeDtypeStruct(attended.shape, jnp.bfloat16),
        in_specs=[SMEM] + [VMEM] * (4 + len(results)),
        out_specs=VMEM,
        compiler_params=pltpu.CompilerParams(vmem_limit_bytes=12 * 1024 * 1024),
        name="combine",
    )(place, attended, position, constant_at, table, *results)


def stacked(parts):
    ids = sum([part[1] for part in parts], [])
    return jnp.concatenate([part[0] for part in parts], axis=0), ids, None


def along(part, axis, mask):
    array, ids, half = part
    moved = exchanged(array, axis, mask)
    if axis == "groups":
        return moved, ids, half ^ mask
    change = (mask, 0) if axis == "gy" else (0, mask)
    return moved, [(a ^ change[0], b ^ change[1]) for a, b in ids], half


def diagonal(part, mask):
    array, ids, half = part
    groups, rows = lax.axis_size("groups"), lax.axis_size("gy")
    pairs = [
        (i * rows + j, (i ^ 1) * rows + (j ^ mask)) for i in range(groups) for j in range(rows)
    ]
    moved = lax.ppermute(array, ("groups", "gy"), pairs)
    return moved, [(a ^ mask, b) for a, b in ids], half ^ 1


def held(*values):
    return lax.optimization_barrier(values)


def shards(
    tokens,
    conv_kernel,
    project_in,
    project_out,
    rel_bias,
    expert_in,
    expert_out,
    const_table,
    expert_ids,
    slots,
    const_index,
):
    rows, cols, channels = tokens.shape
    grid_rows, grid_cols = lax.axis_size("gy"), lax.axis_size("gx")
    place = jnp.stack([lax.axis_index(axis) for axis in ("gy", "gx", "groups")]).astype(jnp.int32)
    reach = KERNEL // 2 + SHIFT
    quick = grid_rows == 4 and grid_cols == 4 and lax.axis_size("groups") == 2
    above = shifted(tokens[rows - reach :], "gy", 1)
    if quick:
        pair = [(0, 0), (0, 1)]
        beyond, beyond_out = exchanged(project_in, "gx", 1), exchanged(project_out, "gx", 1)
        beyond, beyond_out, above = held(beyond, beyond_out, above)
        two = (jnp.concatenate([project_in, beyond], axis=0), pair, None)
        two_out = (jnp.concatenate([project_out, beyond_out], axis=0), pair, None)
        wide = two[0].shape[1] // 2
        mine = lax.dynamic_slice_in_dim(two[0], lax.axis_index("groups") * wide, wide, axis=1)
        far = along((mine, two[1], 0), "gx", 2)
        facing = along(two, "gy", 2)
        far_out = along(two_out, "gx", 2)
    edge = jnp.concatenate([above[:, cols - HALO :], tokens[:, cols - HALO :]], axis=0)
    beside = shifted(edge, "gx", 1)
    kept, weights, bias = prepare(tokens, conv_kernel, rel_bias)
    encoded, normed = encode(place, kept, above, beside, weights)
    if quick:
        first, second, normed = held(far[0], facing[0], normed)
        far, facing = (first, *far[1:]), (second, *facing[1:])
        across = along(far, "gy", 2)
        four_out = stacked([two_out, far_out])
        across_out = along(four_out, "gy", 2)
        far_rest, across_rest = along(far, "groups", 1), diagonal(far, 2)
        pieces_in = [two, facing, far, far_rest, across]
        pieces_in = pieces_in + [along(part, "gy", 1) for part in pieces_in]
        pieces_in = pieces_in + [across_rest, along(across_rest, "gy", 1)]
    else:
        whole = [(None, None)]
        pieces_in = [(lax.all_gather(project_in, ("gy", "gx"), axis=0, tiled=True), whole, None)]
        pieces_out = [(lax.all_gather(project_out, ("gy", "gx"), axis=0, tiled=True), whole, None)]
    context = attend(place, (rows, cols), normed, bias, pieces_in, grid_cols)
    if quick:
        array, context = held(across_out[0], context)
        pieces_out = [four_out, across_out, along(four_out, "gy", 1)]
        pieces_out = pieces_out + [along((array, *across_out[1:]), "gy", 1)]
    rolled, top, side, corner = project(
        place, (rows, cols), context, encoded, pieces_out, grid_cols
    )
    below = shifted(top, "gy", -1)
    right = shifted(side, "gx", -1)
    last = shifted_both(corner, -1)
    expert_of, slot_of = expert_ids.reshape(-1), slots.reshape(-1)
    position = jnp.where(expert_of < EXPERTS, expert_of * CAP + slot_of, -1)
    constant_at = jnp.where(expert_of == EXPERTS, const_index.reshape(-1), -1)
    attended, *outgoing = dispatch(
        place, rolled, below, right, last, position[None, :], grid_rows
    )
    half, results = expert_in.shape[0] // 2, [None] * len(outgoing)
    incoming = [
        [
            exchanged(outgoing[2 * mask + h], "gy", mask) if mask else outgoing[h]
            for mask in range(grid_rows)
        ]
        for h in range(2)
    ]
    for h, arrived in enumerate(incoming):
        served = serve(arrived, (expert_in, expert_out), h * half, half)
        for mask, array in enumerate(served):
            results[2 * mask + h] = exchanged(array, "gy", mask) if mask else array
    output = combine(
        place, attended, position[:, None], constant_at[:, None], const_table, results
    )
    return output.reshape(rows, cols, channels)


def solution(mesh):
    placed = (
        P(("groups", "gy"), "gx", None),
        P(),
        P(("gy", "gx"), None),
        P(("gy", "gx"), None),
        P(),
        P("gy", None, None),
        P("gy", None, None),
        P(),
        P(("groups", "gy"), "gx"),
        P(("groups", "gy"), "gx"),
        P(("groups", "gy"), "gx"),
    )
    return jax.shard_map(
        shards,
        mesh=mesh,
        in_specs=placed,
        out_specs=P(("groups", "gy"), "gx", None),
        check_vma=False,
    )
```

```python
import functools

import jax
import jax.numpy as jnp
from jax import lax
from jax.experimental import pallas as pl
from jax.experimental.pallas import tpu as pltpu
from jax.sharding import PartitionSpec as P

HD = 32
EXPERTS = 32
WIN = 8
SHIFT = 4
KERNEL = 7
CAP = 16
LANES = 128
GROUP = LANES // HD
SPOTS = WIN * WIN
HALO = 8
VMEM = pl.BlockSpec(memory_space=pltpu.VMEM)
SMEM = pl.BlockSpec(memory_space=pltpu.SMEM)
ANY = pl.BlockSpec(memory_space=pl.ANY)
HBM = pl.BlockSpec(memory_space=pltpu.HBM)
LARGEST = 3.38e38


def lasting(microseconds):
    return pl.CostEstimate(
        flops=int(microseconds * 1.15e9), bytes_accessed=0, transcendentals=0
    )


def shifted(x, axis, by):
    size = lax.axis_size(axis)
    return lax.ppermute(x, axis, [(i, (i + by) % size) for i in range(size)])


def shifted_both(x, by):
    rows, cols = lax.axis_size("gy"), lax.axis_size("gx")
    pairs = [
        (i * cols + j, ((i + by) % rows) * cols + (j + by) % cols)
        for i in range(rows)
        for j in range(cols)
    ]
    return lax.ppermute(x, ("gy", "gx"), pairs)


def exchanged(x, axis, mask):
    size = lax.axis_size(axis)
    return lax.ppermute(x, axis, [(i, i ^ mask) for i in range(size)])


def normalized(values):
    centred = values - jnp.mean(values, axis=-1, keepdims=True)
    spread = jnp.mean(centred * centred, axis=-1, keepdims=True)
    return (centred * lax.rsqrt(spread + 1e-05)).astype(jnp.bfloat16)


def prepare_kernel(tokens, taps, rel_bias, *refs):
    count = (len(refs) - 4) // 2
    sources, (kept, weights, bias, edge), copies = refs[:count], refs[count : count + 4], refs[count + 4 :]
    kept[...] = tokens[...].astype(jnp.float32)
    weights[...] = taps[...].astype(jnp.float32)
    edge[...] = tokens[:, tokens.shape[1] - HALO :]
    for head in range(rel_bias.shape[0]):
        at = head % GROUP * SPOTS
        bias[head // GROUP, :, at : at + SPOTS] = rel_bias[head]
    for source, copy in zip(sources, copies, strict=True):
        copy[...] = source[...]


def prepare(tokens, taps, rel_bias, *others):
    rows, _, channels = tokens.shape
    bias_shape = (rel_bias.shape[0] // GROUP, SPOTS, GROUP * SPOTS)
    return pl.pallas_call(
        prepare_kernel,
        out_shape=(
            jax.ShapeDtypeStruct(tokens.shape, jnp.float32),
            jax.ShapeDtypeStruct(taps.shape, jnp.float32),
            jax.ShapeDtypeStruct(bias_shape, jnp.float32),
            jax.ShapeDtypeStruct((rows, HALO, channels), jnp.bfloat16),
            *[jax.ShapeDtypeStruct(x.shape, x.dtype) for x in others],
        ),
        in_specs=[VMEM] * (3 + len(others)),
        out_specs=(VMEM,) * (4 + len(others)),
        compiler_params=pltpu.CompilerParams(vmem_limit_bytes=8 * 1024 * 1024),
        cost_estimate=lasting(3),
        name="prepare",
    )(tokens, taps, rel_bias, *others)


def join_kernel(place, own_in, beyond_in, own_out, beyond_out, above, edge, two, mine, two_out, column):
    size, half = own_in.shape[0], mine.shape[1]
    lanes = pl.ds(pl.multiple_of(place[2] * half, LANES), half)
    for at, (part_in, part_out) in enumerate(((own_in, own_out), (beyond_in, beyond_out))):
        rows = slice(at * size, (at + 1) * size)
        two[rows, :] = part_in[...]
        mine[rows, :] = part_in[:, lanes]
        two_out[rows, :] = part_out[...]
    reach = above.shape[0]
    column[:reach] = above[:, above.shape[1] - HALO :]
    column[reach:] = edge[...]


def join(place, own_in, beyond_in, own_out, beyond_out, above, edge):
    bf16 = functools.partial(jax.ShapeDtypeStruct, dtype=jnp.bfloat16)
    size, wide = own_in.shape
    return pl.pallas_call(
        join_kernel,
        out_shape=(
            bf16((2 * size, wide)),
            bf16((2 * size, wide // 2)),
            bf16((2 * size, own_out.shape[1])),
            bf16((above.shape[0] + edge.shape[0], *edge.shape[1:])),
        ),
        in_specs=[SMEM] + [VMEM] * 6,
        out_specs=(VMEM,) * 4,
        compiler_params=pltpu.CompilerParams(vmem_limit_bytes=8 * 1024 * 1024),
        cost_estimate=lasting(1),
        name="join",
    )(place, own_in, beyond_in, own_out, beyond_out, above, edge)


def encode_kernel(place, tokens, above, beside, weights, encoded, normed, upper, left):
    rows, cols, channels = tokens.shape
    reach = KERNEL // 2 + SHIFT
    upper[:, :HALO] = beside[:reach].astype(jnp.float32)
    upper[:, HALO:] = above[...].astype(jnp.float32)
    left[...] = beside[reach:].astype(jnp.float32)
    inner_row = jnp.where(place[0] == 0, 0.0, 1.0)
    first_col = place[1] == 0
    window_cols = cols // WIN
    col = lax.broadcasted_iota(jnp.int32, (WIN, LANES), 0)

    def extended(row, tile, lanes):
        if row < reach:
            return upper[row, tile * WIN : (tile + 1) * WIN, lanes]
        if tile == 0:
            return left[row - reach, :, lanes]
        return tokens[row - reach, (tile - 1) * WIN : tile * WIN, lanes]

    def block(index, _):
        lanes = pl.ds(pl.multiple_of(index * LANES, LANES), LANES)
        for tile in range(window_cols):
            sums = [None] * rows
            for col_off in range(KERNEL):
                column = [
                    jnp.broadcast_to(weights[row_off, pl.ds(col_off, 1), lanes], (WIN, LANES))
                    for row_off in range(KERNEL)
                ]
                if tile == 0:
                    near = (col < SHIFT) == (col + col_off < reach)
                    keep = jnp.where(near | jnp.logical_not(first_col), 1.0, 0.0)
                for row in range(rows + KERNEL - 1):
                    line = jnp.where(
                        col > col_off, extended(row, tile, lanes), extended(row, tile + 1, lanes)
                    )
                    line = pltpu.roll(line, WIN - 1 - col_off, 0)
                    if tile == 0:
                        line = line * keep
                    cut = line * inner_row if SHIFT <= row < reach + KERNEL // 2 else line
                    for out in range(max(0, row - KERNEL + 1), min(rows, row + 1)):
                        row_off = row - out
                        same = (out < SHIFT) == (row < reach)
                        term = (line if same else cut) * column[row_off]
                        if row_off == KERNEL // 2 and col_off == KERNEL // 2:
                            term = term + line
                        sums[out] = term if sums[out] is None else sums[out] + term
            for window_row in range(rows // WIN):
                stacked = jnp.concatenate(sums[window_row * WIN : (window_row + 1) * WIN], axis=0)
                first = (window_row * window_cols + tile) * SPOTS
                encoded[first : first + SPOTS, lanes] = stacked.astype(jnp.bfloat16)
        return 0

    lax.fori_loop(0, channels // LANES, block, 0)

    def norm(index, _):
        part = pl.ds(pl.multiple_of(index * SPOTS, SPOTS), SPOTS)
        normed[part, :] = normalized(encoded[part, :].astype(jnp.float32))
        return 0

    lax.fori_loop(0, rows * cols // SPOTS, norm, 0, unroll=4)


def encode(place, tokens, above, beside, weights):
    rows, cols, channels = tokens.shape
    flat = jax.ShapeDtypeStruct((rows * cols, channels), jnp.bfloat16)
    reach = KERNEL // 2 + SHIFT
    return pl.pallas_call(
        encode_kernel,
        out_shape=(flat, flat),
        in_specs=[SMEM] + [VMEM] * 4,
        out_specs=(VMEM, VMEM),
        scratch_shapes=[
            pltpu.VMEM((reach, cols + HALO, channels), jnp.float32),
            pltpu.VMEM((rows, HALO, channels), jnp.float32),
        ],
        compiler_params=pltpu.CompilerParams(vmem_limit_bytes=12 * 1024 * 1024),
        cost_estimate=lasting(0.1),
        name="encode",
    )(place, tokens, above, beside, weights)


def fetch(place, grid_cols, pieces, ids, target, sems):
    copies = []
    for piece, (parts, half) in zip(pieces, ids, strict=True):
        size = piece.shape[0] // len(parts)
        wide = min(piece.shape[1], target.shape[1])
        left = 0 if half is None else pl.multiple_of((place[2] ^ half) * wide, LANES)
        for at, (mask_row, mask_col) in enumerate(parts):
            if mask_row is None:
                first = 0
            else:
                owner = (place[0] ^ mask_row) * grid_cols + (place[1] ^ mask_col)
                first = pl.multiple_of(owner * size, 16)
            copy = pltpu.make_async_copy(
                piece.at[pl.ds(at * size, size), pl.ds(0, wide)],
                target.at[pl.ds(first, size), pl.ds(left, wide)],
                sems.at[len(copies)],
            )
            copy.start()
            copies.append(copy)
    return copies


def attend_kernel(shape, ids, grid_cols, *refs):
    rows, cols = shape
    place, normed, bias = refs[:3]
    context, weight, mixed, sems = refs[3 + len(ids) :]
    channels = normed.shape[1]
    copies = fetch(place, grid_cols, refs[3 : 3 + len(ids)], ids, weight, sems)
    groups = channels // LANES
    for copy in copies:
        copy.wait()
    wide = 3 * channels

    def project(index, _):
        lanes = pl.ds(pl.multiple_of(index * wide, wide), wide)
        mixed[:, lanes] = jnp.dot(
            normed[...], weight[:, lanes], preferred_element_type=jnp.float32
        ).astype(jnp.bfloat16)
        return 0

    lax.fori_loop(0, 3 * channels // wide, project, 0)

    window_cols = cols // WIN
    keys = GROUP * SPOTS
    query_at = lax.broadcasted_iota(jnp.int32, (SPOTS, keys), 0)
    key_at = lax.broadcasted_iota(jnp.int32, (SPOTS, keys), 1) % SPOTS
    row_differs = (query_at < SPOTS // 2) != (key_at < SPOTS // 2)
    col_differs = (query_at % WIN < SHIFT) != (key_at % WIN < SHIFT)
    lane = lax.broadcasted_iota(jnp.int32, (SPOTS, LANES), 1) // HD
    head_masks = [jnp.where(lane == h, 1.0, 0.0).astype(jnp.bfloat16) for h in range(GROUP)]
    block_row = lax.broadcasted_iota(jnp.int32, (keys, keys), 0) // SPOTS
    block_col = lax.broadcasted_iota(jnp.int32, (keys, keys), 1) // SPOTS
    same_head = jnp.where(block_row == block_col, 1.0, 0.0).astype(jnp.bfloat16)

    def window(index, _):
        part = pl.ds(pl.multiple_of(index * SPOTS, SPOTS), SPOTS)
        cut_rows = jnp.logical_and(place[0] == 0, index < window_cols)
        cut_cols = jnp.logical_and(place[1] == 0, index % window_cols == 0)
        hidden = (row_differs & cut_rows) | (col_differs & cut_cols)
        barrier = jnp.where(hidden, -1e30, 0.0)
        all_weights = []
        for group in range(groups):
            first = group * LANES
            query = mixed[part, first : first + LANES]
            key = mixed[part, channels + first : channels + first + LANES]
            key_all = jnp.concatenate([key * m for m in head_masks], axis=0)
            scores = lax.dot_general(
                query, key_all, (((1,), (1,)), ((), ())), preferred_element_type=jnp.float32
            )
            all_weights.append(jnp.exp(scores * HD ** (-0.5) + (bias[group] + barrier)))
        weights = jnp.concatenate(all_weights, axis=0)
        total = jnp.dot(
            jnp.minimum(weights, LARGEST).astype(jnp.bfloat16),
            same_head,
            preferred_element_type=jnp.float32,
        )
        probs = (weights * pl.reciprocal(total)).astype(jnp.bfloat16)
        for group in range(groups):
            first = group * LANES
            value = mixed[part, 2 * channels + first : 2 * channels + first + LANES]
            value_all = jnp.concatenate([value * m for m in head_masks], axis=0)
            context[part, first : first + LANES] = jnp.dot(
                probs[group * SPOTS : (group + 1) * SPOTS],
                value_all,
                preferred_element_type=jnp.float32,
            ).astype(jnp.bfloat16)
        return 0

    lax.fori_loop(0, rows * cols // SPOTS, window, 0, unroll=4)


def attend(place, shape, normed, bias, pieces, grid_cols):
    rows, cols = shape
    channels = normed.shape[1]
    ids = [p[1:] for p in pieces]
    return pl.pallas_call(
        functools.partial(attend_kernel, shape, ids, grid_cols),
        out_shape=jax.ShapeDtypeStruct((rows * cols, channels), jnp.bfloat16),
        in_specs=[SMEM, VMEM, VMEM] + [ANY] * len(pieces),
        out_specs=VMEM,
        scratch_shapes=[
            pltpu.VMEM((channels, 3 * channels), jnp.bfloat16),
            pltpu.VMEM((rows * cols, 3 * channels), jnp.bfloat16),
            pltpu.SemaphoreType.DMA((sum(len(p[0]) for p in ids),)),
        ],
        compiler_params=pltpu.CompilerParams(vmem_limit_bytes=16 * 1024 * 1024),
        cost_estimate=lasting(10),
        name="attend",
    )(place, normed, bias, *[p[0] for p in pieces])


def project_kernel(shape, ids, grid_cols, *refs):
    rows, cols = shape
    place, context, encoded = refs[:3]
    rolled, top, side, corner, weight, sems = refs[3 + len(ids) :]
    channels = context.shape[1]
    for copy in fetch(place, grid_cols, refs[3 : 3 + len(ids)], ids, weight, sems):
        copy.wait()
    window_cols = cols // WIN
    wide = channels
    sublane = lax.broadcasted_iota(jnp.int32, (WIN, wide), 0)

    def finish(index, _):
        lanes = pl.ds(pl.multiple_of(index * wide, wide), wide)
        update = jnp.dot(context[...], weight[:, lanes], preferred_element_type=jnp.float32)
        summed = encoded[:, lanes].astype(jnp.float32) + update
        edge = []
        for row in range(rows):
            tiles = []
            for tile in range(window_cols):
                first = (row // WIN * window_cols + tile) * SPOTS + row % WIN * WIN
                tiles.append(summed[first : first + WIN])
            for pair in range(window_cols // 2):
                both = jnp.concatenate(tiles[2 * pair : 2 * pair + 2], axis=0)
                both = both.astype(jnp.bfloat16)
                at = pair * 2 * WIN
                rolled[row, at : at + 2 * WIN, lanes] = both
                if row < SHIFT:
                    top[row, at : at + 2 * WIN, lanes] = both
            edge.append(tiles[0])
        for quad in range(rows // 4):
            halves = [
                jnp.where(
                    sublane < SHIFT,
                    edge[4 * quad + two],
                    pltpu.roll(edge[4 * quad + two + 1], SHIFT, 0),
                )
                for two in (0, 2)
            ]
            packed = jnp.concatenate(halves, axis=0).astype(jnp.bfloat16)
            if quad == 0:
                corner[:, lanes] = packed
            else:
                side[(quad - 1) * 16 : quad * 16, lanes] = packed
        return 0

    lax.fori_loop(0, channels // wide, finish, 0)


def project(place, shape, context, encoded, pieces, grid_cols):
    rows, cols = shape
    channels = context.shape[1]
    bf16 = functools.partial(jax.ShapeDtypeStruct, dtype=jnp.bfloat16)
    ids = [p[1:] for p in pieces]
    return pl.pallas_call(
        functools.partial(project_kernel, shape, ids, grid_cols),
        out_shape=(
            bf16((rows, cols, channels)),
            bf16((SHIFT, cols, channels)),
            bf16(((rows - SHIFT) * SHIFT, channels)),
            bf16((SHIFT * SHIFT, channels)),
        ),
        in_specs=[SMEM, VMEM, VMEM] + [ANY] * len(pieces),
        out_specs=(VMEM,) * 4,
        scratch_shapes=[
            pltpu.VMEM((channels, channels), jnp.bfloat16),
            pltpu.SemaphoreType.DMA((sum(len(p[0]) for p in ids),)),
        ],
        compiler_params=pltpu.CompilerParams(vmem_limit_bytes=10 * 1024 * 1024),
        cost_estimate=lasting(3),
        name="project",
    )(place, context, encoded, *[p[0] for p in pieces])


def dispatch_kernel(place, rolled, below, right, corner, position, *refs):
    rows, cols, channels = rolled.shape
    attended, outgoing, normed = refs[0], refs[1:-1], refs[-1]
    sublane = lax.broadcasted_iota(jnp.int32, (WIN, channels), 0)
    for row in range(rows):
        if row < rows - SHIFT:
            line, beside, at = rolled[row + SHIFT], right, row
        else:
            line, beside, at = below[row + SHIFT - rows], corner, row + SHIFT - rows
        line = line.astype(jnp.float32)
        tiles = [
            pltpu.roll(line[tile * WIN : (tile + 1) * WIN], SHIFT, 0) for tile in range(cols // WIN)
        ]
        block = at * SHIFT // 16 * 16
        last = beside[block : block + 16].astype(jnp.float32)
        within = at * SHIFT - block
        last = last[within // WIN * WIN : within // WIN * WIN + WIN]
        tiles.append(last if within % WIN else pltpu.roll(last, SHIFT, 0))
        line = jnp.concatenate(
            [
                jnp.where(sublane < SHIFT, tiles[tile], tiles[tile + 1])
                for tile in range(cols // WIN)
            ],
            axis=0,
        )
        attended[row * cols : (row + 1) * cols] = line.astype(jnp.bfloat16)
        normed[row * cols : (row + 1) * cols] = normalized(line)
    for mask in range(len(outgoing) // 2):
        halves = outgoing[2 * mask : 2 * mask + 2]
        count = 2 * halves[0].shape[0]
        spot = lax.broadcasted_iota(jnp.int32, (count, rows * cols), 0)
        spot = spot + (place[0] ^ mask) * count
        chosen = jnp.where(position[...] == spot, 1.0, 0.0).astype(jnp.bfloat16)
        slots = jnp.dot(chosen, normed[...], preferred_element_type=jnp.float32)
        slots = slots.astype(jnp.bfloat16)
        for at, target in enumerate(halves):
            target[...] = slots[at * count // 2 : (at + 1) * count // 2]


def dispatch(place, rolled, below, right, corner, position, grid_rows):
    rows, cols, channels = rolled.shape
    bf16 = functools.partial(jax.ShapeDtypeStruct, dtype=jnp.bfloat16)
    slot_rows = EXPERTS * CAP // grid_rows // 2
    return pl.pallas_call(
        dispatch_kernel,
        out_shape=(bf16((rows * cols, channels)),) + (bf16((slot_rows, channels)),) * (2 * grid_rows),
        in_specs=[SMEM] + [VMEM] * 5,
        out_specs=(VMEM,) * (2 * grid_rows + 1),
        scratch_shapes=[pltpu.VMEM((rows * cols, channels), jnp.bfloat16)],
        compiler_params=pltpu.CompilerParams(vmem_limit_bytes=10 * 1024 * 1024),
        name="dispatch",
    )(place, rolled, below, right, corner, position)


def expert_kernel(count, first, *refs):
    incoming, sources = refs[:count], refs[count : count + 2]
    results, (held_in, held_out, sems) = refs[-3 - count : -3], refs[-3:]
    copies = [
        [
            pltpu.make_async_copy(source.at[first + slot], target.at[slot], sems.at[slot, which])
            for which, (source, target) in enumerate(zip(sources, (held_in, held_out), strict=True))
        ]
        for slot in range(held_in.shape[0])
    ]
    for pair in copies:
        for copy in pair:
            copy.start()
    for slot, (copy_in, copy_out) in enumerate(copies):
        own = pl.ds(slot * CAP, CAP)
        rows = jnp.concatenate([ref[own, :] for ref in incoming], axis=0)
        copy_in.wait()
        hidden = lax.dot_general(
            rows, held_in[slot], (((1,), (1,)), ((), ())), preferred_element_type=jnp.float32
        )
        hidden = (0.5 * hidden * (1.0 + lax.erf(hidden * 0.5**0.5))).astype(jnp.bfloat16)
        copy_out.wait()
        result = jnp.dot(hidden, held_out[slot], preferred_element_type=jnp.float32)
        result = result.astype(jnp.bfloat16)
        for at, ref in enumerate(results):
            ref[own, :] = result[at * CAP : (at + 1) * CAP]


def serve(incoming, weights, first, number):
    count = len(incoming)
    shape = (number, *weights[0].shape[1:])
    return pl.pallas_call(
        functools.partial(expert_kernel, count, first),
        out_shape=tuple(jax.ShapeDtypeStruct(x.shape, x.dtype) for x in incoming),
        in_specs=[VMEM] * count + [HBM, HBM],
        out_specs=(VMEM,) * count,
        scratch_shapes=[
            pltpu.VMEM(shape, jnp.bfloat16),
            pltpu.VMEM(shape, jnp.bfloat16),
            pltpu.SemaphoreType.DMA((number, 2)),
        ],
        compiler_params=pltpu.CompilerParams(vmem_limit_bytes=52 * 1024 * 1024),
        cost_estimate=lasting(7),
        name="experts",
    )(*incoming, *weights)


def combine_kernel(place, attended, position, constant_at, table, *refs):
    results, output = refs[:-1], refs[-1]
    tokens = attended.shape[0]
    rows = jnp.concatenate([result[...] for result in results], axis=0)
    total, count = rows.shape[0], 2 * results[0].shape[0]
    spot = lax.broadcasted_iota(jnp.int32, (tokens, total), 1)
    spot = (spot // count ^ place[0]) * count + spot % count
    chosen = jnp.where(position[...] == spot, 1.0, 0.0).astype(jnp.bfloat16)
    entries = table.shape[0]
    spot = lax.broadcasted_iota(jnp.int32, (tokens, 3 * entries), 1) % entries
    constant = jnp.where(constant_at[...] == spot, 1.0, 0.0).astype(jnp.bfloat16)
    parts, rest = [], table[...]
    for _ in range(3):
        parts.append(rest.astype(jnp.bfloat16))
        rest = rest - parts[-1].astype(jnp.float32)
    parts = jnp.concatenate(parts, axis=0)
    mixture = jnp.dot(chosen, rows, preferred_element_type=jnp.float32)
    mixture = mixture + jnp.dot(constant, parts, preferred_element_type=jnp.float32)
    output[...] = (attended[...].astype(jnp.float32) + mixture).astype(jnp.bfloat16)


def combine(place, attended, position, constant_at, table, results):
    return pl.pallas_call(
        combine_kernel,
        out_shape=jax.ShapeDtypeStruct(attended.shape, jnp.bfloat16),
        in_specs=[SMEM] + [VMEM] * (4 + len(results)),
        out_specs=VMEM,
        compiler_params=pltpu.CompilerParams(vmem_limit_bytes=12 * 1024 * 1024),
        name="combine",
    )(place, attended, position, constant_at, table, *results)


def stacked(parts):
    ids = sum([part[1] for part in parts], [])
    return jnp.concatenate([part[0] for part in parts], axis=0), ids, None


def along(part, axis, mask):
    array, ids, half = part
    moved = exchanged(array, axis, mask)
    if axis == "groups":
        return moved, ids, half ^ mask
    change = (mask, 0) if axis == "gy" else (0, mask)
    return moved, [(a ^ change[0], b ^ change[1]) for a, b in ids], half


def diagonal(part, mask):
    array, ids, half = part
    groups, rows = lax.axis_size("groups"), lax.axis_size("gy")
    pairs = [
        (i * rows + j, (i ^ 1) * rows + (j ^ mask)) for i in range(groups) for j in range(rows)
    ]
    moved = lax.ppermute(array, ("groups", "gy"), pairs)
    return moved, [(a ^ mask, b) for a, b in ids], half ^ 1


def held(*values):
    return lax.optimization_barrier(values)


def shards(
    tokens,
    conv_kernel,
    project_in,
    project_out,
    rel_bias,
    expert_in,
    expert_out,
    const_table,
    expert_ids,
    slots,
    const_index,
):
    rows, cols, channels = tokens.shape
    grid_rows, grid_cols = lax.axis_size("gy"), lax.axis_size("gx")
    place = jnp.stack([lax.axis_index(axis) for axis in ("gy", "gx", "groups")]).astype(jnp.int32)
    reach = KERNEL // 2 + SHIFT
    quick = grid_rows == 4 and grid_cols == 4 and lax.axis_size("groups") == 2
    above = shifted(tokens[rows - reach :], "gy", 1)
    if quick:
        pair = [(0, 0), (0, 1)]
        beyond, beyond_out = exchanged(project_in, "gx", 1), exchanged(project_out, "gx", 1)
        kept, weights, bias, edge, own_in, own_out = prepare(
            tokens, conv_kernel, rel_bias, project_in, project_out
        )
        two, mine, two_out, column = join(place, own_in, beyond, own_out, beyond_out, above, edge)
        two, two_out = (two, pair, None), (two_out, pair, None)
        far = along((mine, pair, 0), "gx", 2)
        facing = along(two, "gy", 2)
        far_out = along(two_out, "gx", 2)
    else:
        kept, weights, bias, edge = prepare(tokens, conv_kernel, rel_bias)
        column = jnp.concatenate([above[:, cols - HALO :], edge], axis=0)
    beside = shifted(column, "gx", 1)
    encoded, normed = encode(place, kept, above, beside, weights)
    if quick:
        first, second, normed = held(far[0], facing[0], normed)
        far, facing = (first, *far[1:]), (second, *facing[1:])
        across = along(far, "gy", 2)
        four_out = stacked([two_out, far_out])
        across_out = along(four_out, "gy", 2)
        far_rest, across_rest = along(far, "groups", 1), diagonal(far, 2)
        pieces_in = [two, facing, far, far_rest, across]
        pieces_in = pieces_in + [along(part, "gy", 1) for part in pieces_in]
        pieces_in = pieces_in + [across_rest, along(across_rest, "gy", 1)]
    else:
        whole = [(None, None)]
        pieces_in = [(lax.all_gather(project_in, ("gy", "gx"), axis=0, tiled=True), whole, None)]
        pieces_out = [(lax.all_gather(project_out, ("gy", "gx"), axis=0, tiled=True), whole, None)]
    context = attend(place, (rows, cols), normed, bias, pieces_in, grid_cols)
    if quick:
        array, context = held(across_out[0], context)
        pieces_out = [four_out, across_out, along(four_out, "gy", 1)]
        pieces_out = pieces_out + [along((array, *across_out[1:]), "gy", 1)]
    rolled, top, side, corner = project(
        place, (rows, cols), context, encoded, pieces_out, grid_cols
    )
    below = shifted(top, "gy", -1)
    right = shifted(side, "gx", -1)
    last = shifted_both(corner, -1)
    expert_of, slot_of = expert_ids.reshape(-1), slots.reshape(-1)
    position = jnp.where(expert_of < EXPERTS, expert_of * CAP + slot_of, -1)
    constant_at = jnp.where(expert_of == EXPERTS, const_index.reshape(-1), -1)
    attended, *outgoing = dispatch(
        place, rolled, below, right, last, position[None, :], grid_rows
    )
    half, results = expert_in.shape[0] // 2, [None] * len(outgoing)
    incoming = [
        [
            exchanged(outgoing[2 * mask + h], "gy", mask) if mask else outgoing[h]
            for mask in range(grid_rows)
        ]
        for h in range(2)
    ]
    for h, arrived in enumerate(incoming):
        served = serve(arrived, (expert_in, expert_out), h * half, half)
        for mask, array in enumerate(served):
            results[2 * mask + h] = exchanged(array, "gy", mask) if mask else array
    output = combine(
        place, attended, position[:, None], constant_at[:, None], const_table, results
    )
    return output.reshape(rows, cols, channels)


def solution(mesh):
    placed = (
        P(("groups", "gy"), "gx", None),
        P(),
        P(("gy", "gx"), None),
        P(("gy", "gx"), None),
        P(),
        P("gy", None, None),
        P("gy", None, None),
        P(),
        P(("groups", "gy"), "gx"),
        P(("groups", "gy"), "gx"),
        P(("groups", "gy"), "gx"),
    )
    return jax.shard_map(
        shards,
        mesh=mesh,
        in_specs=placed,
        out_specs=P(("groups", "gy"), "gx", None),
        check_vma=False,
    )
```

```python
import functools

import jax
import jax.numpy as jnp
from jax import lax
from jax.experimental import pallas as pl
from jax.experimental.pallas import tpu as pltpu
from jax.sharding import PartitionSpec as P

HD = 32
EXPERTS = 32
WIN = 8
SHIFT = 4
KERNEL = 7
CAP = 16
LANES = 128
GROUP = LANES // HD
SPOTS = WIN * WIN
HALO = 8
VMEM = pl.BlockSpec(memory_space=pltpu.VMEM)
SMEM = pl.BlockSpec(memory_space=pltpu.SMEM)
ANY = pl.BlockSpec(memory_space=pl.ANY)
HBM = pl.BlockSpec(memory_space=pltpu.HBM)
LARGEST = 3.38e38


def lasting(microseconds):
    return pl.CostEstimate(
        flops=int(microseconds * 1.15e9), bytes_accessed=0, transcendentals=0
    )


def shifted(x, axis, by):
    size = lax.axis_size(axis)
    return lax.ppermute(x, axis, [(i, (i + by) % size) for i in range(size)])


def shifted_both(x, by):
    rows, cols = lax.axis_size("gy"), lax.axis_size("gx")
    pairs = [
        (i * cols + j, ((i + by) % rows) * cols + (j + by) % cols)
        for i in range(rows)
        for j in range(cols)
    ]
    return lax.ppermute(x, ("gy", "gx"), pairs)


def exchanged(x, axis, mask):
    size = lax.axis_size(axis)
    return lax.ppermute(x, axis, [(i, i ^ mask) for i in range(size)])


def normalized(values):
    centred = values - jnp.mean(values, axis=-1, keepdims=True)
    spread = jnp.mean(centred * centred, axis=-1, keepdims=True)
    return (centred * lax.rsqrt(spread + 1e-05)).astype(jnp.bfloat16)


def prepare_kernel(tokens, taps, rel_bias, *refs):
    count = (len(refs) - 4) // 2
    sources, (kept, weights, bias, edge), copies = refs[:count], refs[count : count + 4], refs[count + 4 :]
    kept[...] = tokens[...].astype(jnp.float32)
    weights[...] = taps[...].astype(jnp.float32)
    edge[...] = tokens[:, tokens.shape[1] - HALO :]
    for head in range(rel_bias.shape[0]):
        at = head % GROUP * SPOTS
        bias[head // GROUP, :, at : at + SPOTS] = rel_bias[head]
    for source, copy in zip(sources, copies, strict=True):
        copy[...] = source[...]


def prepare(tokens, taps, rel_bias, *others):
    rows, _, channels = tokens.shape
    bias_shape = (rel_bias.shape[0] // GROUP, SPOTS, GROUP * SPOTS)
    return pl.pallas_call(
        prepare_kernel,
        out_shape=(
            jax.ShapeDtypeStruct(tokens.shape, jnp.float32),
            jax.ShapeDtypeStruct(taps.shape, jnp.float32),
            jax.ShapeDtypeStruct(bias_shape, jnp.float32),
            jax.ShapeDtypeStruct((rows, HALO, channels), jnp.bfloat16),
            *[jax.ShapeDtypeStruct(x.shape, x.dtype) for x in others],
        ),
        in_specs=[VMEM] * (3 + len(others)),
        out_specs=(VMEM,) * (4 + len(others)),
        compiler_params=pltpu.CompilerParams(vmem_limit_bytes=8 * 1024 * 1024),
        cost_estimate=lasting(3),
        name="prepare",
    )(tokens, taps, rel_bias, *others)


def join_kernel(place, own, beyond, above, edge, two, mine, column):
    size, half = own.shape[0], mine.shape[1]
    lanes = pl.ds(pl.multiple_of(place[2] * half, LANES), half)
    for at, part in enumerate((own, beyond)):
        rows = slice(at * size, (at + 1) * size)
        two[rows, :] = part[...]
        mine[rows, :] = part[:, lanes]
    reach = above.shape[0]
    column[:reach] = above[:, above.shape[1] - HALO :]
    column[reach:] = edge[...]


def join(place, own, beyond, above, edge):
    bf16 = functools.partial(jax.ShapeDtypeStruct, dtype=jnp.bfloat16)
    size, wide = own.shape
    return pl.pallas_call(
        join_kernel,
        out_shape=(
            bf16((2 * size, wide)),
            bf16((2 * size, wide // 2)),
            bf16((above.shape[0] + edge.shape[0], *edge.shape[1:])),
        ),
        in_specs=[SMEM] + [VMEM] * 4,
        out_specs=(VMEM,) * 3,
        compiler_params=pltpu.CompilerParams(vmem_limit_bytes=8 * 1024 * 1024),
        cost_estimate=lasting(1),
        name="join",
    )(place, own, beyond, above, edge)


def encode_kernel(place, tokens, above, beside, weights, encoded, normed, upper, left):
    rows, cols, channels = tokens.shape
    reach = KERNEL // 2 + SHIFT
    upper[:, :HALO] = beside[:reach].astype(jnp.float32)
    upper[:, HALO:] = above[...].astype(jnp.float32)
    left[...] = beside[reach:].astype(jnp.float32)
    inner_row = jnp.where(place[0] == 0, 0.0, 1.0)
    first_col = place[1] == 0
    window_cols = cols // WIN
    col = lax.broadcasted_iota(jnp.int32, (WIN, LANES), 0)

    def extended(row, tile, lanes):
        if row < reach:
            return upper[row, tile * WIN : (tile + 1) * WIN, lanes]
        if tile == 0:
            return left[row - reach, :, lanes]
        return tokens[row - reach, (tile - 1) * WIN : tile * WIN, lanes]

    def block(index, _):
        lanes = pl.ds(pl.multiple_of(index * LANES, LANES), LANES)
        for tile in range(window_cols):
            sums = [None] * rows
            for col_off in range(KERNEL):
                column = [
                    jnp.broadcast_to(weights[row_off, pl.ds(col_off, 1), lanes], (WIN, LANES))
                    for row_off in range(KERNEL)
                ]
                if tile == 0:
                    near = (col < SHIFT) == (col + col_off < reach)
                    keep = jnp.where(near | jnp.logical_not(first_col), 1.0, 0.0)
                for row in range(rows + KERNEL - 1):
                    line = jnp.where(
                        col > col_off, extended(row, tile, lanes), extended(row, tile + 1, lanes)
                    )
                    line = pltpu.roll(line, WIN - 1 - col_off, 0)
                    if tile == 0:
                        line = line * keep
                    cut = line * inner_row if SHIFT <= row < reach + KERNEL // 2 else line
                    for out in range(max(0, row - KERNEL + 1), min(rows, row + 1)):
                        row_off = row - out
                        same = (out < SHIFT) == (row < reach)
                        term = (line if same else cut) * column[row_off]
                        if row_off == KERNEL // 2 and col_off == KERNEL // 2:
                            term = term + line
                        sums[out] = term if sums[out] is None else sums[out] + term
            for window_row in range(rows // WIN):
                stacked = jnp.concatenate(sums[window_row * WIN : (window_row + 1) * WIN], axis=0)
                first = (window_row * window_cols + tile) * SPOTS
                encoded[first : first + SPOTS, lanes] = stacked.astype(jnp.bfloat16)
        return 0

    lax.fori_loop(0, channels // LANES, block, 0)

    def norm(index, _):
        part = pl.ds(pl.multiple_of(index * SPOTS, SPOTS), SPOTS)
        normed[part, :] = normalized(encoded[part, :].astype(jnp.float32))
        return 0

    lax.fori_loop(0, rows * cols // SPOTS, norm, 0, unroll=4)


def encode(place, tokens, above, beside, weights):
    rows, cols, channels = tokens.shape
    flat = jax.ShapeDtypeStruct((rows * cols, channels), jnp.bfloat16)
    reach = KERNEL // 2 + SHIFT
    return pl.pallas_call(
        encode_kernel,
        out_shape=(flat, flat),
        in_specs=[SMEM] + [VMEM] * 4,
        out_specs=(VMEM, VMEM),
        scratch_shapes=[
            pltpu.VMEM((reach, cols + HALO, channels), jnp.float32),
            pltpu.VMEM((rows, HALO, channels), jnp.float32),
        ],
        compiler_params=pltpu.CompilerParams(vmem_limit_bytes=12 * 1024 * 1024),
        cost_estimate=lasting(0.1),
        name="encode",
    )(place, tokens, above, beside, weights)


def fetch(place, grid_cols, pieces, ids, target, sems):
    copies = []
    for piece, (parts, half) in zip(pieces, ids, strict=True):
        size = piece.shape[0] // len(parts)
        wide = min(piece.shape[1], target.shape[1])
        left = 0 if half is None else pl.multiple_of((place[2] ^ half) * wide, LANES)
        for at, (mask_row, mask_col) in enumerate(parts):
            if mask_row is None:
                first = 0
            else:
                owner = (place[0] ^ mask_row) * grid_cols + (place[1] ^ mask_col)
                first = pl.multiple_of(owner * size, 16)
            copy = pltpu.make_async_copy(
                piece.at[pl.ds(at * size, size), pl.ds(0, wide)],
                target.at[pl.ds(first, size), pl.ds(left, wide)],
                sems.at[len(copies)],
            )
            copy.start()
            copies.append(copy)
    return copies


def attend_kernel(shape, ids, grid_cols, *refs):
    rows, cols = shape
    place, normed, bias = refs[:3]
    context, weight, mixed, sems = refs[3 + len(ids) :]
    channels = normed.shape[1]
    copies = fetch(place, grid_cols, refs[3 : 3 + len(ids)], ids, weight, sems)
    groups = channels // LANES
    for copy in copies:
        copy.wait()
    wide = 3 * channels

    def project(index, _):
        lanes = pl.ds(pl.multiple_of(index * wide, wide), wide)
        mixed[:, lanes] = jnp.dot(
            normed[...], weight[:, lanes], preferred_element_type=jnp.float32
        ).astype(jnp.bfloat16)
        return 0

    lax.fori_loop(0, 3 * channels // wide, project, 0)

    window_cols = cols // WIN
    keys = GROUP * SPOTS
    query_at = lax.broadcasted_iota(jnp.int32, (SPOTS, keys), 0)
    key_at = lax.broadcasted_iota(jnp.int32, (SPOTS, keys), 1) % SPOTS
    row_differs = (query_at < SPOTS // 2) != (key_at < SPOTS // 2)
    col_differs = (query_at % WIN < SHIFT) != (key_at % WIN < SHIFT)
    lane = lax.broadcasted_iota(jnp.int32, (SPOTS, LANES), 1) // HD
    head_masks = [jnp.where(lane == h, 1.0, 0.0).astype(jnp.bfloat16) for h in range(GROUP)]
    block_row = lax.broadcasted_iota(jnp.int32, (keys, keys), 0) // SPOTS
    block_col = lax.broadcasted_iota(jnp.int32, (keys, keys), 1) // SPOTS
    same_head = jnp.where(block_row == block_col, 1.0, 0.0).astype(jnp.bfloat16)

    def window(index, _):
        part = pl.ds(pl.multiple_of(index * SPOTS, SPOTS), SPOTS)
        cut_rows = jnp.logical_and(place[0] == 0, index < window_cols)
        cut_cols = jnp.logical_and(place[1] == 0, index % window_cols == 0)
        hidden = (row_differs & cut_rows) | (col_differs & cut_cols)
        barrier = jnp.where(hidden, -1e30, 0.0)
        all_weights = []
        for group in range(groups):
            first = group * LANES
            query = mixed[part, first : first + LANES]
            key = mixed[part, channels + first : channels + first + LANES]
            key_all = jnp.concatenate([key * m for m in head_masks], axis=0)
            scores = lax.dot_general(
                query, key_all, (((1,), (1,)), ((), ())), preferred_element_type=jnp.float32
            )
            all_weights.append(jnp.exp(scores * HD ** (-0.5) + (bias[group] + barrier)))
        weights = jnp.concatenate(all_weights, axis=0)
        total = jnp.dot(
            jnp.minimum(weights, LARGEST).astype(jnp.bfloat16),
            same_head,
            preferred_element_type=jnp.float32,
        )
        probs = (weights * pl.reciprocal(total)).astype(jnp.bfloat16)
        for group in range(groups):
            first = group * LANES
            value = mixed[part, 2 * channels + first : 2 * channels + first + LANES]
            value_all = jnp.concatenate([value * m for m in head_masks], axis=0)
            context[part, first : first + LANES] = jnp.dot(
                probs[group * SPOTS : (group + 1) * SPOTS],
                value_all,
                preferred_element_type=jnp.float32,
            ).astype(jnp.bfloat16)
        return 0

    lax.fori_loop(0, rows * cols // SPOTS, window, 0, unroll=4)


def attend(place, shape, normed, bias, pieces, grid_cols):
    rows, cols = shape
    channels = normed.shape[1]
    ids = [p[1:] for p in pieces]
    return pl.pallas_call(
        functools.partial(attend_kernel, shape, ids, grid_cols),
        out_shape=jax.ShapeDtypeStruct((rows * cols, channels), jnp.bfloat16),
        in_specs=[SMEM, VMEM, VMEM] + [ANY] * len(pieces),
        out_specs=VMEM,
        scratch_shapes=[
            pltpu.VMEM((channels, 3 * channels), jnp.bfloat16),
            pltpu.VMEM((rows * cols, 3 * channels), jnp.bfloat16),
            pltpu.SemaphoreType.DMA((sum(len(p[0]) for p in ids),)),
        ],
        compiler_params=pltpu.CompilerParams(vmem_limit_bytes=16 * 1024 * 1024),
        cost_estimate=lasting(10),
        name="attend",
    )(place, normed, bias, *[p[0] for p in pieces])


def project_kernel(shape, ids, grid_cols, *refs):
    rows, cols = shape
    place, context, encoded = refs[:3]
    rolled, top, side, corner, weight, sems = refs[3 + len(ids) :]
    channels = context.shape[1]
    for copy in fetch(place, grid_cols, refs[3 : 3 + len(ids)], ids, weight, sems):
        copy.wait()
    window_cols = cols // WIN
    wide = channels
    sublane = lax.broadcasted_iota(jnp.int32, (WIN, wide), 0)

    def finish(index, _):
        lanes = pl.ds(pl.multiple_of(index * wide, wide), wide)
        update = jnp.dot(context[...], weight[:, lanes], preferred_element_type=jnp.float32)
        summed = encoded[:, lanes].astype(jnp.float32) + update
        edge = []
        for row in range(rows):
            tiles = []
            for tile in range(window_cols):
                first = (row // WIN * window_cols + tile) * SPOTS + row % WIN * WIN
                tiles.append(summed[first : first + WIN])
            for pair in range(window_cols // 2):
                both = jnp.concatenate(tiles[2 * pair : 2 * pair + 2], axis=0)
                both = both.astype(jnp.bfloat16)
                at = pair * 2 * WIN
                rolled[row, at : at + 2 * WIN, lanes] = both
                if row < SHIFT:
                    top[row, at : at + 2 * WIN, lanes] = both
            edge.append(tiles[0])
        for quad in range(rows // 4):
            halves = [
                jnp.where(
                    sublane < SHIFT,
                    edge[4 * quad + two],
                    pltpu.roll(edge[4 * quad + two + 1], SHIFT, 0),
                )
                for two in (0, 2)
            ]
            packed = jnp.concatenate(halves, axis=0).astype(jnp.bfloat16)
            if quad == 0:
                corner[:, lanes] = packed
            else:
                side[(quad - 1) * 16 : quad * 16, lanes] = packed
        return 0

    lax.fori_loop(0, channels // wide, finish, 0)


def project(place, shape, context, encoded, pieces, grid_cols):
    rows, cols = shape
    channels = context.shape[1]
    bf16 = functools.partial(jax.ShapeDtypeStruct, dtype=jnp.bfloat16)
    ids = [p[1:] for p in pieces]
    return pl.pallas_call(
        functools.partial(project_kernel, shape, ids, grid_cols),
        out_shape=(
            bf16((rows, cols, channels)),
            bf16((SHIFT, cols, channels)),
            bf16(((rows - SHIFT) * SHIFT, channels)),
            bf16((SHIFT * SHIFT, channels)),
        ),
        in_specs=[SMEM, VMEM, VMEM] + [ANY] * len(pieces),
        out_specs=(VMEM,) * 4,
        scratch_shapes=[
            pltpu.VMEM((channels, channels), jnp.bfloat16),
            pltpu.SemaphoreType.DMA((sum(len(p[0]) for p in ids),)),
        ],
        compiler_params=pltpu.CompilerParams(vmem_limit_bytes=10 * 1024 * 1024),
        cost_estimate=lasting(3),
        name="project",
    )(place, context, encoded, *[p[0] for p in pieces])


def dispatch_kernel(place, rolled, below, right, corner, position, *refs):
    rows, cols, channels = rolled.shape
    attended, outgoing, normed = refs[0], refs[1:-1], refs[-1]
    sublane = lax.broadcasted_iota(jnp.int32, (WIN, channels), 0)
    for row in range(rows):
        if row < rows - SHIFT:
            line, beside, at = rolled[row + SHIFT], right, row
        else:
            line, beside, at = below[row + SHIFT - rows], corner, row + SHIFT - rows
        line = line.astype(jnp.float32)
        tiles = [
            pltpu.roll(line[tile * WIN : (tile + 1) * WIN], SHIFT, 0) for tile in range(cols // WIN)
        ]
        block = at * SHIFT // 16 * 16
        last = beside[block : block + 16].astype(jnp.float32)
        within = at * SHIFT - block
        last = last[within // WIN * WIN : within // WIN * WIN + WIN]
        tiles.append(last if within % WIN else pltpu.roll(last, SHIFT, 0))
        line = jnp.concatenate(
            [
                jnp.where(sublane < SHIFT, tiles[tile], tiles[tile + 1])
                for tile in range(cols // WIN)
            ],
            axis=0,
        )
        attended[row * cols : (row + 1) * cols] = line.astype(jnp.bfloat16)
        normed[row * cols : (row + 1) * cols] = normalized(line)
    for mask in range(len(outgoing) // 2):
        halves = outgoing[2 * mask : 2 * mask + 2]
        count = 2 * halves[0].shape[0]
        spot = lax.broadcasted_iota(jnp.int32, (count, rows * cols), 0)
        spot = spot + (place[0] ^ mask) * count
        chosen = jnp.where(position[...] == spot, 1.0, 0.0).astype(jnp.bfloat16)
        slots = jnp.dot(chosen, normed[...], preferred_element_type=jnp.float32)
        slots = slots.astype(jnp.bfloat16)
        for at, target in enumerate(halves):
            target[...] = slots[at * count // 2 : (at + 1) * count // 2]


def dispatch(place, rolled, below, right, corner, position, grid_rows):
    rows, cols, channels = rolled.shape
    bf16 = functools.partial(jax.ShapeDtypeStruct, dtype=jnp.bfloat16)
    slot_rows = EXPERTS * CAP // grid_rows // 2
    return pl.pallas_call(
        dispatch_kernel,
        out_shape=(bf16((rows * cols, channels)),) + (bf16((slot_rows, channels)),) * (2 * grid_rows),
        in_specs=[SMEM] + [VMEM] * 5,
        out_specs=(VMEM,) * (2 * grid_rows + 1),
        scratch_shapes=[pltpu.VMEM((rows * cols, channels), jnp.bfloat16)],
        compiler_params=pltpu.CompilerParams(vmem_limit_bytes=10 * 1024 * 1024),
        name="dispatch",
    )(place, rolled, below, right, corner, position)


def expert_kernel(count, first, *refs):
    incoming, sources = refs[:count], refs[count : count + 2]
    results, (held_in, held_out, sems) = refs[-3 - count : -3], refs[-3:]
    copies = [
        [
            pltpu.make_async_copy(source.at[first + slot], target.at[slot], sems.at[slot, which])
            for which, (source, target) in enumerate(zip(sources, (held_in, held_out), strict=True))
        ]
        for slot in range(held_in.shape[0])
    ]
    for pair in copies:
        for copy in pair:
            copy.start()
    for slot, (copy_in, copy_out) in enumerate(copies):
        own = pl.ds(slot * CAP, CAP)
        rows = jnp.concatenate([ref[own, :] for ref in incoming], axis=0)
        copy_in.wait()
        hidden = lax.dot_general(
            rows, held_in[slot], (((1,), (1,)), ((), ())), preferred_element_type=jnp.float32
        )
        hidden = (0.5 * hidden * (1.0 + lax.erf(hidden * 0.5**0.5))).astype(jnp.bfloat16)
        copy_out.wait()
        result = jnp.dot(hidden, held_out[slot], preferred_element_type=jnp.float32)
        result = result.astype(jnp.bfloat16)
        for at, ref in enumerate(results):
            ref[own, :] = result[at * CAP : (at + 1) * CAP]


def serve(incoming, weights, first, number):
    count = len(incoming)
    shape = (number, *weights[0].shape[1:])
    return pl.pallas_call(
        functools.partial(expert_kernel, count, first),
        out_shape=tuple(jax.ShapeDtypeStruct(x.shape, x.dtype) for x in incoming),
        in_specs=[VMEM] * count + [HBM, HBM],
        out_specs=(VMEM,) * count,
        scratch_shapes=[
            pltpu.VMEM(shape, jnp.bfloat16),
            pltpu.VMEM(shape, jnp.bfloat16),
            pltpu.SemaphoreType.DMA((number, 2)),
        ],
        compiler_params=pltpu.CompilerParams(vmem_limit_bytes=52 * 1024 * 1024),
        cost_estimate=lasting(7),
        name="experts",
    )(*incoming, *weights)


def combine_kernel(place, attended, position, constant_at, table, *refs):
    results, output = refs[:-1], refs[-1]
    tokens = attended.shape[0]
    rows = jnp.concatenate([result[...] for result in results], axis=0)
    total, count = rows.shape[0], 2 * results[0].shape[0]
    spot = lax.broadcasted_iota(jnp.int32, (tokens, total), 1)
    spot = (spot // count ^ place[0]) * count + spot % count
    chosen = jnp.where(position[...] == spot, 1.0, 0.0).astype(jnp.bfloat16)
    entries = table.shape[0]
    spot = lax.broadcasted_iota(jnp.int32, (tokens, 3 * entries), 1) % entries
    constant = jnp.where(constant_at[...] == spot, 1.0, 0.0).astype(jnp.bfloat16)
    parts, rest = [], table[...]
    for _ in range(3):
        parts.append(rest.astype(jnp.bfloat16))
        rest = rest - parts[-1].astype(jnp.float32)
    parts = jnp.concatenate(parts, axis=0)
    mixture = jnp.dot(chosen, rows, preferred_element_type=jnp.float32)
    mixture = mixture + jnp.dot(constant, parts, preferred_element_type=jnp.float32)
    output[...] = (attended[...].astype(jnp.float32) + mixture).astype(jnp.bfloat16)


def combine(place, attended, position, constant_at, table, results):
    return pl.pallas_call(
        combine_kernel,
        out_shape=jax.ShapeDtypeStruct(attended.shape, jnp.bfloat16),
        in_specs=[SMEM] + [VMEM] * (4 + len(results)),
        out_specs=VMEM,
        compiler_params=pltpu.CompilerParams(vmem_limit_bytes=12 * 1024 * 1024),
        name="combine",
    )(place, attended, position, constant_at, table, *results)


def stacked(parts):
    ids = sum([part[1] for part in parts], [])
    return jnp.concatenate([part[0] for part in parts], axis=0), ids, None


def along(part, axis, mask):
    array, ids, half = part
    moved = exchanged(array, axis, mask)
    if axis == "groups":
        return moved, ids, half ^ mask
    change = (mask, 0) if axis == "gy" else (0, mask)
    return moved, [(a ^ change[0], b ^ change[1]) for a, b in ids], half


def diagonal(part, mask):
    array, ids, half = part
    groups, rows = lax.axis_size("groups"), lax.axis_size("gy")
    pairs = [
        (i * rows + j, (i ^ 1) * rows + (j ^ mask)) for i in range(groups) for j in range(rows)
    ]
    moved = lax.ppermute(array, ("groups", "gy"), pairs)
    return moved, [(a ^ mask, b) for a, b in ids], half ^ 1


def held(*values):
    return lax.optimization_barrier(values)


def shards(
    tokens,
    conv_kernel,
    project_in,
    project_out,
    rel_bias,
    expert_in,
    expert_out,
    const_table,
    expert_ids,
    slots,
    const_index,
):
    rows, cols, channels = tokens.shape
    grid_rows, grid_cols = lax.axis_size("gy"), lax.axis_size("gx")
    place = jnp.stack([lax.axis_index(axis) for axis in ("gy", "gx", "groups")]).astype(jnp.int32)
    reach = KERNEL // 2 + SHIFT
    quick = grid_rows == 4 and grid_cols == 4 and lax.axis_size("groups") == 2
    above = shifted(tokens[rows - reach :], "gy", 1)
    if quick:
        pair = [(0, 0), (0, 1)]
        beyond, beyond_out = exchanged(project_in, "gx", 1), exchanged(project_out, "gx", 1)
        kept, weights, bias, edge, own = prepare(tokens, conv_kernel, rel_bias, project_in)
        two, mine, column = join(place, own, beyond, above, edge)
        two = (two, pair, None)
        far = along((mine, pair, 0), "gx", 2)
        facing = along(two, "gy", 2)
    else:
        kept, weights, bias, edge = prepare(tokens, conv_kernel, rel_bias)
        column = jnp.concatenate([above[:, cols - HALO :], edge], axis=0)
    beside = shifted(column, "gx", 1)
    if quick:
        own_out, beyond_out, beside = held(project_out, beyond_out, beside)
        two_out = (jnp.concatenate([own_out, beyond_out], axis=0), pair, None)
        far_out = along(two_out, "gx", 2)
    encoded, normed = encode(place, kept, above, beside, weights)
    if quick:
        first, second, normed = held(far[0], facing[0], normed)
        far, facing = (first, *far[1:]), (second, *facing[1:])
        across = along(far, "gy", 2)
        four_out = stacked([two_out, far_out])
        across_out = along(four_out, "gy", 2)
        far_rest, across_rest = along(far, "groups", 1), diagonal(far, 2)
        pieces_in = [two, facing, far, far_rest, across]
        pieces_in = pieces_in + [along(part, "gy", 1) for part in pieces_in]
        pieces_in = pieces_in + [across_rest, along(across_rest, "gy", 1)]
    else:
        whole = [(None, None)]
        pieces_in = [(lax.all_gather(project_in, ("gy", "gx"), axis=0, tiled=True), whole, None)]
        pieces_out = [(lax.all_gather(project_out, ("gy", "gx"), axis=0, tiled=True), whole, None)]
    context = attend(place, (rows, cols), normed, bias, pieces_in, grid_cols)
    if quick:
        array, context = held(across_out[0], context)
        pieces_out = [four_out, across_out, along(four_out, "gy", 1)]
        pieces_out = pieces_out + [along((array, *across_out[1:]), "gy", 1)]
    rolled, top, side, corner = project(
        place, (rows, cols), context, encoded, pieces_out, grid_cols
    )
    below = shifted(top, "gy", -1)
    right = shifted(side, "gx", -1)
    last = shifted_both(corner, -1)
    expert_of, slot_of = expert_ids.reshape(-1), slots.reshape(-1)
    position = jnp.where(expert_of < EXPERTS, expert_of * CAP + slot_of, -1)
    constant_at = jnp.where(expert_of == EXPERTS, const_index.reshape(-1), -1)
    attended, *outgoing = dispatch(
        place, rolled, below, right, last, position[None, :], grid_rows
    )
    half, results = expert_in.shape[0] // 2, [None] * len(outgoing)
    incoming = [
        [
            exchanged(outgoing[2 * mask + h], "gy", mask) if mask else outgoing[h]
            for mask in range(grid_rows)
        ]
        for h in range(2)
    ]
    for h, arrived in enumerate(incoming):
        served = serve(arrived, (expert_in, expert_out), h * half, half)
        for mask, array in enumerate(served):
            results[2 * mask + h] = exchanged(array, "gy", mask) if mask else array
    output = combine(
        place, attended, position[:, None], constant_at[:, None], const_table, results
    )
    return output.reshape(rows, cols, channels)


def solution(mesh):
    placed = (
        P(("groups", "gy"), "gx", None),
        P(),
        P(("gy", "gx"), None),
        P(("gy", "gx"), None),
        P(),
        P("gy", None, None),
        P("gy", None, None),
        P(),
        P(("groups", "gy"), "gx"),
        P(("groups", "gy"), "gx"),
        P(("groups", "gy"), "gx"),
    )
    return jax.shard_map(
        shards,
        mesh=mesh,
        in_specs=placed,
        out_specs=P(("groups", "gy"), "gx", None),
        check_vma=False,
    )
```

```python
import functools

import jax
import jax.numpy as jnp
from jax import lax
from jax.experimental import pallas as pl
from jax.experimental.pallas import tpu as pltpu
from jax.sharding import PartitionSpec as P

HD = 32
EXPERTS = 32
WIN = 8
SHIFT = 4
KERNEL = 7
CAP = 16
LANES = 128
GROUP = LANES // HD
SPOTS = WIN * WIN
HALO = 8
VMEM = pl.BlockSpec(memory_space=pltpu.VMEM)
SMEM = pl.BlockSpec(memory_space=pltpu.SMEM)
ANY = pl.BlockSpec(memory_space=pl.ANY)
HBM = pl.BlockSpec(memory_space=pltpu.HBM)
LARGEST = 3.38e38


def lasting(microseconds):
    return pl.CostEstimate(
        flops=int(microseconds * 1.15e9), bytes_accessed=0, transcendentals=0
    )


def shifted(x, axis, by):
    size = lax.axis_size(axis)
    return lax.ppermute(x, axis, [(i, (i + by) % size) for i in range(size)])


def shifted_both(x, by):
    rows, cols = lax.axis_size("gy"), lax.axis_size("gx")
    pairs = [
        (i * cols + j, ((i + by) % rows) * cols + (j + by) % cols)
        for i in range(rows)
        for j in range(cols)
    ]
    return lax.ppermute(x, ("gy", "gx"), pairs)


def exchanged(x, axis, mask):
    size = lax.axis_size(axis)
    return lax.ppermute(x, axis, [(i, i ^ mask) for i in range(size)])


def normalized(values):
    centred = values - jnp.mean(values, axis=-1, keepdims=True)
    spread = jnp.mean(centred * centred, axis=-1, keepdims=True)
    return (centred * lax.rsqrt(spread + 1e-05)).astype(jnp.bfloat16)


def prepare_kernel(tokens, taps, rel_bias, *refs):
    count = (len(refs) - 4) // 2
    sources, (kept, weights, bias, edge), copies = refs[:count], refs[count : count + 4], refs[count + 4 :]
    kept[...] = tokens[...].astype(jnp.float32)
    weights[...] = taps[...].astype(jnp.float32)
    edge[...] = tokens[:, tokens.shape[1] - HALO :]
    for head in range(rel_bias.shape[0]):
        at = head % GROUP * SPOTS
        bias[head // GROUP, :, at : at + SPOTS] = rel_bias[head]
    for source, copy in zip(sources, copies, strict=True):
        copy[...] = source[...]


def prepare(tokens, taps, rel_bias, *others):
    rows, _, channels = tokens.shape
    bias_shape = (rel_bias.shape[0] // GROUP, SPOTS, GROUP * SPOTS)
    return pl.pallas_call(
        prepare_kernel,
        out_shape=(
            jax.ShapeDtypeStruct(tokens.shape, jnp.float32),
            jax.ShapeDtypeStruct(taps.shape, jnp.float32),
            jax.ShapeDtypeStruct(bias_shape, jnp.float32),
            jax.ShapeDtypeStruct((rows, HALO, channels), jnp.bfloat16),
            *[jax.ShapeDtypeStruct(x.shape, x.dtype) for x in others],
        ),
        in_specs=[VMEM] * (3 + len(others)),
        out_specs=(VMEM,) * (4 + len(others)),
        compiler_params=pltpu.CompilerParams(vmem_limit_bytes=8 * 1024 * 1024),
        cost_estimate=lasting(3),
        name="prepare",
    )(tokens, taps, rel_bias, *others)


def join_kernel(place, own, beyond, above, edge, two, mine, column):
    size, half = own.shape[0], mine.shape[1]
    lanes = pl.ds(pl.multiple_of(place[2] * half, LANES), half)
    for at, part in enumerate((own, beyond)):
        rows = slice(at * size, (at + 1) * size)
        two[rows, :] = part[...]
        mine[rows, :] = part[:, lanes]
    reach = above.shape[0]
    column[:reach] = above[:, above.shape[1] - HALO :]
    column[reach:] = edge[...]


def join(place, own, beyond, above, edge):
    bf16 = functools.partial(jax.ShapeDtypeStruct, dtype=jnp.bfloat16)
    size, wide = own.shape
    return pl.pallas_call(
        join_kernel,
        out_shape=(
            bf16((2 * size, wide)),
            bf16((2 * size, wide // 2)),
            bf16((above.shape[0] + edge.shape[0], *edge.shape[1:])),
        ),
        in_specs=[SMEM] + [VMEM] * 4,
        out_specs=(VMEM,) * 3,
        compiler_params=pltpu.CompilerParams(vmem_limit_bytes=8 * 1024 * 1024),
        cost_estimate=lasting(1),
        name="join",
    )(place, own, beyond, above, edge)


def encode_kernel(place, tokens, above, beside, weights, encoded, normed, upper, left):
    rows, cols, channels = tokens.shape
    reach = KERNEL // 2 + SHIFT
    upper[:, :HALO] = beside[:reach].astype(jnp.float32)
    upper[:, HALO:] = above[...].astype(jnp.float32)
    left[...] = beside[reach:].astype(jnp.float32)
    inner_row = jnp.where(place[0] == 0, 0.0, 1.0)
    first_col = place[1] == 0
    window_cols = cols // WIN
    col = lax.broadcasted_iota(jnp.int32, (WIN, LANES), 0)

    def extended(row, tile, lanes):
        if row < reach:
            return upper[row, tile * WIN : (tile + 1) * WIN, lanes]
        if tile == 0:
            return left[row - reach, :, lanes]
        return tokens[row - reach, (tile - 1) * WIN : tile * WIN, lanes]

    def block(index, _):
        lanes = pl.ds(pl.multiple_of(index * LANES, LANES), LANES)
        for tile in range(window_cols):
            sums = [None] * rows
            for col_off in range(KERNEL):
                column = [
                    jnp.broadcast_to(weights[row_off, pl.ds(col_off, 1), lanes], (WIN, LANES))
                    for row_off in range(KERNEL)
                ]
                if tile == 0:
                    near = (col < SHIFT) == (col + col_off < reach)
                    keep = jnp.where(near | jnp.logical_not(first_col), 1.0, 0.0)
                for row in range(rows + KERNEL - 1):
                    line = jnp.where(
                        col > col_off, extended(row, tile, lanes), extended(row, tile + 1, lanes)
                    )
                    line = pltpu.roll(line, WIN - 1 - col_off, 0)
                    if tile == 0:
                        line = line * keep
                    cut = line * inner_row if SHIFT <= row < reach + KERNEL // 2 else line
                    for out in range(max(0, row - KERNEL + 1), min(rows, row + 1)):
                        row_off = row - out
                        same = (out < SHIFT) == (row < reach)
                        term = (line if same else cut) * column[row_off]
                        if row_off == KERNEL // 2 and col_off == KERNEL // 2:
                            term = term + line
                        sums[out] = term if sums[out] is None else sums[out] + term
            for window_row in range(rows // WIN):
                stacked = jnp.concatenate(sums[window_row * WIN : (window_row + 1) * WIN], axis=0)
                first = (window_row * window_cols + tile) * SPOTS
                encoded[first : first + SPOTS, lanes] = stacked.astype(jnp.bfloat16)
        return 0

    lax.fori_loop(0, channels // LANES, block, 0)

    def norm(index, _):
        part = pl.ds(pl.multiple_of(index * SPOTS, SPOTS), SPOTS)
        normed[part, :] = normalized(encoded[part, :].astype(jnp.float32))
        return 0

    lax.fori_loop(0, rows * cols // SPOTS, norm, 0, unroll=8)


def encode(place, tokens, above, beside, weights):
    rows, cols, channels = tokens.shape
    flat = jax.ShapeDtypeStruct((rows * cols, channels), jnp.bfloat16)
    reach = KERNEL // 2 + SHIFT
    return pl.pallas_call(
        encode_kernel,
        out_shape=(flat, flat),
        in_specs=[SMEM] + [VMEM] * 4,
        out_specs=(VMEM, VMEM),
        scratch_shapes=[
            pltpu.VMEM((reach, cols + HALO, channels), jnp.float32),
            pltpu.VMEM((rows, HALO, channels), jnp.float32),
        ],
        compiler_params=pltpu.CompilerParams(vmem_limit_bytes=12 * 1024 * 1024),
        cost_estimate=lasting(0.1),
        name="encode",
    )(place, tokens, above, beside, weights)


def fetch(place, grid_cols, pieces, ids, target, sems):
    copies = []
    for piece, (parts, half) in zip(pieces, ids, strict=True):
        size = piece.shape[0] // len(parts)
        wide = min(piece.shape[1], target.shape[1])
        left = 0 if half is None else pl.multiple_of((place[2] ^ half) * wide, LANES)
        for at, (mask_row, mask_col) in enumerate(parts):
            if mask_row is None:
                first = 0
            else:
                owner = (place[0] ^ mask_row) * grid_cols + (place[1] ^ mask_col)
                first = pl.multiple_of(owner * size, 16)
            copy = pltpu.make_async_copy(
                piece.at[pl.ds(at * size, size), pl.ds(0, wide)],
                target.at[pl.ds(first, size), pl.ds(left, wide)],
                sems.at[len(copies)],
            )
            copy.start()
            copies.append(copy)
    return copies


def attend_kernel(shape, ids, grid_cols, *refs):
    rows, cols = shape
    place, normed, bias = refs[:3]
    context, weight, mixed, sems = refs[3 + len(ids) :]
    channels = normed.shape[1]
    copies = fetch(place, grid_cols, refs[3 : 3 + len(ids)], ids, weight, sems)
    groups = channels // LANES
    for copy in copies:
        copy.wait()
    wide = 3 * channels

    def project(index, _):
        lanes = pl.ds(pl.multiple_of(index * wide, wide), wide)
        mixed[:, lanes] = jnp.dot(
            normed[...], weight[:, lanes], preferred_element_type=jnp.float32
        ).astype(jnp.bfloat16)
        return 0

    lax.fori_loop(0, 3 * channels // wide, project, 0)

    window_cols = cols // WIN
    keys = GROUP * SPOTS
    query_at = lax.broadcasted_iota(jnp.int32, (SPOTS, keys), 0)
    key_at = lax.broadcasted_iota(jnp.int32, (SPOTS, keys), 1) % SPOTS
    row_differs = (query_at < SPOTS // 2) != (key_at < SPOTS // 2)
    col_differs = (query_at % WIN < SHIFT) != (key_at % WIN < SHIFT)
    lane = lax.broadcasted_iota(jnp.int32, (SPOTS, LANES), 1) // HD
    head_masks = [jnp.where(lane == h, 1.0, 0.0).astype(jnp.bfloat16) for h in range(GROUP)]
    block_row = lax.broadcasted_iota(jnp.int32, (keys, keys), 0) // SPOTS
    block_col = lax.broadcasted_iota(jnp.int32, (keys, keys), 1) // SPOTS
    same_head = jnp.where(block_row == block_col, 1.0, 0.0).astype(jnp.bfloat16)

    def window(index, _):
        part = pl.ds(pl.multiple_of(index * SPOTS, SPOTS), SPOTS)
        cut_rows = jnp.logical_and(place[0] == 0, index < window_cols)
        cut_cols = jnp.logical_and(place[1] == 0, index % window_cols == 0)
        hidden = (row_differs & cut_rows) | (col_differs & cut_cols)
        barrier = jnp.where(hidden, -1e30, 0.0)
        all_weights = []
        for group in range(groups):
            first = group * LANES
            query = mixed[part, first : first + LANES]
            key = mixed[part, channels + first : channels + first + LANES]
            key_all = jnp.concatenate([key * m for m in head_masks], axis=0)
            scores = lax.dot_general(
                query, key_all, (((1,), (1,)), ((), ())), preferred_element_type=jnp.float32
            )
            all_weights.append(jnp.exp(scores * HD ** (-0.5) + (bias[group] + barrier)))
        weights = jnp.concatenate(all_weights, axis=0)
        total = jnp.dot(
            jnp.minimum(weights, LARGEST).astype(jnp.bfloat16),
            same_head,
            preferred_element_type=jnp.float32,
        )
        probs = (weights * pl.reciprocal(total)).astype(jnp.bfloat16)
        for group in range(groups):
            first = group * LANES
            value = mixed[part, 2 * channels + first : 2 * channels + first + LANES]
            value_all = jnp.concatenate([value * m for m in head_masks], axis=0)
            context[part, first : first + LANES] = jnp.dot(
                probs[group * SPOTS : (group + 1) * SPOTS],
                value_all,
                preferred_element_type=jnp.float32,
            ).astype(jnp.bfloat16)
        return 0

    lax.fori_loop(0, rows * cols // SPOTS, window, 0, unroll=8)


def attend(place, shape, normed, bias, pieces, grid_cols):
    rows, cols = shape
    channels = normed.shape[1]
    ids = [p[1:] for p in pieces]
    return pl.pallas_call(
        functools.partial(attend_kernel, shape, ids, grid_cols),
        out_shape=jax.ShapeDtypeStruct((rows * cols, channels), jnp.bfloat16),
        in_specs=[SMEM, VMEM, VMEM] + [ANY] * len(pieces),
        out_specs=VMEM,
        scratch_shapes=[
            pltpu.VMEM((channels, 3 * channels), jnp.bfloat16),
            pltpu.VMEM((rows * cols, 3 * channels), jnp.bfloat16),
            pltpu.SemaphoreType.DMA((sum(len(p[0]) for p in ids),)),
        ],
        compiler_params=pltpu.CompilerParams(vmem_limit_bytes=16 * 1024 * 1024),
        cost_estimate=lasting(10),
        name="attend",
    )(place, normed, bias, *[p[0] for p in pieces])


def project_kernel(shape, ids, grid_cols, *refs):
    rows, cols = shape
    place, context, encoded = refs[:3]
    rolled, top, side, corner, weight, sems = refs[3 + len(ids) :]
    channels = context.shape[1]
    for copy in fetch(place, grid_cols, refs[3 : 3 + len(ids)], ids, weight, sems):
        copy.wait()
    window_cols = cols // WIN
    wide = channels
    sublane = lax.broadcasted_iota(jnp.int32, (WIN, wide), 0)

    def finish(index, _):
        lanes = pl.ds(pl.multiple_of(index * wide, wide), wide)
        update = jnp.dot(context[...], weight[:, lanes], preferred_element_type=jnp.float32)
        summed = encoded[:, lanes].astype(jnp.float32) + update
        edge = []
        for row in range(rows):
            tiles = []
            for tile in range(window_cols):
                first = (row // WIN * window_cols + tile) * SPOTS + row % WIN * WIN
                tiles.append(summed[first : first + WIN])
            for pair in range(window_cols // 2):
                both = jnp.concatenate(tiles[2 * pair : 2 * pair + 2], axis=0)
                both = both.astype(jnp.bfloat16)
                at = pair * 2 * WIN
                rolled[row, at : at + 2 * WIN, lanes] = both
                if row < SHIFT:
                    top[row, at : at + 2 * WIN, lanes] = both
            edge.append(tiles[0])
        for quad in range(rows // 4):
            halves = [
                jnp.where(
                    sublane < SHIFT,
                    edge[4 * quad + two],
                    pltpu.roll(edge[4 * quad + two + 1], SHIFT, 0),
                )
                for two in (0, 2)
            ]
            packed = jnp.concatenate(halves, axis=0).astype(jnp.bfloat16)
            if quad == 0:
                corner[:, lanes] = packed
            else:
                side[(quad - 1) * 16 : quad * 16, lanes] = packed
        return 0

    lax.fori_loop(0, channels // wide, finish, 0)


def project(place, shape, context, encoded, pieces, grid_cols):
    rows, cols = shape
    channels = context.shape[1]
    bf16 = functools.partial(jax.ShapeDtypeStruct, dtype=jnp.bfloat16)
    ids = [p[1:] for p in pieces]
    return pl.pallas_call(
        functools.partial(project_kernel, shape, ids, grid_cols),
        out_shape=(
            bf16((rows, cols, channels)),
            bf16((SHIFT, cols, channels)),
            bf16(((rows - SHIFT) * SHIFT, channels)),
            bf16((SHIFT * SHIFT, channels)),
        ),
        in_specs=[SMEM, VMEM, VMEM] + [ANY] * len(pieces),
        out_specs=(VMEM,) * 4,
        scratch_shapes=[
            pltpu.VMEM((channels, channels), jnp.bfloat16),
            pltpu.SemaphoreType.DMA((sum(len(p[0]) for p in ids),)),
        ],
        compiler_params=pltpu.CompilerParams(vmem_limit_bytes=10 * 1024 * 1024),
        cost_estimate=lasting(3),
        name="project",
    )(place, context, encoded, *[p[0] for p in pieces])


def dispatch_kernel(place, rolled, below, right, corner, position, *refs):
    rows, cols, channels = rolled.shape
    attended, outgoing, normed = refs[0], refs[1:-1], refs[-1]
    sublane = lax.broadcasted_iota(jnp.int32, (WIN, channels), 0)
    for row in range(rows):
        if row < rows - SHIFT:
            line, beside, at = rolled[row + SHIFT], right, row
        else:
            line, beside, at = below[row + SHIFT - rows], corner, row + SHIFT - rows
        line = line.astype(jnp.float32)
        tiles = [
            pltpu.roll(line[tile * WIN : (tile + 1) * WIN], SHIFT, 0) for tile in range(cols // WIN)
        ]
        block = at * SHIFT // 16 * 16
        last = beside[block : block + 16].astype(jnp.float32)
        within = at * SHIFT - block
        last = last[within // WIN * WIN : within // WIN * WIN + WIN]
        tiles.append(last if within % WIN else pltpu.roll(last, SHIFT, 0))
        line = jnp.concatenate(
            [
                jnp.where(sublane < SHIFT, tiles[tile], tiles[tile + 1])
                for tile in range(cols // WIN)
            ],
            axis=0,
        )
        attended[row * cols : (row + 1) * cols] = line.astype(jnp.bfloat16)
        normed[row * cols : (row + 1) * cols] = normalized(line)
    for mask in range(len(outgoing) // 2):
        halves = outgoing[2 * mask : 2 * mask + 2]
        count = 2 * halves[0].shape[0]
        spot = lax.broadcasted_iota(jnp.int32, (count, rows * cols), 0)
        spot = spot + (place[0] ^ mask) * count
        chosen = jnp.where(position[...] == spot, 1.0, 0.0).astype(jnp.bfloat16)
        slots = jnp.dot(chosen, normed[...], preferred_element_type=jnp.float32)
        slots = slots.astype(jnp.bfloat16)
        for at, target in enumerate(halves):
            target[...] = slots[at * count // 2 : (at + 1) * count // 2]


def dispatch(place, rolled, below, right, corner, position, grid_rows):
    rows, cols, channels = rolled.shape
    bf16 = functools.partial(jax.ShapeDtypeStruct, dtype=jnp.bfloat16)
    slot_rows = EXPERTS * CAP // grid_rows // 2
    return pl.pallas_call(
        dispatch_kernel,
        out_shape=(bf16((rows * cols, channels)),) + (bf16((slot_rows, channels)),) * (2 * grid_rows),
        in_specs=[SMEM] + [VMEM] * 5,
        out_specs=(VMEM,) * (2 * grid_rows + 1),
        scratch_shapes=[pltpu.VMEM((rows * cols, channels), jnp.bfloat16)],
        compiler_params=pltpu.CompilerParams(vmem_limit_bytes=10 * 1024 * 1024),
        name="dispatch",
    )(place, rolled, below, right, corner, position)


def expert_kernel(count, first, *refs):
    incoming, sources = refs[:count], refs[count : count + 2]
    results, (held_in, held_out, sems) = refs[-3 - count : -3], refs[-3:]
    copies = [
        [
            pltpu.make_async_copy(source.at[first + slot], target.at[slot], sems.at[slot, which])
            for which, (source, target) in enumerate(zip(sources, (held_in, held_out), strict=True))
        ]
        for slot in range(held_in.shape[0])
    ]
    for pair in copies:
        for copy in pair:
            copy.start()
    for slot, (copy_in, copy_out) in enumerate(copies):
        own = pl.ds(slot * CAP, CAP)
        rows = jnp.concatenate([ref[own, :] for ref in incoming], axis=0)
        copy_in.wait()
        hidden = lax.dot_general(
            rows, held_in[slot], (((1,), (1,)), ((), ())), preferred_element_type=jnp.float32
        )
        hidden = (0.5 * hidden * (1.0 + lax.erf(hidden * 0.5**0.5))).astype(jnp.bfloat16)
        copy_out.wait()
        result = jnp.dot(hidden, held_out[slot], preferred_element_type=jnp.float32)
        result = result.astype(jnp.bfloat16)
        for at, ref in enumerate(results):
            ref[own, :] = result[at * CAP : (at + 1) * CAP]


def serve(incoming, weights, first, number):
    count = len(incoming)
    shape = (number, *weights[0].shape[1:])
    return pl.pallas_call(
        functools.partial(expert_kernel, count, first),
        out_shape=tuple(jax.ShapeDtypeStruct(x.shape, x.dtype) for x in incoming),
        in_specs=[VMEM] * count + [HBM, HBM],
        out_specs=(VMEM,) * count,
        scratch_shapes=[
            pltpu.VMEM(shape, jnp.bfloat16),
            pltpu.VMEM(shape, jnp.bfloat16),
            pltpu.SemaphoreType.DMA((number, 2)),
        ],
        compiler_params=pltpu.CompilerParams(vmem_limit_bytes=52 * 1024 * 1024),
        cost_estimate=lasting(7),
        name="experts",
    )(*incoming, *weights)


def combine_kernel(place, attended, position, constant_at, table, *refs):
    results, output = refs[:-1], refs[-1]
    tokens = attended.shape[0]
    rows = jnp.concatenate([result[...] for result in results], axis=0)
    total, count = rows.shape[0], 2 * results[0].shape[0]
    spot = lax.broadcasted_iota(jnp.int32, (tokens, total), 1)
    spot = (spot // count ^ place[0]) * count + spot % count
    chosen = jnp.where(position[...] == spot, 1.0, 0.0).astype(jnp.bfloat16)
    entries = table.shape[0]
    spot = lax.broadcasted_iota(jnp.int32, (tokens, 3 * entries), 1) % entries
    constant = jnp.where(constant_at[...] == spot, 1.0, 0.0).astype(jnp.bfloat16)
    parts, rest = [], table[...]
    for _ in range(3):
        parts.append(rest.astype(jnp.bfloat16))
        rest = rest - parts[-1].astype(jnp.float32)
    parts = jnp.concatenate(parts, axis=0)
    mixture = jnp.dot(chosen, rows, preferred_element_type=jnp.float32)
    mixture = mixture + jnp.dot(constant, parts, preferred_element_type=jnp.float32)
    output[...] = (attended[...].astype(jnp.float32) + mixture).astype(jnp.bfloat16)


def combine(place, attended, position, constant_at, table, results):
    return pl.pallas_call(
        combine_kernel,
        out_shape=jax.ShapeDtypeStruct(attended.shape, jnp.bfloat16),
        in_specs=[SMEM] + [VMEM] * (4 + len(results)),
        out_specs=VMEM,
        compiler_params=pltpu.CompilerParams(vmem_limit_bytes=12 * 1024 * 1024),
        name="combine",
    )(place, attended, position, constant_at, table, *results)


def stacked(parts):
    ids = sum([part[1] for part in parts], [])
    return jnp.concatenate([part[0] for part in parts], axis=0), ids, None


def along(part, axis, mask):
    array, ids, half = part
    moved = exchanged(array, axis, mask)
    if axis == "groups":
        return moved, ids, half ^ mask
    change = (mask, 0) if axis == "gy" else (0, mask)
    return moved, [(a ^ change[0], b ^ change[1]) for a, b in ids], half


def diagonal(part, mask):
    array, ids, half = part
    groups, rows = lax.axis_size("groups"), lax.axis_size("gy")
    pairs = [
        (i * rows + j, (i ^ 1) * rows + (j ^ mask)) for i in range(groups) for j in range(rows)
    ]
    moved = lax.ppermute(array, ("groups", "gy"), pairs)
    return moved, [(a ^ mask, b) for a, b in ids], half ^ 1


def held(*values):
    return lax.optimization_barrier(values)


def shards(
    tokens,
    conv_kernel,
    project_in,
    project_out,
    rel_bias,
    expert_in,
    expert_out,
    const_table,
    expert_ids,
    slots,
    const_index,
):
    rows, cols, channels = tokens.shape
    grid_rows, grid_cols = lax.axis_size("gy"), lax.axis_size("gx")
    place = jnp.stack([lax.axis_index(axis) for axis in ("gy", "gx", "groups")]).astype(jnp.int32)
    reach = KERNEL // 2 + SHIFT
    quick = grid_rows == 4 and grid_cols == 4 and lax.axis_size("groups") == 2
    above = shifted(tokens[rows - reach :], "gy", 1)
    if quick:
        pair = [(0, 0), (0, 1)]
        beyond, beyond_out = exchanged(project_in, "gx", 1), exchanged(project_out, "gx", 1)
        kept, weights, bias, edge, own = prepare(tokens, conv_kernel, rel_bias, project_in)
        two, mine, column = join(place, own, beyond, above, edge)
        two = (two, pair, None)
        far = along((mine, pair, 0), "gx", 2)
        facing = along(two, "gy", 2)
    else:
        kept, weights, bias, edge = prepare(tokens, conv_kernel, rel_bias)
        column = jnp.concatenate([above[:, cols - HALO :], edge], axis=0)
    beside = shifted(column, "gx", 1)
    if quick:
        own_out, beyond_out, beside = held(project_out, beyond_out, beside)
        two_out = (jnp.concatenate([own_out, beyond_out], axis=0), pair, None)
        far_out = along(two_out, "gx", 2)
    encoded, normed = encode(place, kept, above, beside, weights)
    if quick:
        first, second, normed = held(far[0], facing[0], normed)
        far, facing = (first, *far[1:]), (second, *facing[1:])
        across = along(far, "gy", 2)
        four_out = stacked([two_out, far_out])
        across_out = along(four_out, "gy", 2)
        far_rest, across_rest = along(far, "groups", 1), diagonal(far, 2)
        pieces_in = [two, facing, far, far_rest, across]
        pieces_in = pieces_in + [along(part, "gy", 1) for part in pieces_in]
        pieces_in = pieces_in + [across_rest, along(across_rest, "gy", 1)]
    else:
        whole = [(None, None)]
        pieces_in = [(lax.all_gather(project_in, ("gy", "gx"), axis=0, tiled=True), whole, None)]
        pieces_out = [(lax.all_gather(project_out, ("gy", "gx"), axis=0, tiled=True), whole, None)]
    context = attend(place, (rows, cols), normed, bias, pieces_in, grid_cols)
    if quick:
        array, context = held(across_out[0], context)
        pieces_out = [four_out, across_out, along(four_out, "gy", 1)]
        pieces_out = pieces_out + [along((array, *across_out[1:]), "gy", 1)]
    rolled, top, side, corner = project(
        place, (rows, cols), context, encoded, pieces_out, grid_cols
    )
    below = shifted(top, "gy", -1)
    right = shifted(side, "gx", -1)
    last = shifted_both(corner, -1)
    expert_of, slot_of = expert_ids.reshape(-1), slots.reshape(-1)
    position = jnp.where(expert_of < EXPERTS, expert_of * CAP + slot_of, -1)
    constant_at = jnp.where(expert_of == EXPERTS, const_index.reshape(-1), -1)
    attended, *outgoing = dispatch(
        place, rolled, below, right, last, position[None, :], grid_rows
    )
    half, results = expert_in.shape[0] // 2, [None] * len(outgoing)
    incoming = [
        [
            exchanged(outgoing[2 * mask + h], "gy", mask) if mask else outgoing[h]
            for mask in range(grid_rows)
        ]
        for h in range(2)
    ]
    for h, arrived in enumerate(incoming):
        served = serve(arrived, (expert_in, expert_out), h * half, half)
        for mask, array in enumerate(served):
            results[2 * mask + h] = exchanged(array, "gy", mask) if mask else array
    output = combine(
        place, attended, position[:, None], constant_at[:, None], const_table, results
    )
    return output.reshape(rows, cols, channels)


def solution(mesh):
    placed = (
        P(("groups", "gy"), "gx", None),
        P(),
        P(("gy", "gx"), None),
        P(("gy", "gx"), None),
        P(),
        P("gy", None, None),
        P("gy", None, None),
        P(),
        P(("groups", "gy"), "gx"),
        P(("groups", "gy"), "gx"),
        P(("groups", "gy"), "gx"),
    )
    return jax.shard_map(
        shards,
        mesh=mesh,
        in_specs=placed,
        out_specs=P(("groups", "gy"), "gx", None),
        check_vma=False,
    )
```

```python
import functools

import jax
import jax.numpy as jnp
from jax import lax
from jax.experimental import pallas as pl
from jax.experimental.pallas import tpu as pltpu
from jax.sharding import PartitionSpec as P

HD = 32
EXPERTS = 32
WIN = 8
SHIFT = 4
KERNEL = 7
CAP = 16
LANES = 128
GROUP = LANES // HD
SPOTS = WIN * WIN
HALO = 8
VMEM = pl.BlockSpec(memory_space=pltpu.VMEM)
SMEM = pl.BlockSpec(memory_space=pltpu.SMEM)
ANY = pl.BlockSpec(memory_space=pl.ANY)
HBM = pl.BlockSpec(memory_space=pltpu.HBM)
LARGEST = 3.38e38


def lasting(microseconds):
    return pl.CostEstimate(
        flops=int(microseconds * 1.15e9), bytes_accessed=0, transcendentals=0
    )


def shifted(x, axis, by):
    size = lax.axis_size(axis)
    return lax.ppermute(x, axis, [(i, (i + by) % size) for i in range(size)])


def shifted_both(x, by):
    rows, cols = lax.axis_size("gy"), lax.axis_size("gx")
    pairs = [
        (i * cols + j, ((i + by) % rows) * cols + (j + by) % cols)
        for i in range(rows)
        for j in range(cols)
    ]
    return lax.ppermute(x, ("gy", "gx"), pairs)


def exchanged(x, axis, mask):
    size = lax.axis_size(axis)
    return lax.ppermute(x, axis, [(i, i ^ mask) for i in range(size)])


def normalized(values):
    centred = values - jnp.mean(values, axis=-1, keepdims=True)
    spread = jnp.mean(centred * centred, axis=-1, keepdims=True)
    return (centred * lax.rsqrt(spread + 1e-05)).astype(jnp.bfloat16)


def prepare_kernel(tokens, taps, rel_bias, *refs):
    count = (len(refs) - 4) // 2
    sources, (kept, weights, bias, edge), copies = refs[:count], refs[count : count + 4], refs[count + 4 :]
    kept[...] = tokens[...].astype(jnp.float32)
    weights[...] = taps[...].astype(jnp.float32)
    edge[...] = tokens[:, tokens.shape[1] - HALO :]
    for head in range(rel_bias.shape[0]):
        at = head % GROUP * SPOTS
        bias[head // GROUP, :, at : at + SPOTS] = rel_bias[head]
    for source, copy in zip(sources, copies, strict=True):
        copy[...] = source[...]


def prepare(tokens, taps, rel_bias, *others):
    rows, _, channels = tokens.shape
    bias_shape = (rel_bias.shape[0] // GROUP, SPOTS, GROUP * SPOTS)
    return pl.pallas_call(
        prepare_kernel,
        out_shape=(
            jax.ShapeDtypeStruct(tokens.shape, jnp.float32),
            jax.ShapeDtypeStruct(taps.shape, jnp.float32),
            jax.ShapeDtypeStruct(bias_shape, jnp.float32),
            jax.ShapeDtypeStruct((rows, HALO, channels), jnp.bfloat16),
            *[jax.ShapeDtypeStruct(x.shape, x.dtype) for x in others],
        ),
        in_specs=[VMEM] * (3 + len(others)),
        out_specs=(VMEM,) * (4 + len(others)),
        compiler_params=pltpu.CompilerParams(vmem_limit_bytes=8 * 1024 * 1024),
        cost_estimate=lasting(3),
        name="prepare",
    )(tokens, taps, rel_bias, *others)


def join_kernel(place, own, beyond, above, edge, two, mine, column):
    size, half = own.shape[0], mine.shape[1]
    lanes = pl.ds(pl.multiple_of(place[2] * half, LANES), half)
    for at, part in enumerate((own, beyond)):
        rows = slice(at * size, (at + 1) * size)
        two[rows, :] = part[...]
        mine[rows, :] = part[:, lanes]
    reach = above.shape[0]
    column[:reach] = above[:, above.shape[1] - HALO :]
    column[reach:] = edge[...]


def join(place, own, beyond, above, edge):
    bf16 = functools.partial(jax.ShapeDtypeStruct, dtype=jnp.bfloat16)
    size, wide = own.shape
    return pl.pallas_call(
        join_kernel,
        out_shape=(
            bf16((2 * size, wide)),
            bf16((2 * size, wide // 2)),
            bf16((above.shape[0] + edge.shape[0], *edge.shape[1:])),
        ),
        in_specs=[SMEM] + [VMEM] * 4,
        out_specs=(VMEM,) * 3,
        compiler_params=pltpu.CompilerParams(vmem_limit_bytes=8 * 1024 * 1024),
        cost_estimate=lasting(1),
        name="join",
    )(place, own, beyond, above, edge)


def encode_kernel(place, tokens, above, beside, weights, encoded, normed, upper, left):
    rows, cols, channels = tokens.shape
    reach = KERNEL // 2 + SHIFT
    upper[:, :HALO] = beside[:reach].astype(jnp.float32)
    upper[:, HALO:] = above[...].astype(jnp.float32)
    left[...] = beside[reach:].astype(jnp.float32)
    inner_row = jnp.where(place[0] == 0, 0.0, 1.0)
    first_col = place[1] == 0
    window_cols = cols // WIN
    col = lax.broadcasted_iota(jnp.int32, (WIN, LANES), 0)

    def extended(row, tile, lanes):
        if row < reach:
            return upper[row, tile * WIN : (tile + 1) * WIN, lanes]
        if tile == 0:
            return left[row - reach, :, lanes]
        return tokens[row - reach, (tile - 1) * WIN : tile * WIN, lanes]

    def block(index, _):
        lanes = pl.ds(pl.multiple_of(index * LANES, LANES), LANES)
        for tile in range(window_cols):
            sums = [None] * rows
            for col_off in range(KERNEL):
                column = [
                    jnp.broadcast_to(weights[row_off, pl.ds(col_off, 1), lanes], (WIN, LANES))
                    for row_off in range(KERNEL)
                ]
                if tile == 0:
                    near = (col < SHIFT) == (col + col_off < reach)
                    keep = jnp.where(near | jnp.logical_not(first_col), 1.0, 0.0)
                for row in range(rows + KERNEL - 1):
                    line = jnp.where(
                        col > col_off, extended(row, tile, lanes), extended(row, tile + 1, lanes)
                    )
                    line = pltpu.roll(line, WIN - 1 - col_off, 0)
                    if tile == 0:
                        line = line * keep
                    cut = line * inner_row if SHIFT <= row < reach + KERNEL // 2 else line
                    for out in range(max(0, row - KERNEL + 1), min(rows, row + 1)):
                        row_off = row - out
                        same = (out < SHIFT) == (row < reach)
                        term = (line if same else cut) * column[row_off]
                        if row_off == KERNEL // 2 and col_off == KERNEL // 2:
                            term = term + line
                        sums[out] = term if sums[out] is None else sums[out] + term
            for window_row in range(rows // WIN):
                stacked = jnp.concatenate(sums[window_row * WIN : (window_row + 1) * WIN], axis=0)
                first = (window_row * window_cols + tile) * SPOTS
                encoded[first : first + SPOTS, lanes] = stacked.astype(jnp.bfloat16)
        return 0

    lax.fori_loop(0, channels // LANES, block, 0)

    def norm(index, _):
        part = pl.ds(pl.multiple_of(index * SPOTS, SPOTS), SPOTS)
        normed[part, :] = normalized(encoded[part, :].astype(jnp.float32))
        return 0

    lax.fori_loop(0, rows * cols // SPOTS, norm, 0, unroll=8)


def encode(place, tokens, above, beside, weights):
    rows, cols, channels = tokens.shape
    flat = jax.ShapeDtypeStruct((rows * cols, channels), jnp.bfloat16)
    reach = KERNEL // 2 + SHIFT
    return pl.pallas_call(
        encode_kernel,
        out_shape=(flat, flat),
        in_specs=[SMEM] + [VMEM] * 4,
        out_specs=(VMEM, VMEM),
        scratch_shapes=[
            pltpu.VMEM((reach, cols + HALO, channels), jnp.float32),
            pltpu.VMEM((rows, HALO, channels), jnp.float32),
        ],
        compiler_params=pltpu.CompilerParams(vmem_limit_bytes=12 * 1024 * 1024),
        cost_estimate=lasting(0.1),
        name="encode",
    )(place, tokens, above, beside, weights)


def fetch(place, grid_cols, pieces, ids, target, sems):
    copies = []
    for piece, (parts, half) in zip(pieces, ids, strict=True):
        size = piece.shape[0] // len(parts)
        wide = min(piece.shape[1], target.shape[1])
        left = 0 if half is None else pl.multiple_of((place[2] ^ half) * wide, LANES)
        for at, (mask_row, mask_col) in enumerate(parts):
            if mask_row is None:
                first = 0
            else:
                owner = (place[0] ^ mask_row) * grid_cols + (place[1] ^ mask_col)
                first = pl.multiple_of(owner * size, 16)
            copy = pltpu.make_async_copy(
                piece.at[pl.ds(at * size, size), pl.ds(0, wide)],
                target.at[pl.ds(first, size), pl.ds(left, wide)],
                sems.at[len(copies)],
            )
            copy.start()
            copies.append(copy)
    return copies


def attend_kernel(shape, ids, grid_cols, *refs):
    rows, cols = shape
    place, normed, bias = refs[:3]
    context, weight, mixed, sems = refs[3 + len(ids) :]
    channels = normed.shape[1]
    copies = fetch(place, grid_cols, refs[3 : 3 + len(ids)], ids, weight, sems)
    groups = channels // LANES
    for copy in copies:
        copy.wait()
    wide = 3 * channels

    def project(index, _):
        lanes = pl.ds(pl.multiple_of(index * wide, wide), wide)
        mixed[:, lanes] = jnp.dot(
            normed[...], weight[:, lanes], preferred_element_type=jnp.float32
        ).astype(jnp.bfloat16)
        return 0

    lax.fori_loop(0, 3 * channels // wide, project, 0)

    window_cols = cols // WIN
    keys = GROUP * SPOTS
    query_at = lax.broadcasted_iota(jnp.int32, (SPOTS, keys), 0)
    key_at = lax.broadcasted_iota(jnp.int32, (SPOTS, keys), 1) % SPOTS
    row_differs = (query_at < SPOTS // 2) != (key_at < SPOTS // 2)
    col_differs = (query_at % WIN < SHIFT) != (key_at % WIN < SHIFT)
    lane = lax.broadcasted_iota(jnp.int32, (SPOTS, LANES), 1) // HD
    head_masks = [jnp.where(lane == h, 1.0, 0.0).astype(jnp.bfloat16) for h in range(GROUP)]
    block_row = lax.broadcasted_iota(jnp.int32, (keys, keys), 0) // SPOTS
    block_col = lax.broadcasted_iota(jnp.int32, (keys, keys), 1) // SPOTS
    same_head = jnp.where(block_row == block_col, 1.0, 0.0).astype(jnp.bfloat16)

    def window(index, _):
        part = pl.ds(pl.multiple_of(index * SPOTS, SPOTS), SPOTS)
        cut_rows = jnp.logical_and(place[0] == 0, index < window_cols)
        cut_cols = jnp.logical_and(place[1] == 0, index % window_cols == 0)
        hidden = (row_differs & cut_rows) | (col_differs & cut_cols)
        barrier = jnp.where(hidden, -1e30, 0.0)
        all_weights = []
        for group in range(groups):
            first = group * LANES
            query = mixed[part, first : first + LANES]
            key = mixed[part, channels + first : channels + first + LANES]
            key_all = jnp.concatenate([key * m for m in head_masks], axis=0)
            scores = lax.dot_general(
                query, key_all, (((1,), (1,)), ((), ())), preferred_element_type=jnp.float32
            )
            all_weights.append(jnp.exp(scores * HD ** (-0.5) + (bias[group] + barrier)))
        weights = jnp.concatenate(all_weights, axis=0)
        total = jnp.dot(
            jnp.minimum(weights, LARGEST).astype(jnp.bfloat16),
            same_head,
            preferred_element_type=jnp.float32,
        )
        probs = (weights * pl.reciprocal(total)).astype(jnp.bfloat16)
        for group in range(groups):
            first = group * LANES
            value = mixed[part, 2 * channels + first : 2 * channels + first + LANES]
            value_all = jnp.concatenate([value * m for m in head_masks], axis=0)
            context[part, first : first + LANES] = jnp.dot(
                probs[group * SPOTS : (group + 1) * SPOTS],
                value_all,
                preferred_element_type=jnp.float32,
            ).astype(jnp.bfloat16)
        return 0

    lax.fori_loop(0, rows * cols // SPOTS, window, 0, unroll=8)


def attend(place, shape, normed, bias, pieces, grid_cols):
    rows, cols = shape
    channels = normed.shape[1]
    ids = [p[1:] for p in pieces]
    return pl.pallas_call(
        functools.partial(attend_kernel, shape, ids, grid_cols),
        out_shape=jax.ShapeDtypeStruct((rows * cols, channels), jnp.bfloat16),
        in_specs=[SMEM, VMEM, VMEM] + [ANY] * len(pieces),
        out_specs=VMEM,
        scratch_shapes=[
            pltpu.VMEM((channels, 3 * channels), jnp.bfloat16),
            pltpu.VMEM((rows * cols, 3 * channels), jnp.bfloat16),
            pltpu.SemaphoreType.DMA((sum(len(p[0]) for p in ids),)),
        ],
        compiler_params=pltpu.CompilerParams(vmem_limit_bytes=16 * 1024 * 1024),
        cost_estimate=lasting(10),
        name="attend",
    )(place, normed, bias, *[p[0] for p in pieces])


def project_kernel(shape, ids, grid_cols, *refs):
    rows, cols = shape
    place, context, encoded = refs[:3]
    rolled, top, side, corner, weight, sems = refs[3 + len(ids) :]
    channels = context.shape[1]
    for copy in fetch(place, grid_cols, refs[3 : 3 + len(ids)], ids, weight, sems):
        copy.wait()
    window_cols = cols // WIN
    wide = channels
    sublane = lax.broadcasted_iota(jnp.int32, (WIN, wide), 0)

    def finish(index, _):
        lanes = pl.ds(pl.multiple_of(index * wide, wide), wide)
        update = jnp.dot(context[...], weight[:, lanes], preferred_element_type=jnp.float32)
        summed = encoded[:, lanes].astype(jnp.float32) + update
        edge = []
        for row in range(rows):
            tiles = []
            for tile in range(window_cols):
                first = (row // WIN * window_cols + tile) * SPOTS + row % WIN * WIN
                tiles.append(summed[first : first + WIN])
            for pair in range(window_cols // 2):
                both = jnp.concatenate(tiles[2 * pair : 2 * pair + 2], axis=0)
                both = both.astype(jnp.bfloat16)
                at = pair * 2 * WIN
                rolled[row, at : at + 2 * WIN, lanes] = both
                if row < SHIFT:
                    top[row, at : at + 2 * WIN, lanes] = both
            edge.append(tiles[0])
        for quad in range(rows // 4):
            halves = [
                jnp.where(
                    sublane < SHIFT,
                    edge[4 * quad + two],
                    pltpu.roll(edge[4 * quad + two + 1], SHIFT, 0),
                )
                for two in (0, 2)
            ]
            packed = jnp.concatenate(halves, axis=0).astype(jnp.bfloat16)
            if quad == 0:
                corner[:, lanes] = packed
            else:
                side[(quad - 1) * 16 : quad * 16, lanes] = packed
        return 0

    lax.fori_loop(0, channels // wide, finish, 0)


def project(place, shape, context, encoded, pieces, grid_cols):
    rows, cols = shape
    channels = context.shape[1]
    bf16 = functools.partial(jax.ShapeDtypeStruct, dtype=jnp.bfloat16)
    ids = [p[1:] for p in pieces]
    return pl.pallas_call(
        functools.partial(project_kernel, shape, ids, grid_cols),
        out_shape=(
            bf16((rows, cols, channels)),
            bf16((SHIFT, cols, channels)),
            bf16(((rows - SHIFT) * SHIFT, channels)),
            bf16((SHIFT * SHIFT, channels)),
        ),
        in_specs=[SMEM, VMEM, VMEM] + [ANY] * len(pieces),
        out_specs=(VMEM,) * 4,
        scratch_shapes=[
            pltpu.VMEM((channels, channels), jnp.bfloat16),
            pltpu.SemaphoreType.DMA((sum(len(p[0]) for p in ids),)),
        ],
        compiler_params=pltpu.CompilerParams(vmem_limit_bytes=10 * 1024 * 1024),
        cost_estimate=lasting(3),
        name="project",
    )(place, context, encoded, *[p[0] for p in pieces])


def dispatch_kernel(place, rolled, below, right, corner, position, *refs):
    rows, cols, channels = rolled.shape
    attended, outgoing, normed = refs[0], refs[1:-1], refs[-1]
    sublane = lax.broadcasted_iota(jnp.int32, (WIN, channels), 0)
    for row in range(rows):
        if row < rows - SHIFT:
            line, beside, at = rolled[row + SHIFT], right, row
        else:
            line, beside, at = below[row + SHIFT - rows], corner, row + SHIFT - rows
        line = line.astype(jnp.float32)
        tiles = [
            pltpu.roll(line[tile * WIN : (tile + 1) * WIN], SHIFT, 0) for tile in range(cols // WIN)
        ]
        block = at * SHIFT // 16 * 16
        last = beside[block : block + 16].astype(jnp.float32)
        within = at * SHIFT - block
        last = last[within // WIN * WIN : within // WIN * WIN + WIN]
        tiles.append(last if within % WIN else pltpu.roll(last, SHIFT, 0))
        line = jnp.concatenate(
            [
                jnp.where(sublane < SHIFT, tiles[tile], tiles[tile + 1])
                for tile in range(cols // WIN)
            ],
            axis=0,
        )
        attended[row * cols : (row + 1) * cols] = line.astype(jnp.bfloat16)
        normed[row * cols : (row + 1) * cols] = normalized(line)
    for mask in range(len(outgoing) // 2):
        halves = outgoing[2 * mask : 2 * mask + 2]
        count = 2 * halves[0].shape[0]
        spot = lax.broadcasted_iota(jnp.int32, (count, rows * cols), 0)
        spot = spot + (place[0] ^ mask) * count
        chosen = jnp.where(position[...] == spot, 1.0, 0.0).astype(jnp.bfloat16)
        slots = jnp.dot(chosen, normed[...], preferred_element_type=jnp.float32)
        slots = slots.astype(jnp.bfloat16)
        for at, target in enumerate(halves):
            target[...] = slots[at * count // 2 : (at + 1) * count // 2]


def dispatch(place, rolled, below, right, corner, position, grid_rows):
    rows, cols, channels = rolled.shape
    bf16 = functools.partial(jax.ShapeDtypeStruct, dtype=jnp.bfloat16)
    slot_rows = EXPERTS * CAP // grid_rows // 2
    return pl.pallas_call(
        dispatch_kernel,
        out_shape=(bf16((rows * cols, channels)),) + (bf16((slot_rows, channels)),) * (2 * grid_rows),
        in_specs=[SMEM] + [VMEM] * 5,
        out_specs=(VMEM,) * (2 * grid_rows + 1),
        scratch_shapes=[pltpu.VMEM((rows * cols, channels), jnp.bfloat16)],
        compiler_params=pltpu.CompilerParams(vmem_limit_bytes=10 * 1024 * 1024),
        name="dispatch",
    )(place, rolled, below, right, corner, position)


def expert_kernel(count, first, *refs):
    incoming, sources = refs[:count], refs[count : count + 2]
    results, (held_in, held_out, sems) = refs[-3 - count : -3], refs[-3:]
    copies = [
        [
            pltpu.make_async_copy(source.at[first + slot], target.at[slot], sems.at[slot, which])
            for which, (source, target) in enumerate(zip(sources, (held_in, held_out), strict=True))
        ]
        for slot in range(held_in.shape[0])
    ]
    for pair in copies:
        for copy in pair:
            copy.start()
    for slot, (copy_in, copy_out) in enumerate(copies):
        own = pl.ds(slot * CAP, CAP)
        rows = jnp.concatenate([ref[own, :] for ref in incoming], axis=0)
        copy_in.wait()
        hidden = lax.dot_general(
            rows, held_in[slot], (((1,), (1,)), ((), ())), preferred_element_type=jnp.float32
        )
        hidden = (0.5 * hidden * (1.0 + lax.erf(hidden * 0.5**0.5))).astype(jnp.bfloat16)
        copy_out.wait()
        result = jnp.dot(hidden, held_out[slot], preferred_element_type=jnp.float32)
        result = result.astype(jnp.bfloat16)
        for at, ref in enumerate(results):
            ref[own, :] = result[at * CAP : (at + 1) * CAP]


def serve(incoming, weights, first, number):
    count = len(incoming)
    shape = (number, *weights[0].shape[1:])
    return pl.pallas_call(
        functools.partial(expert_kernel, count, first),
        out_shape=tuple(jax.ShapeDtypeStruct(x.shape, x.dtype) for x in incoming),
        in_specs=[VMEM] * count + [HBM, HBM],
        out_specs=(VMEM,) * count,
        scratch_shapes=[
            pltpu.VMEM(shape, jnp.bfloat16),
            pltpu.VMEM(shape, jnp.bfloat16),
            pltpu.SemaphoreType.DMA((number, 2)),
        ],
        compiler_params=pltpu.CompilerParams(vmem_limit_bytes=52 * 1024 * 1024),
        cost_estimate=lasting(7),
        name="experts",
    )(*incoming, *weights)


def combine_kernel(place, attended, position, constant_at, table, *refs):
    results, output = refs[:-1], refs[-1]
    tokens = attended.shape[0]
    rows = jnp.concatenate([result[...] for result in results], axis=0)
    total, count = rows.shape[0], 2 * results[0].shape[0]
    spot = lax.broadcasted_iota(jnp.int32, (tokens, total), 1)
    spot = (spot // count ^ place[0]) * count + spot % count
    chosen = jnp.where(position[...] == spot, 1.0, 0.0).astype(jnp.bfloat16)
    entries = table.shape[0]
    spot = lax.broadcasted_iota(jnp.int32, (tokens, 3 * entries), 1) % entries
    constant = jnp.where(constant_at[...] == spot, 1.0, 0.0).astype(jnp.bfloat16)
    parts, rest = [], table[...]
    for _ in range(3):
        parts.append(rest.astype(jnp.bfloat16))
        rest = rest - parts[-1].astype(jnp.float32)
    parts = jnp.concatenate(parts, axis=0)
    mixture = jnp.dot(chosen, rows, preferred_element_type=jnp.float32)
    mixture = mixture + jnp.dot(constant, parts, preferred_element_type=jnp.float32)
    output[...] = (attended[...].astype(jnp.float32) + mixture).astype(jnp.bfloat16)


def combine(place, attended, position, constant_at, table, results):
    return pl.pallas_call(
        combine_kernel,
        out_shape=jax.ShapeDtypeStruct(attended.shape, jnp.bfloat16),
        in_specs=[SMEM] + [VMEM] * (4 + len(results)),
        out_specs=VMEM,
        compiler_params=pltpu.CompilerParams(vmem_limit_bytes=12 * 1024 * 1024),
        name="combine",
    )(place, attended, position, constant_at, table, *results)


def stacked(parts):
    ids = sum([part[1] for part in parts], [])
    return jnp.concatenate([part[0] for part in parts], axis=0), ids, None


def along(part, axis, mask):
    array, ids, half = part
    moved = exchanged(array, axis, mask)
    if axis == "groups":
        return moved, ids, half ^ mask
    change = (mask, 0) if axis == "gy" else (0, mask)
    return moved, [(a ^ change[0], b ^ change[1]) for a, b in ids], half


def diagonal(part, mask):
    array, ids, half = part
    groups, rows = lax.axis_size("groups"), lax.axis_size("gy")
    pairs = [
        (i * rows + j, (i ^ 1) * rows + (j ^ mask)) for i in range(groups) for j in range(rows)
    ]
    moved = lax.ppermute(array, ("groups", "gy"), pairs)
    return moved, [(a ^ mask, b) for a, b in ids], half ^ 1


def held(*values):
    return lax.optimization_barrier(values)


def shards(
    tokens,
    conv_kernel,
    project_in,
    project_out,
    rel_bias,
    expert_in,
    expert_out,
    const_table,
    expert_ids,
    slots,
    const_index,
):
    rows, cols, channels = tokens.shape
    grid_rows, grid_cols = lax.axis_size("gy"), lax.axis_size("gx")
    place = jnp.stack([lax.axis_index(axis) for axis in ("gy", "gx", "groups")]).astype(jnp.int32)
    reach = KERNEL // 2 + SHIFT
    quick = grid_rows == 4 and grid_cols == 4 and lax.axis_size("groups") == 2
    above = shifted(tokens[rows - reach :], "gy", 1)
    if quick:
        pair = [(0, 0), (0, 1)]
        beyond, beyond_out = exchanged(project_in, "gx", 1), exchanged(project_out, "gx", 1)
        kept, weights, bias, edge, own = prepare(tokens, conv_kernel, rel_bias, project_in)
        two, mine, column = join(place, own, beyond, above, edge)
        two = (two, pair, None)
        far = along((mine, pair, 0), "gx", 2)
        facing = along(two, "gy", 2)
    else:
        kept, weights, bias, edge = prepare(tokens, conv_kernel, rel_bias)
        column = jnp.concatenate([above[:, cols - HALO :], edge], axis=0)
    beside = shifted(column, "gx", 1)
    if quick:
        own_out, beside = held(project_out, beside)
        two_out = (jnp.concatenate([own_out, beyond_out], axis=0), pair, None)
        far_out = along(two_out, "gx", 2)
    encoded, normed = encode(place, kept, above, beside, weights)
    if quick:
        first, second, normed = held(far[0], facing[0], normed)
        far, facing = (first, *far[1:]), (second, *facing[1:])
        across = along(far, "gy", 2)
        four_out = stacked([two_out, far_out])
        across_out = along(four_out, "gy", 2)
        far_rest, across_rest = along(far, "groups", 1), diagonal(far, 2)
        pieces_in = [two, facing, far, far_rest, across]
        pieces_in = pieces_in + [along(part, "gy", 1) for part in pieces_in]
        pieces_in = pieces_in + [across_rest, along(across_rest, "gy", 1)]
    else:
        whole = [(None, None)]
        pieces_in = [(lax.all_gather(project_in, ("gy", "gx"), axis=0, tiled=True), whole, None)]
        pieces_out = [(lax.all_gather(project_out, ("gy", "gx"), axis=0, tiled=True), whole, None)]
    context = attend(place, (rows, cols), normed, bias, pieces_in, grid_cols)
    if quick:
        array, context = held(across_out[0], context)
        pieces_out = [four_out, across_out, along(four_out, "gy", 1)]
        pieces_out = pieces_out + [along((array, *across_out[1:]), "gy", 1)]
    rolled, top, side, corner = project(
        place, (rows, cols), context, encoded, pieces_out, grid_cols
    )
    below = shifted(top, "gy", -1)
    right = shifted(side, "gx", -1)
    last = shifted_both(corner, -1)
    expert_of, slot_of = expert_ids.reshape(-1), slots.reshape(-1)
    position = jnp.where(expert_of < EXPERTS, expert_of * CAP + slot_of, -1)
    constant_at = jnp.where(expert_of == EXPERTS, const_index.reshape(-1), -1)
    attended, *outgoing = dispatch(
        place, rolled, below, right, last, position[None, :], grid_rows
    )
    half, results = expert_in.shape[0] // 2, [None] * len(outgoing)
    incoming = [
        [
            exchanged(outgoing[2 * mask + h], "gy", mask) if mask else outgoing[h]
            for mask in range(grid_rows)
        ]
        for h in range(2)
    ]
    for h, arrived in enumerate(incoming):
        served = serve(arrived, (expert_in, expert_out), h * half, half)
        for mask, array in enumerate(served):
            results[2 * mask + h] = exchanged(array, "gy", mask) if mask else array
    output = combine(
        place, attended, position[:, None], constant_at[:, None], const_table, results
    )
    return output.reshape(rows, cols, channels)


def solution(mesh):
    placed = (
        P(("groups", "gy"), "gx", None),
        P(),
        P(("gy", "gx"), None),
        P(("gy", "gx"), None),
        P(),
        P("gy", None, None),
        P("gy", None, None),
        P(),
        P(("groups", "gy"), "gx"),
        P(("groups", "gy"), "gx"),
        P(("groups", "gy"), "gx"),
    )
    return jax.shard_map(
        shards,
        mesh=mesh,
        in_specs=placed,
        out_specs=P(("groups", "gy"), "gx", None),
        check_vma=False,
    )
```
